256 devices in a mesh: row: 64 (over y, z_hi, x), col: 4 (over z_lo, core).
Axes of the slice: x: 4, y: 4, z: 8 (z_hi: 4, z_lo: 2; z = z_hi * 2 + z_lo), core: 2. Of those that a mesh axis runs over, the one named last changes fastest.
Arguments:
- tile_values: bfloat16 [64, 4, 8, 512, 512], P('row', 'col'), may hold values from -0.25 to 0.25
- tile_coords: int32 [64, 4, 8, 2], P('row', 'col'), may hold values from 0 to 3, as said below
- tile_counts: int32 [64, 4], P('row', 'col'), may hold values from 1 to 8, as said below
- sketch: bfloat16 [4096, 1024], P('col'), may hold values from -6 to 6
Outputs:
- sketch_basis: float32 [4, 1024, 1024], P('col', 'row')
- triangle: float32 [1024, 1024], replicated
The draws below stay inside these ranges and needn't reach their ends.
Inputs may be any that keep to these rules, and one draw needn't show every extreme that they name: `tile_coords`: entry [..., 0] is a tile row below 4 and entry [..., 1] a tile column below 2; the 8 positions in the list of one scenario block and column group are all distinct. `tile_counts`: some scenario block and column group has all 8 slots live.
All inputs are finite; a program needn't handle non-finite values.
Results may differ from the reference program's by a relative error of at most 0.00072.
Values may be sent and summed in bfloat16 or wider, within the bound.
No kernel may reach another device: no remote copies, remote signals or barrier semaphores. Data moves between devices by JAX's collectives and lax.ppermute only.
A program may use at most 128 MiB of HBM per device.

```python
import jax
import jax.numpy as jnp
from jax import lax

TILE = 512
K = 1024
R_DEV = 4
C_DEV = 2
MAXT = 8
NCOLS = 4096
N_ROW = 64
N_COL = 4


def draw_tile_coords(key, part):
    key = jax.random.fold_in(key, 11)
    slot_count = R_DEV * C_DEV
    scores = jax.random.randint(key, (N_ROW, N_COL, slot_count), 0, 1 << 20) * slot_count + jnp.arange(slot_count, dtype=jnp.int32)
    ranking = jnp.argsort(scores, axis=-1, stable=True).astype(jnp.int32)
    return jnp.stack([ranking // C_DEV, ranking % C_DEV], axis=-1).astype(jnp.int32)


def draw_tile_counts(key, part):
    key = jax.random.fold_in(key, 23)
    first_key, second_key, third_key = jax.random.split(key, 3)
    slot_count = R_DEV * C_DEV
    first_draw = jax.random.randint(first_key, (N_ROW, N_COL), 0, slot_count)
    second_draw = jax.random.randint(second_key, (N_ROW, N_COL), 0, slot_count)
    counts = jnp.minimum(first_draw, second_draw) + 1
    chosen = jax.random.randint(third_key, (), 0, N_ROW * N_COL)
    flat_index = jnp.arange(N_ROW * N_COL, dtype=jnp.int32).reshape(N_ROW, N_COL)
    return jnp.where(flat_index == chosen, slot_count, counts).astype(jnp.int32)


def with_spikes(drawn, key, source, target, shards_of, factor):
    def block_of(dim):
        return (jnp.arange(drawn.shape[dim]) // (drawn.shape[dim] // shards_of)).reshape((-1,) + (1,) * (drawn.ndim - 1 - dim))

    one_side = jax.random.permutation(key, shards_of)[block_of(target)]
    second = (block_of(target) + shards_of // 2) % shards_of
    return jnp.where((block_of(source) == one_side) | (block_of(source) == second), factor * drawn, drawn)


def level_of(own_key, extent, cuts, smallest, largest):
    factor_of = 1.0
    for dim, parts in cuts:
        steps = jax.random.uniform(jax.random.fold_in(jax.random.fold_in(own_key, 6), dim), (parts,), jnp.float32, smallest / len(cuts), largest / len(cuts))
        factor_of = factor_of * jnp.repeat(jnp.exp(steps), extent[dim] // parts).reshape((-1,) + (1,) * (len(extent) - 1 - dim))
    return factor_of


def noise(key, shape, scale, bound, shards=(), held_as=jnp.bfloat16):
    factor_of = level_of(key, shape, shards, -0.22, 0.18) if shards else 1.0
    drawn = jax.random.normal(key, shape, jnp.float32) * scale * factor_of
    return jnp.minimum(jnp.maximum(drawn, -bound), bound).astype(held_as)


def bell_draw_with(stream_key, extent, spread, limit, cuts, heavy, kind=jnp.bfloat16):
    array = spread * jax.random.normal(stream_key, extent, jnp.float32)
    if cuts:
        array = array * level_of(stream_key, extent, cuts, -0.22, 0.18)
    return jnp.clip(with_spikes(array, jax.random.fold_in(stream_key, 3), *heavy), -limit, limit).astype(kind)


def setup_inputs(seed: int = 0) -> dict:
    seeds = jax.random.split(jax.random.key(seed), 5)
    return {
        "tile_values": bell_draw_with(seeds[0], (N_ROW, N_COL, MAXT, TILE, TILE), NCOLS ** -0.5, 0.25, ((0, 64), (1, 4)), (0, 4, 64, 4.0)),
        "tile_coords": draw_tile_coords(jax.random.fold_in(seeds[4], 71), 0),
        "tile_counts": draw_tile_counts(jax.random.fold_in(seeds[4], 71), 0),
        "sketch": noise(seeds[3], (NCOLS, K), 1.0, 6.0, ((0, 4),)),
    }


shift_weight = 0.5

def reference(tile_values, tile_coords, tile_counts, sketch):
    column_rows = C_DEV * TILE
    scenario_rows = R_DEV * TILE

    def scenario(column_sum, inputs):
        blocks, places, live_counts = inputs
        row_partial = jnp.zeros((scenario_rows, K), jnp.float32)
        for column_group in range(N_COL):

            def forward_step(slot_index, running, column_group=column_group):
                strip_start = column_group * column_rows + places[column_group, slot_index, 1] * TILE
                sketch_strip = lax.dynamic_slice_in_dim(sketch, strip_start, TILE, 0)
                product = jnp.dot(blocks[column_group, slot_index].astype(jnp.float32), sketch_strip.astype(jnp.float32), preferred_element_type=jnp.float32)
                row_start = places[column_group, slot_index, 0] * TILE
                current = lax.dynamic_slice_in_dim(running, row_start, TILE, 0)
                return lax.dynamic_update_slice_in_dim(running, current + product, row_start, 0)
            row_partial = lax.fori_loop(0, live_counts[column_group], forward_step, row_partial)
        image_rows = row_partial.astype(jnp.bfloat16)
        for column_group in range(N_COL):

            def back_step(slot_index, running, column_group=column_group):
                row_start = places[column_group, slot_index, 0] * TILE
                source_rows = lax.dynamic_slice_in_dim(image_rows, row_start, TILE, 0)
                product = lax.dot_general(blocks[column_group, slot_index].astype(jnp.float32), source_rows.astype(jnp.float32), (((0,), (0,)), ((), ())), preferred_element_type=jnp.float32)
                col_start = column_group * column_rows + places[column_group, slot_index, 1] * TILE
                current = lax.dynamic_slice_in_dim(running, col_start, TILE, 0)
                return lax.dynamic_update_slice_in_dim(running, current + product, col_start, 0)
            column_sum = lax.fori_loop(0, live_counts[column_group], back_step, column_sum)
        return (column_sum, None)
    start_sum = jnp.zeros((N_COL * column_rows, K), jnp.float32)
    gathered, _ = lax.scan(scenario, start_sum, (tile_values, tile_coords, tile_counts))
    shifted = gathered + shift_weight * sketch.astype(jnp.float32)
    gram_matrix = jnp.dot(shifted.T, shifted, precision=lax.Precision.HIGHEST) / shifted.shape[0]
    lower_factor = jnp.linalg.cholesky(gram_matrix)
    basis_rows = jax.scipy.linalg.solve_triangular(lower_factor, shifted.T, lower=True).T
    return (basis_rows.reshape(N_COL, column_rows, K), lower_factor.T)
```

```python
import functools

import jax
import jax.numpy as jnp
from jax import lax
from jax.experimental import pallas as pl
from jax.experimental.pallas import tpu as pltpu
from jax.sharding import PartitionSpec as P

F32 = jnp.float32
BF16 = jnp.bfloat16
HI = lax.Precision.HIGHEST
TILE = 512
K = 1024
PARTS = 2
KW = K // PARTS
KH = KW // 2
NB = 128
shift_weight = 0.5

VMEM = pl.BlockSpec(memory_space=pltpu.VMEM)
SMEM = pl.BlockSpec(memory_space=pltpu.SMEM)


def call(body, outs, in_specs, args, scratch=(), limit=32, flops=0, moved=0):
    return pl.pallas_call(
        body,
        out_shape=tuple(jax.ShapeDtypeStruct(shape, dtype) for shape, dtype in outs),
        in_specs=in_specs,
        out_specs=tuple(VMEM for _ in outs),
        scratch_shapes=list(scratch),
        compiler_params=pltpu.CompilerParams(vmem_limit_bytes=limit << 20),
        cost_estimate=pl.CostEstimate(flops=flops, bytes_accessed=moved, transcendentals=0),
    )(*args)


def place():
    row = lax.axis_index("row")
    return row // 16, lax.rem(row // 4, 4), lax.rem(row, 4)


def moved(row, axis, step):
    y, z, x = row // 16, (row // 4) % 4, row % 4
    if axis == "x":
        x = (x + step) % 4
    elif axis == "y":
        y = (y + step) % 4
    else:
        z = (z + step) % 4
    return y * 16 + z * 4 + x


def send(value, axis, step):
    return lax.ppermute(value, "row", [(r, moved(r, axis, step)) for r in range(64)])


def fetch(value, axis, step):
    return lax.ppermute(value, "row", [(moved(r, axis, step), r) for r in range(64)])


def swap(value, bit):
    return lax.ppermute(value, "col", [(c, c ^ bit) for c in range(4)])


def ring(index, step):
    row, col = index // 4, index % 4
    level = (((row // 4) % 4) * 2 + col // 2 + step) % 8
    return ((row // 16) * 16 + (level // 2) * 4 + row % 4) * 4 + (level % 2) * 2 + col % 2


def ring_send(value, step):
    return lax.ppermute(value, ("row", "col"), [(i, ring(i, step)) for i in range(256)])


def ring_fetch(value, step):
    return lax.ppermute(value, ("row", "col"), [(ring(i, step), i) for i in range(256)])


def find(places, count, i, j):
    slot, live = jnp.int32(0), jnp.int32(0)
    for s in range(8):
        match = (places[s, 0] == i) & (places[s, 1] == j) & (s < count)
        slot = jnp.where(match, s, slot)
        live = jnp.where(match, 1, live)
    return slot, live


def forward_body(places, count, tiles, sketch, *outs):
    me = lax.axis_index("col")
    for k in range(4):
        total = jnp.zeros((TILE, KW), F32)
        for j in range(2):
            slot, live = find(places, count[0, 0], me ^ k, j)
            product = jnp.dot(tiles[slot], sketch[j * TILE:(j + 1) * TILE, :], preferred_element_type=F32)
            total = total + jnp.where(live > 0, product, 0.0)
        outs[k][...] = total


def forward(places, count, tiles, sketch):
    return call(
        forward_body, [((TILE, KW), F32)] * 4, [SMEM, SMEM, VMEM, VMEM], (places, count, tiles, sketch),
        flops=16 * TILE * TILE * KW, moved=9 << 20,
    )


def backward_body(places, count, tiles, i0, i1, i2, i3, *rest):
    outs, total = rest[:8], rest[8]
    me = lax.axis_index("col")
    images = (i0, i1, i2, i3)
    for j in range(2):
        part = jnp.zeros((TILE, KW), F32)
        for k in range(4):
            slot, live = find(places, count[0, 0], me ^ k, j)
            product = lax.dot_general(
                tiles[slot], images[k][...], (((0,), (0,)), ((), ())), preferred_element_type=F32
            )
            part = part + jnp.where(live > 0, product, 0.0)
        total[j * TILE:(j + 1) * TILE, :] = part
    y, _, x = place()
    for d in range(4):
        xd = lax.rem(x + d, 4)
        for block in range(16):
            start = pl.multiple_of(block * 64 + xd * 16, 16)
            outs[d][block * 16:(block + 1) * 16, :] = total[pl.ds(start, 16), :KH]
        start = pl.multiple_of(lax.rem(y + d, 4) * 256, 256)
        outs[4 + d][...] = total[pl.ds(start, 256), KH:]


def backward(places, count, tiles, images):
    return call(
        backward_body, [((256, KH), F32)] * 8, [SMEM, SMEM] + [VMEM] * 5, (places, count, tiles, *images),
        scratch=[pltpu.VMEM((2 * TILE, KW), F32)], flops=16 * TILE * TILE * KW, moved=8 << 20,
    )


def second_body(*refs):
    ins, outs, left, right = refs[:8], refs[8:16], refs[16], refs[17]
    left[...] = (ins[0][...] + ins[1][...]) + (ins[2][...] + ins[3][...])
    right[...] = (ins[4][...] + ins[5][...]) + (ins[6][...] + ins[7][...])
    y, _, x = place()
    for d in range(4):
        outs[d][...] = left[pl.ds(pl.multiple_of(lax.rem(y + d, 4) * 64, 64), 64), :]
        xd = lax.rem(x + d, 4)
        for z in range(4):
            start = pl.multiple_of(z * 64 + xd * 16, 16)
            outs[4 + d][z * 16:(z + 1) * 16, :] = right[pl.ds(start, 16), :]


def third_body(*refs):
    ins, outs, total = refs[:8], refs[8:12], refs[12]
    total[:, :KH] = (ins[0][...] + ins[1][...]) + (ins[2][...] + ins[3][...])
    total[:, KH:] = (ins[4][...] + ins[5][...]) + (ins[6][...] + ins[7][...])
    _, z, _ = place()
    for d in range(4):
        outs[d][...] = total[pl.ds(pl.multiple_of(lax.rem(z + d, 4) * 16, 16), 16), :]


def sum_rows(parts):
    got = [parts[0]] + [send(parts[d], "x", d) for d in (1, 2, 3)]
    got += [parts[4]] + [send(parts[4 + d], "y", d) for d in (1, 2, 3)]
    parts = call(
        second_body, [((64, KH), F32)] * 8, [VMEM] * 8, got,
        scratch=[pltpu.VMEM((256, KH), F32)] * 2, moved=3 << 20,
    )
    got = [parts[0]] + [send(parts[d], "y", d) for d in (1, 2, 3)]
    got += [parts[4]] + [send(parts[4 + d], "x", d) for d in (1, 2, 3)]
    parts = call(
        third_body, [((16, KW), F32)] * 4, [VMEM] * 8, got,
        scratch=[pltpu.VMEM((64, KW), F32)], moved=1 << 20,
    )
    got = [parts[0]] + [send(parts[d], "z", d) for d in (1, 2, 3)]
    return (got[0] + got[1]) + (got[2] + got[3])


def strip_body(*refs):
    ins, keep, give, rows, strip = refs[:8], refs[8], refs[9], refs[10], refs[11]
    for a in range(4):
        rows[a * 64:(a + 1) * 64, :K // 2] = ins[a][...]
        for b in range(4):
            rows[(a * 4 + b) * 16:(a * 4 + b + 1) * 16, K // 2:] = ins[4 + b][a * 16:(a + 1) * 16, :]
    y, _, x = place()
    block = y * 2 + x // 2
    own = rows[:, pl.ds(pl.multiple_of(block * NB, NB), NB)]
    strip[...] = lax.dot_general(
        own, rows[...], (((0,), (0,)), ((), ())), precision=HI, preferred_element_type=F32
    )
    core = lax.rem(lax.axis_index("col"), 2)
    start = lax.rem(x, 2) * 64
    keep[...] = strip[pl.ds(pl.multiple_of(start + core * 32, 32), 32), :]
    give[...] = strip[pl.ds(pl.multiple_of(start + (1 - core) * 32, 32), 32), :]


def spread_body(keep, got, *rest):
    outs, total = rest[:8], rest[8]
    total[...] = keep[...] + got[...]
    _, z, _ = place()
    level = z * 2 + lax.axis_index("col") // 2
    for d in range(8):
        outs[d][...] = total[:, pl.ds(pl.multiple_of(lax.rem(level + d, 8) * NB, NB), NB)]


def gram_parts(shifted, total_columns):
    left, right = shifted[:, :K // 2], shifted[:, K // 2:]
    left = jnp.concatenate([left] + [fetch(left, "x", d) for d in (1, 2, 3)], axis=0)
    right = jnp.concatenate([right] + [fetch(right, "y", d) for d in (1, 2, 3)], axis=0)
    got = [left] + [fetch(left, "y", d) for d in (1, 2, 3)]
    got += [right] + [fetch(right, "x", d) for d in (1, 2, 3)]
    keep, give = call(
        strip_body, [((32, K), F32)] * 2, [VMEM] * 8, got,
        scratch=[pltpu.VMEM((256, K), F32), pltpu.VMEM((NB, K), F32)],
        flops=12 * 256 * NB * K, moved=2 << 20,
    )
    parts = call(
        spread_body, [((32, NB), F32)] * 8, [VMEM] * 2, (keep, swap(give, 1)),
        scratch=[pltpu.VMEM((32, K), F32)], moved=1 << 19,
    )
    got = [parts[0]] + [ring_send(parts[d], d) for d in range(1, 8)]
    piece = (((got[0] + got[1]) + (got[2] + got[3])) + ((got[4] + got[5]) + (got[6] + got[7]))) / total_columns
    pieces = [piece] + [ring_fetch(piece, d) for d in range(1, 8)]
    left = jnp.stack(pieces[:4])
    right = jnp.stack(pieces[4:])
    left = jnp.stack([left] + [fetch(left, "x", d) for d in (1, 2, 3)])
    right = jnp.stack([right] + [fetch(right, "y", d) for d in (1, 2, 3)])
    own = [left] + [fetch(left, "y", d) for d in (1, 2, 3)]
    own += [right] + [fetch(right, "x", d) for d in (1, 2, 3)]
    return own + [swap(part, 1) for part in own]


def dot(a, b):
    return jnp.dot(a, b, precision=HI, preferred_element_type=F32)


def dot_tn(a, b):
    return lax.dot_general(a, b, (((0,), (0,)), ((), ())), precision=HI, preferred_element_type=F32)


def dot_nt(a, b):
    return lax.dot_general(a, b, (((1,), (1,)), ((), ())), precision=HI, preferred_element_type=F32)


def inverse_factor(block):
    groups = NB // 8
    sub = lax.broadcasted_iota(jnp.int32, (8, NB), 0)
    lane = lax.broadcasted_iota(jnp.int32, (8, NB), 1)
    w = [block[8 * g:8 * g + 8, :] for g in range(groups)]
    e = [jnp.where(lane == sub + 8 * g, 1.0, 0.0).astype(F32) for g in range(groups)]
    done = []
    for g in range(groups):
        z, ez = w[g], e[g]
        cols = [jnp.broadcast_to(z[:, 8 * g + k:8 * g + k + 1], (8, NB)) for k in range(8)]
        scale = jnp.zeros((8, NB), F32)
        kept = jnp.zeros((8, NB), F32)
        for k in range(8):
            here = sub == k
            pivot = jnp.broadcast_to(cols[k][k:k + 1, :], (8, NB))
            r = 1.0 / pivot
            zrow = jnp.broadcast_to(z[k:k + 1, :], (8, NB))
            erow = jnp.broadcast_to(ez[k:k + 1, :], (8, NB))
            scale = jnp.where(here, lax.rsqrt(pivot), scale)
            kept = jnp.where(here, erow, kept)
            t = jnp.where(here, 1.0 - r, cols[k] * r)
            z = z - t * zrow
            ez = ez - t * erow
            for l in range(k + 1, 8):
                cols[l] = cols[l] - t * jnp.broadcast_to(cols[l][k:k + 1, :], (8, NB))
        done.append(kept * scale)
        if g + 1 < groups:
            zrows = [jnp.broadcast_to(z[k:k + 1, :], (8, NB)) for k in range(8)]
            erows = [jnp.broadcast_to(ez[k:k + 1, :], (8, NB)) for k in range(8)]
            for i in range(g + 1, groups):
                acc, eacc = w[i], e[i]
                for k in range(8):
                    c = jnp.broadcast_to(w[i][:, 8 * g + k:8 * g + k + 1], (8, NB))
                    acc = acc - c * zrows[k]
                    eacc = eacc - c * erows[k]
                w[i], e[i] = acc, eacc
    return jnp.concatenate(done, axis=0)


def factor_body(*refs):
    parts, shifted, basis, triangle, work, inv = refs[:16], refs[16], refs[17], refs[18], refs[19], refs[20]
    y, z, x = place()
    col = lax.axis_index("col")
    core = lax.rem(col, 2)
    level = z * 2 + col // 2
    for half in range(2):
        lane0 = [pl.multiple_of(lax.rem(level + half * 4 + d, 8) * NB, NB) for d in range(4)]
        for a in range(4):
            for b in range(4):
                dy, dx = (a, b) if half == 0 else (b, a)
                owner = lax.rem(y + dy, 4) * 4 + lax.rem(x + dx, 4)
                for other in range(2):
                    held = parts[other * 8 + half * 4 + a]
                    start = owner * 64 + (core if other == 0 else 1 - core) * 32
                    here = pl.ds(pl.multiple_of(start, 32), 32)
                    for d in range(4):
                        work[here, pl.ds(lane0[d], NB)] = held[b, d]
    basis[...] = shifted[...]
    rows = lax.broadcasted_iota(jnp.int32, (NB, K), 0)
    lanes = lax.broadcasted_iota(jnp.int32, (NB, K), 1)

    def panel(j, _):
        offset = pl.multiple_of(j * NB, NB)
        here = pl.ds(offset, NB)
        inv[...] = inverse_factor(work[here, here])
        row = dot(inv[...], work[here, :])
        row = jnp.where(lanes >= rows + offset, row, 0.0)
        triangle[here, :] = row
        own = dot_nt(basis[:, here], inv[...])
        basis[...] = basis[...] - dot(own, row)
        basis[:, here] = own

        def trail(k, _):
            there = pl.ds(pl.multiple_of(k * NB, NB), NB)
            work[there, :] = work[there, :] - dot_tn(triangle[here, there], triangle[here, :])
            return 0

        lax.fori_loop(j + 1, K // NB, trail, 0)
        return 0

    lax.fori_loop(0, K // NB, panel, 0)


def local(tile_values, tile_coords, tile_counts, sketch):
    tiles, places = tile_values[0, 0], tile_coords[0, 0]
    partial = [forward(places, tile_counts, tiles, sketch[:, q * KW:(q + 1) * KW]) for q in range(PARTS)]
    paired = [(p[0] + swap(p[1], 1), p[2] + swap(p[3], 1)) for p in partial]
    images = [(own + swap(other, 2)).astype(BF16) for own, other in paired]
    summed = []
    for image in images:
        across = swap(image, 2)
        four = (image, swap(image, 1), across, swap(across, 1))
        summed.append(sum_rows(backward(places, tile_counts, tiles, four)))
    summed = jnp.concatenate(summed, axis=1)
    own_count = summed.shape[0]
    offset = lax.axis_index("row") * own_count
    shifted = summed + shift_weight * lax.dynamic_slice_in_dim(sketch, offset, own_count, 0).astype(F32)
    parts = gram_parts(shifted, sketch.shape[0] * 4)
    basis, triangle = call(
        factor_body, [((16, K), F32), ((K, K), F32)], [VMEM] * 17, (*parts, shifted),
        scratch=[pltpu.VMEM((K, K), F32), pltpu.VMEM((NB, NB), F32)], limit=40,
        flops=4 * K * K * K, moved=8 << 20,
    )
    return (basis[None], triangle)


def solution(mesh):
    in_specs = (
        P("row", "col", None, None, None),
        P("row", "col", None, None),
        P("row", "col"),
        P("col", None),
    )
    out_specs = (P("col", "row", None), P())
    return jax.shard_map(local, mesh=mesh, in_specs=in_specs, out_specs=out_specs, check_vma=False)
```

```python
import functools

import jax
import jax.numpy as jnp
from jax import lax
from jax.experimental import pallas as pl
from jax.experimental.pallas import tpu as pltpu
from jax.sharding import PartitionSpec as P

F32 = jnp.float32
BF16 = jnp.bfloat16
HI = lax.Precision.HIGHEST
TILE = 512
K = 1024
PARTS = 2
KW = K // PARTS
KH = KW // 2
NB = 128
shift_weight = 0.5

VMEM = pl.BlockSpec(memory_space=pltpu.VMEM)
SMEM = pl.BlockSpec(memory_space=pltpu.SMEM)


def call(body, outs, in_specs, args, scratch=(), limit=32, flops=0, moved=0):
    return pl.pallas_call(
        body,
        out_shape=tuple(jax.ShapeDtypeStruct(shape, dtype) for shape, dtype in outs),
        in_specs=in_specs,
        out_specs=tuple(VMEM for _ in outs),
        scratch_shapes=list(scratch),
        compiler_params=pltpu.CompilerParams(vmem_limit_bytes=limit << 20),
        cost_estimate=pl.CostEstimate(flops=flops, bytes_accessed=moved, transcendentals=0),
    )(*args)


PLANES = [[y * 16 + z * 4 + x for y in range(4) for x in range(4)] for z in range(4)]
COLUMNS = [[y * 16 + z * 4 + x for z in range(4)] for y in range(4) for x in range(4)]


def trade(value, groups):
    return lax.all_to_all(value, "row", 0, 0, tiled=True, axis_index_groups=groups)


def swap(value, bit):
    return lax.ppermute(value, "col", [(c, c ^ bit) for c in range(4)])


def swap_level(value, bit):
    return lax.ppermute(value, "row", [(r, r ^ (bit * 4)) for r in range(64)])


def find(places, count, i, j):
    slot, live = jnp.int32(0), jnp.int32(0)
    for s in range(8):
        match = (places[s, 0] == i) & (places[s, 1] == j) & (s < count)
        slot = jnp.where(match, s, slot)
        live = jnp.where(match, 1, live)
    return slot, live


def forward_body(first, places, count, tiles, sketch, *outs):
    me = lax.axis_index("col")
    for k in range(4):
        total = jnp.zeros((TILE, KW), F32)
        for j in range(2):
            slot, live = find(places, count[0, 0], me ^ k, j)
            strip = sketch[j * TILE:(j + 1) * TILE, first:first + KW]
            product = jnp.dot(tiles[slot], strip, preferred_element_type=F32)
            total = total + jnp.where(live > 0, product, 0.0)
        outs[k][...] = total


def forward(q, places, count, tiles, sketch):
    return call(
        functools.partial(forward_body, q * KW), [((TILE, KW), F32)] * 4, [SMEM, SMEM, VMEM, VMEM],
        (places, count, tiles, sketch), flops=16 * TILE * TILE * KW, moved=9 << 20,
    )


def backward_body(places, count, tiles, i0, i1, i2, i3, out):
    me = lax.axis_index("col")
    images = (i0, i1, i2, i3)
    for j in range(2):
        part = jnp.zeros((TILE, KW), F32)
        for k in range(4):
            slot, live = find(places, count[0, 0], me ^ k, j)
            product = lax.dot_general(
                tiles[slot], images[k][...], (((0,), (0,)), ((), ())), preferred_element_type=F32
            )
            part = part + jnp.where(live > 0, product, 0.0)
        for y in range(2):
            for z in range(4):
                for x in range(4):
                    start = y * 256 + z * 64 + x * 16
                    out[(2 * j + y) * 4 + x, z * 16:(z + 1) * 16, :] = part[start:start + 16, :]


def backward(places, count, tiles, images):
    return call(
        backward_body, [((16, 64, KW), F32)], [SMEM, SMEM] + [VMEM] * 5, (places, count, tiles, *images),
        flops=16 * TILE * TILE * KW, moved=8 << 20,
    )[0]


WIDE = 5 * NB


def strip_body(scale, rows_in, keep, give, rows, strip):
    for p in range(16):
        rows[p * 16:(p + 1) * 16, :K] = rows_in[p]
        rows[p * 16:(p + 1) * 16, K:] = rows_in[p, :, :WIDE]
    row = lax.axis_index("row")
    x = lax.rem(row, 4)
    start = pl.multiple_of(((row // 16) * 2 + x // 2) * NB, NB)
    strip[...] = scale * lax.dot_general(
        rows[:, pl.ds(start, NB)], rows[:, pl.ds(start, WIDE)], (((0,), (0,)), ((), ())),
        precision=HI, preferred_element_type=F32,
    )
    core = lax.rem(lax.axis_index("col"), 2)
    half = lax.rem(x, 2) * 64
    keep[...] = strip[pl.ds(pl.multiple_of(half + core * 32, 32), 32), :]
    give[...] = strip[pl.ds(pl.multiple_of(half + (1 - core) * 32, 32), 32), :]


def gram_parts(shifted, total_columns):
    rows = trade(jnp.broadcast_to(shifted[None], (16, *shifted.shape)), PLANES)
    keep, give = call(
        functools.partial(strip_body, 1.0 / total_columns), [((32, WIDE), F32)] * 2, [VMEM], (rows,),
        scratch=[pltpu.VMEM((256, K + WIDE), F32), pltpu.VMEM((NB, WIDE), F32)],
        flops=12 * 256 * NB * WIDE, moved=2 << 20,
    )
    total = keep + swap(give, 1)
    total = total + swap(total, 2)
    total = total + swap_level(total, 1)
    total = total + swap_level(total, 2)
    own = trade(jnp.broadcast_to(total[None], (16, *total.shape)), PLANES)
    return own, swap(own, 1)


def dot(a, b):
    return jnp.dot(a, b, precision=HI, preferred_element_type=F32)


def dot_tn(a, b):
    return lax.dot_general(a, b, (((0,), (0,)), ((), ())), precision=HI, preferred_element_type=F32)


def dot_nt(a, b):
    return lax.dot_general(a, b, (((1,), (1,)), ((), ())), precision=HI, preferred_element_type=F32)


def inverse_factor(block):
    groups = NB // 8
    sub = lax.broadcasted_iota(jnp.int32, (8, NB), 0)
    lane = lax.broadcasted_iota(jnp.int32, (8, NB), 1)
    w = [block[8 * g:8 * g + 8, :] for g in range(groups)]
    e = [jnp.where(lane == sub + 8 * g, 1.0, 0.0).astype(F32) for g in range(groups)]
    done = []
    for g in range(groups):
        z, ez = w[g], e[g]
        cols = [jnp.broadcast_to(z[:, 8 * g + k:8 * g + k + 1], (8, NB)) for k in range(8)]
        scale = jnp.zeros((8, NB), F32)
        kept = jnp.zeros((8, NB), F32)
        for k in range(8):
            here = sub == k
            pivot = jnp.broadcast_to(cols[k][k:k + 1, :], (8, NB))
            r = 1.0 / pivot
            zrow = jnp.broadcast_to(z[k:k + 1, :], (8, NB))
            erow = jnp.broadcast_to(ez[k:k + 1, :], (8, NB))
            scale = jnp.where(here, lax.rsqrt(pivot), scale)
            kept = jnp.where(here, erow, kept)
            t = jnp.where(here, 1.0 - r, cols[k] * r)
            z = z - t * zrow
            ez = ez - t * erow
            for l in range(k + 1, 8):
                cols[l] = cols[l] - t * jnp.broadcast_to(cols[l][k:k + 1, :], (8, NB))
        done.append(kept * scale)
        if g + 1 < groups:
            zrows = [jnp.broadcast_to(z[k:k + 1, :], (8, NB)) for k in range(8)]
            erows = [jnp.broadcast_to(ez[k:k + 1, :], (8, NB)) for k in range(8)]
            for i in range(g + 1, groups):
                acc, eacc = w[i], e[i]
                for k in range(8):
                    c = jnp.broadcast_to(w[i][:, 8 * g + k:8 * g + k + 1], (8, NB))
                    acc = acc - c * zrows[k]
                    eacc = eacc - c * erows[k]
                w[i], e[i] = acc, eacc
    return jnp.concatenate(done, axis=0)


def factor_body(own, other, shifted, basis, triangle, work, inv):
    core = lax.rem(lax.axis_index("col"), 2)
    for p in range(16):
        for held, half in ((own, core), (other, 1 - core)):
            here = pl.ds(pl.multiple_of(p * 64 + half * 32, 32), 32)
            for d in range(5):
                block = (p // 2 + d) % 8
                work[here, block * NB:(block + 1) * NB] = held[p, :, d * NB:(d + 1) * NB]
    for i in range(3):
        for j in range(i + 5, 8):
            low = work[j * NB:(j + 1) * NB, i * NB:(i + 1) * NB]
            work[i * NB:(i + 1) * NB, j * NB:(j + 1) * NB] = low.T
    basis[...] = shifted[...]
    rows = lax.broadcasted_iota(jnp.int32, (NB, K), 0)
    lanes = lax.broadcasted_iota(jnp.int32, (NB, K), 1)

    def panel(j, _):
        offset = pl.multiple_of(j * NB, NB)
        here = pl.ds(offset, NB)
        inv[...] = inverse_factor(work[here, here])
        row = dot(inv[...], work[here, :])
        row = jnp.where(lanes >= rows + offset, row, 0.0)
        triangle[here, :] = row
        own = dot_nt(basis[:, here], inv[...])
        basis[...] = basis[...] - dot(own, row)
        basis[:, here] = own

        def trail(k, _):
            there = pl.ds(pl.multiple_of(k * NB, NB), NB)
            work[there, :] = work[there, :] - dot_tn(triangle[here, there], triangle[here, :])
            return 0

        lax.fori_loop(j + 1, K // NB, trail, 0)
        return 0

    lax.fori_loop(0, K // NB, panel, 0)


def local(tile_values, tile_coords, tile_counts, sketch):
    tiles, places = tile_values[0, 0], tile_coords[0, 0]
    partial = [forward(q, places, tile_counts, tiles, sketch) for q in range(PARTS)]
    paired = [(p[0] + swap(p[1], 1), p[2] + swap(p[3], 1)) for p in partial]
    summed, image = [], None
    for own, other in paired:
        if image is not None:
            other, image = lax.optimization_barrier((other, image))
        image = (own + swap(other, 2)).astype(BF16)
        across = swap(image, 2)
        four = (image, swap(image, 1), across, swap(across, 1))
        summed.append(jnp.sum(trade(backward(places, tile_counts, tiles, four), PLANES), axis=0))
    summed = jnp.concatenate(summed, axis=1)
    summed = jnp.sum(trade(summed.reshape(4, 16, K), COLUMNS), axis=0)
    own_count = summed.shape[0]
    offset = lax.axis_index("row") * own_count
    shifted = summed + shift_weight * lax.dynamic_slice_in_dim(sketch, offset, own_count, 0).astype(F32)
    own, other = gram_parts(shifted, sketch.shape[0] * 4)
    basis, triangle = call(
        factor_body, [((16, K), F32), ((K, K), F32)], [VMEM] * 3, (own, other, shifted),
        scratch=[pltpu.VMEM((K, K), F32), pltpu.VMEM((NB, NB), F32)], limit=40,
        flops=4 * K * K * K, moved=8 << 20,
    )
    return (basis[None], triangle)


def solution(mesh):
    in_specs = (
        P("row", "col", None, None, None),
        P("row", "col", None, None),
        P("row", "col"),
        P("col", None),
    )
    out_specs = (P("col", "row", None), P())
    return jax.shard_map(local, mesh=mesh, in_specs=in_specs, out_specs=out_specs, check_vma=False)
```

```python
import functools

import jax
import jax.numpy as jnp
from jax import lax
from jax.experimental import pallas as pl
from jax.experimental.pallas import tpu as pltpu
from jax.sharding import PartitionSpec as P

F32 = jnp.float32
BF16 = jnp.bfloat16
HI = lax.Precision.HIGHEST
TILE = 512
K = 1024
PARTS = 2
KW = K // PARTS
KH = KW // 2
NB = 128
shift_weight = 0.5

VMEM = pl.BlockSpec(memory_space=pltpu.VMEM)
SMEM = pl.BlockSpec(memory_space=pltpu.SMEM)
HBM = pl.BlockSpec(memory_space=pltpu.HBM)


def call(body, outs, in_specs, args, scratch=(), limit=32, flops=0, moved=0):
    return pl.pallas_call(
        body,
        out_shape=tuple(jax.ShapeDtypeStruct(shape, dtype) for shape, dtype in outs),
        in_specs=in_specs,
        out_specs=tuple(VMEM for _ in outs),
        scratch_shapes=list(scratch),
        compiler_params=pltpu.CompilerParams(vmem_limit_bytes=limit << 20),
        cost_estimate=pl.CostEstimate(flops=flops, bytes_accessed=moved, transcendentals=0),
    )(*args)


PLANES = [[y * 16 + z * 4 + x for y in range(4) for x in range(4)] for z in range(4)]
COLUMNS = [[y * 16 + z * 4 + x for z in range(4)] for y in range(4) for x in range(4)]


def trade(value, groups):
    return lax.all_to_all(value, "row", 0, 0, tiled=True, axis_index_groups=groups)


def swap(value, bit):
    return lax.ppermute(value, "col", [(c, c ^ bit) for c in range(4)])


def swap_level(value, bit):
    return lax.ppermute(value, "row", [(r, r ^ (bit * 4)) for r in range(64)])


def find(places, count, i, j):
    slot, live = jnp.int32(0), jnp.int32(0)
    for s in range(8):
        match = (places[s, 0] == i) & (places[s, 1] == j) & (s < count)
        slot = jnp.where(match, s, slot)
        live = jnp.where(match, 1, live)
    return slot, live


def start_tiles(order, places, count, tiles, held, sems):
    copies, lives = {}, {}
    for n, (k, j) in enumerate(order):
        slot, lives[k, j] = find(places, count[0, 0], lax.axis_index("col") ^ k, j)
        copies[k, j] = pltpu.make_async_copy(tiles.at[slot], held.at[n], sems.at[n])
        copies[k, j].start()
    return copies, lives


def forward_body(first, places, count, tiles, sketch, o0, o1, o2, o3, held, strip, sems):
    outs = (o0, o1, o2, o3)
    order = [(k, j) for k in (1, 3, 0, 2) for j in range(2)]
    load = pltpu.make_async_copy(sketch.at[:, pl.ds(first, KW)], strip, sems.at[8])
    load.start()
    copies, lives = start_tiles(order, places, count, tiles, held, sems)
    load.wait()
    for k in (1, 3, 0, 2):
        total = jnp.zeros((TILE, KW), F32)
        for j in range(2):
            copies[k, j].wait()
            tile = held[order.index((k, j))]
            product = jnp.dot(tile, strip[j * TILE:(j + 1) * TILE, :], preferred_element_type=F32)
            total = total + jnp.where(lives[k, j] > 0, product, 0.0)
        outs[k][...] = total


def forward(q, places, count, tiles, sketch):
    return call(
        functools.partial(forward_body, q * KW), [((TILE, KW), F32)] * 4, [SMEM, SMEM, HBM, HBM],
        (places, count, tiles, sketch),
        scratch=[pltpu.VMEM((8, TILE, TILE), BF16), pltpu.VMEM((2 * TILE, KW), BF16), pltpu.SemaphoreType.DMA((9,))],
        limit=20, flops=16 * TILE * TILE * KW, moved=9 << 20,
    )


def backward_body(places, count, tiles, i0, i1, i2, i3, out, held, sems):
    images = (i0, i1, i2, i3)
    order = [(k, j) for j in range(2) for k in range(4)]
    copies, lives = start_tiles(order, places, count, tiles, held, sems)
    for j in range(2):
        part = jnp.zeros((TILE, KW), F32)
        for k in range(4):
            copies[k, j].wait()
            product = lax.dot_general(
                held[order.index((k, j))], images[k][...], (((0,), (0,)), ((), ())), preferred_element_type=F32
            )
            part = part + jnp.where(lives[k, j] > 0, product, 0.0)
        for y in range(2):
            for z in range(4):
                for x in range(4):
                    start = y * 256 + z * 64 + x * 16
                    out[(2 * j + y) * 4 + x, z * 16:(z + 1) * 16, :] = part[start:start + 16, :]


def backward(places, count, tiles, images):
    return call(
        backward_body, [((16, 64, KW), F32)], [SMEM, SMEM, HBM] + [VMEM] * 4, (places, count, tiles, *images),
        scratch=[pltpu.VMEM((8, TILE, TILE), BF16), pltpu.SemaphoreType.DMA((8,))],
        limit=20, flops=16 * TILE * TILE * KW, moved=8 << 20,
    )[0]


WIDE = 5 * NB


def strip_body(scale, rows_in, keep, give, rows, strip):
    for p in range(16):
        rows[p * 16:(p + 1) * 16, :K] = rows_in[p]
        rows[p * 16:(p + 1) * 16, K:] = rows_in[p, :, :WIDE]
    row = lax.axis_index("row")
    x = lax.rem(row, 4)
    start = pl.multiple_of(((row // 16) * 2 + x // 2) * NB, NB)
    strip[...] = scale * lax.dot_general(
        rows[:, pl.ds(start, NB)], rows[:, pl.ds(start, WIDE)], (((0,), (0,)), ((), ())),
        precision=HI, preferred_element_type=F32,
    )
    core = lax.rem(lax.axis_index("col"), 2)
    half = lax.rem(x, 2) * 64
    keep[...] = strip[pl.ds(pl.multiple_of(half + core * 32, 32), 32), :]
    give[...] = strip[pl.ds(pl.multiple_of(half + (1 - core) * 32, 32), 32), :]


def gram_parts(shifted, total_columns):
    rows = trade(jnp.broadcast_to(shifted[None], (16, *shifted.shape)), PLANES)
    keep, give = call(
        functools.partial(strip_body, 1.0 / total_columns), [((32, WIDE), F32)] * 2, [VMEM], (rows,),
        scratch=[pltpu.VMEM((256, K + WIDE), F32), pltpu.VMEM((NB, WIDE), F32)],
        flops=12 * 256 * NB * WIDE, moved=2 << 20,
    )
    total = keep + swap(give, 1)
    total = total + swap(total, 2)
    total = total + swap_level(total, 1)
    total = total + swap_level(total, 2)
    own = trade(jnp.broadcast_to(total[None], (16, *total.shape)), PLANES)
    return own, swap(own, 1)


def dot(a, b):
    return jnp.dot(a, b, precision=HI, preferred_element_type=F32)


def dot_tn(a, b):
    return lax.dot_general(a, b, (((0,), (0,)), ((), ())), precision=HI, preferred_element_type=F32)


def dot_nt(a, b):
    return lax.dot_general(a, b, (((1,), (1,)), ((), ())), precision=HI, preferred_element_type=F32)


def inverse_factor(block):
    groups = NB // 8
    sub = lax.broadcasted_iota(jnp.int32, (8, NB), 0)
    lane = lax.broadcasted_iota(jnp.int32, (8, NB), 1)
    w = [block[8 * g:8 * g + 8, :] for g in range(groups)]
    e = [jnp.where(lane == sub + 8 * g, 1.0, 0.0).astype(F32) for g in range(groups)]
    done = []
    for g in range(groups):
        z, ez = w[g], e[g]
        cols = [jnp.broadcast_to(z[:, 8 * g + k:8 * g + k + 1], (8, NB)) for k in range(8)]
        scale = jnp.zeros((8, NB), F32)
        kept = jnp.zeros((8, NB), F32)
        for k in range(8):
            here = sub == k
            pivot = jnp.broadcast_to(cols[k][k:k + 1, :], (8, NB))
            r = 1.0 / pivot
            zrow = jnp.broadcast_to(z[k:k + 1, :], (8, NB))
            erow = jnp.broadcast_to(ez[k:k + 1, :], (8, NB))
            scale = jnp.where(here, lax.rsqrt(pivot), scale)
            kept = jnp.where(here, erow, kept)
            t = jnp.where(here, 1.0 - r, cols[k] * r)
            z = z - t * zrow
            ez = ez - t * erow
            for l in range(k + 1, 8):
                cols[l] = cols[l] - t * jnp.broadcast_to(cols[l][k:k + 1, :], (8, NB))
        done.append(kept * scale)
        if g + 1 < groups:
            zrows = [jnp.broadcast_to(z[k:k + 1, :], (8, NB)) for k in range(8)]
            erows = [jnp.broadcast_to(ez[k:k + 1, :], (8, NB)) for k in range(8)]
            for i in range(g + 1, groups):
                acc, eacc = w[i], e[i]
                for k in range(8):
                    c = jnp.broadcast_to(w[i][:, 8 * g + k:8 * g + k + 1], (8, NB))
                    acc = acc - c * zrows[k]
                    eacc = eacc - c * erows[k]
                w[i], e[i] = acc, eacc
    return jnp.concatenate(done, axis=0)


def factor_body(own, other, shifted, basis, triangle, work, inv):
    core = lax.rem(lax.axis_index("col"), 2)
    for p in range(16):
        for held, half in ((own, core), (other, 1 - core)):
            here = pl.ds(pl.multiple_of(p * 64 + half * 32, 32), 32)
            for d in range(5):
                block = (p // 2 + d) % 8
                work[here, block * NB:(block + 1) * NB] = held[p, :, d * NB:(d + 1) * NB]
    for i in range(3):
        for j in range(i + 5, 8):
            low = work[j * NB:(j + 1) * NB, i * NB:(i + 1) * NB]
            work[i * NB:(i + 1) * NB, j * NB:(j + 1) * NB] = low.T
    basis[...] = shifted[...]
    rows = lax.broadcasted_iota(jnp.int32, (NB, K), 0)
    lanes = lax.broadcasted_iota(jnp.int32, (NB, K), 1)

    def panel(j, _):
        offset = pl.multiple_of(j * NB, NB)
        here = pl.ds(offset, NB)
        inv[...] = inverse_factor(work[here, here])
        row = dot(inv[...], work[here, :])
        row = jnp.where(lanes >= rows + offset, row, 0.0)
        triangle[here, :] = row
        own = dot_nt(basis[:, here], inv[...])
        basis[...] = basis[...] - dot(own, row)
        basis[:, here] = own

        def trail(k, _):
            there = pl.ds(pl.multiple_of(k * NB, NB), NB)
            work[there, :] = work[there, :] - dot_tn(triangle[here, there], triangle[here, :])
            return 0

        lax.fori_loop(j + 1, K // NB, trail, 0)
        return 0

    lax.fori_loop(0, K // NB, panel, 0)


def local(tile_values, tile_coords, tile_counts, sketch):
    tiles = pltpu.with_memory_space_constraint(tile_values[0, 0], pltpu.HBM)
    strips = pltpu.with_memory_space_constraint(sketch, pltpu.HBM)
    places = tile_coords[0, 0]
    partial = [forward(q, places, tile_counts, tiles, strips) for q in range(PARTS)]
    paired = [(p[0] + swap(p[1], 1), p[2] + swap(p[3], 1)) for p in partial]
    sketch_rows = lax.dynamic_slice_in_dim(sketch, lax.axis_index("row") * 16, 16, 0).astype(F32)
    images, others = [], [other for _, other in paired]
    for q in range(PARTS):
        image = (paired[q][0] + swap(others[q], 2)).astype(BF16)
        image, *others = lax.optimization_barrier((image, *others))
        across = swap(image, 2)
        images.append((image, swap(image, 1), across, swap(across, 1)))
    summed = []
    for four in images:
        part = backward(places, tile_counts, tiles, four)
        part, sketch_rows, *summed = lax.optimization_barrier((part, sketch_rows, *summed))
        summed.append(jnp.sum(trade(part, PLANES), axis=0))
    summed = jnp.concatenate(summed, axis=1)
    summed = jnp.sum(trade(summed.reshape(4, 16, K), COLUMNS), axis=0)
    shifted = summed + shift_weight * sketch_rows
    own, other = gram_parts(shifted, sketch.shape[0] * 4)
    basis, triangle = call(
        factor_body, [((16, K), F32), ((K, K), F32)], [VMEM] * 3, (own, other, shifted),
        scratch=[pltpu.VMEM((K, K), F32), pltpu.VMEM((NB, NB), F32)], limit=40,
        flops=4 * K * K * K, moved=8 << 20,
    )
    return (basis[None], triangle)


def solution(mesh):
    in_specs = (
        P("row", "col", None, None, None),
        P("row", "col", None, None),
        P("row", "col"),
        P("col", None),
    )
    out_specs = (P("col", "row", None), P())
    return jax.shard_map(local, mesh=mesh, in_specs=in_specs, out_specs=out_specs, check_vma=False)
```

```python
import functools

import jax
import jax.numpy as jnp
from jax import lax
from jax.experimental import pallas as pl
from jax.experimental.pallas import tpu as pltpu
from jax.sharding import PartitionSpec as P

F32 = jnp.float32
BF16 = jnp.bfloat16
HI = lax.Precision.HIGHEST
TILE = 512
K = 1024
PARTS = 4
KW = K // PARTS
NB = 128
shift_weight = 0.5

VMEM = pl.BlockSpec(memory_space=pltpu.VMEM)
SMEM = pl.BlockSpec(memory_space=pltpu.SMEM)
HBM = pl.BlockSpec(memory_space=pltpu.HBM)


def call(body, outs, in_specs, args, scratch=(), limit=32, flops=0, moved=0):
    return pl.pallas_call(
        body,
        out_shape=tuple(jax.ShapeDtypeStruct(shape, dtype) for shape, dtype in outs),
        in_specs=in_specs,
        out_specs=tuple(VMEM for _ in outs),
        scratch_shapes=list(scratch),
        compiler_params=pltpu.CompilerParams(vmem_limit_bytes=limit << 20),
        cost_estimate=pl.CostEstimate(flops=flops, bytes_accessed=moved, transcendentals=0),
    )(*args)


PLANES = [[y * 16 + z * 4 + x for y in range(4) for x in range(4)] for z in range(4)]
COLUMNS = [[y * 16 + z * 4 + x for z in range(4)] for y in range(4) for x in range(4)]


def trade(value, groups):
    return lax.all_to_all(value, "row", 0, 0, tiled=True, axis_index_groups=groups)


def swap(value, bit):
    return lax.ppermute(value, "col", [(c, c ^ bit) for c in range(4)])


def swap_level(value, bit):
    return lax.ppermute(value, "row", [(r, r ^ (bit * 4)) for r in range(64)])


def find(places, count, i, j):
    slot, live = jnp.int32(0), jnp.int32(0)
    for s in range(8):
        match = (places[s, 0] == i) & (places[s, 1] == j) & (s < count)
        slot = jnp.where(match, s, slot)
        live = jnp.where(match, 1, live)
    return slot, live


def start_tiles(order, places, count, tiles, held, sems):
    copies, lives = {}, {}
    for n, (k, j) in enumerate(order):
        slot, lives[k, j] = find(places, count[0, 0], lax.axis_index("col") ^ k, j)
        copies[k, j] = pltpu.make_async_copy(tiles.at[slot], held.at[n], sems.at[n])
        copies[k, j].start()
    return copies, lives


def forward_body(parts, places, count, tiles, sketch, *rest):
    outs, held, strip, sems = rest[:-3], rest[-3], rest[-2], rest[-1]
    order = [(k, j) for k in (1, 3, 0, 2) for j in range(2)]
    width = len(parts) * KW
    load = pltpu.make_async_copy(sketch.at[:, pl.ds(parts[0] * KW, width)], strip, sems.at[8])
    load.start()
    copies, lives = start_tiles(order, places, count, tiles, held, sems)
    load.wait()
    for k in (1, 3, 0, 2):
        total = jnp.zeros((TILE, width), F32)
        for j in range(2):
            copies[k, j].wait()
            tile = held[order.index((k, j))]
            product = jnp.dot(tile, strip[j * TILE:(j + 1) * TILE, :], preferred_element_type=F32)
            total = total + jnp.where(lives[k, j] > 0, product, 0.0)
        for n in range(len(parts)):
            piece = total[:, n * KW:(n + 1) * KW]
            if k % 2:
                outs[3 * n + 2][k // 2] = piece
            else:
                outs[3 * n + k // 2][...] = piece


def forward(parts, places, count, tiles, sketch):
    width = len(parts) * KW
    outs = call(
        functools.partial(forward_body, parts),
        [((TILE, KW), F32), ((TILE, KW), F32), ((2, TILE, KW), F32)] * len(parts), [SMEM, SMEM, HBM, HBM],
        (places, count, tiles, sketch),
        scratch=[
            pltpu.VMEM((8, TILE, TILE), BF16), pltpu.VMEM((2 * TILE, width), BF16), pltpu.SemaphoreType.DMA((9,)),
        ],
        limit=20,
    )
    return [outs[3 * n:3 * n + 3] for n in range(len(parts))]


def backward_body(places, count, tiles, i0, i1, i2, i3, out, held, sems):
    images = (i0, i1, i2, i3)
    order = [(k, j) for j in range(2) for k in range(4)]
    copies, lives = start_tiles(order, places, count, tiles, held, sems)
    for j in range(2):
        part = jnp.zeros((TILE, KW), F32)
        for k in range(4):
            copies[k, j].wait()
            product = lax.dot_general(
                held[order.index((k, j))], images[k][...], (((0,), (0,)), ((), ())), preferred_element_type=F32
            )
            part = part + jnp.where(lives[k, j] > 0, product, 0.0)
        for y in range(2):
            for z in range(4):
                for x in range(4):
                    start = y * 256 + z * 64 + x * 16
                    out[(2 * j + y) * 4 + x, z * 16:(z + 1) * 16, :] = part[start:start + 16, :]


def backward(places, count, tiles, images):
    return call(
        backward_body, [((16, 64, KW), F32)], [SMEM, SMEM, HBM] + [VMEM] * 4, (places, count, tiles, *images),
        scratch=[pltpu.VMEM((8, TILE, TILE), BF16), pltpu.SemaphoreType.DMA((8,))],
        limit=20,
    )[0]


def join_body(s0, s1, s2, last, out):
    for n, held in enumerate((s0, s1, s2)):
        for z in range(4):
            out[z, :, n * KW:(n + 1) * KW] = held[z * 16:(z + 1) * 16, :]
    for z in range(4):
        total = last[0, z * 16:(z + 1) * 16, :]
        for p in range(1, 16):
            total = total + last[p, z * 16:(z + 1) * 16, :]
        out[z, :, 3 * KW:] = total


WIDE = 5 * NB


def finish_body(got, sketch_rows, shifted, spread):
    total = (got[0] + got[1]) + (got[2] + got[3]) + shift_weight * sketch_rows[...].astype(F32)
    shifted[...] = total
    for p in range(16):
        for d in range(5):
            block = (p // 2 + d) % 8
            spread[p, :, d * NB:(d + 1) * NB] = total[:, block * NB:(block + 1) * NB]


def strip_body(scale, rows_in, keep, give, strip):
    rows = jnp.concatenate([rows_in[p] for p in range(16)], axis=0)
    strip[...] = scale * lax.dot_general(
        rows[:, :NB], rows, (((0,), (0,)), ((), ())), precision=HI, preferred_element_type=F32
    )
    core = lax.rem(lax.axis_index("col"), 2)
    half = lax.rem(lax.axis_index("row"), 2) * 64
    keep[...] = strip[pl.ds(pl.multiple_of(half + core * 32, 32), 32), :]
    give[...] = strip[pl.ds(pl.multiple_of(half + (1 - core) * 32, 32), 32), :]


def gram_parts(spread, total_columns):
    rows = trade(spread, PLANES)
    keep, give = call(
        functools.partial(strip_body, 1.0 / total_columns), [((32, WIDE), F32)] * 2, [VMEM], (rows,),
        scratch=[pltpu.VMEM((NB, WIDE), F32)], limit=16,
        flops=12 * 256 * NB * WIDE, moved=2 << 20,
    )
    total = keep + swap(give, 1)
    total = total + swap(total, 2)
    total = total + swap_level(total, 1)
    total = total + swap_level(total, 2)
    own = trade(jnp.broadcast_to(total[None], (16, *total.shape)), PLANES)
    return own, swap(own, 1)


def dot(a, b):
    return jnp.dot(a, b, precision=HI, preferred_element_type=F32)


def dot_tn(a, b):
    return lax.dot_general(a, b, (((0,), (0,)), ((), ())), precision=HI, preferred_element_type=F32)


def dot_nt(a, b):
    return lax.dot_general(a, b, (((1,), (1,)), ((), ())), precision=HI, preferred_element_type=F32)


def inverse_factor(block):
    groups = NB // 8
    sub = lax.broadcasted_iota(jnp.int32, (8, NB), 0)
    lane = lax.broadcasted_iota(jnp.int32, (8, NB), 1)
    w = [block[8 * g:8 * g + 8, :] for g in range(groups)]
    e = [jnp.where(lane == sub + 8 * g, 1.0, 0.0).astype(F32) for g in range(groups)]
    done = []
    for g in range(groups):
        z, ez = w[g], e[g]
        cols = [jnp.broadcast_to(z[:, 8 * g + k:8 * g + k + 1], (8, NB)) for k in range(8)]
        scale = jnp.zeros((8, NB), F32)
        kept = jnp.zeros((8, NB), F32)
        for k in range(8):
            here = sub == k
            pivot = jnp.broadcast_to(cols[k][k:k + 1, :], (8, NB))
            r = 1.0 / pivot
            zrow = jnp.broadcast_to(z[k:k + 1, :], (8, NB))
            erow = jnp.broadcast_to(ez[k:k + 1, :], (8, NB))
            scale = jnp.where(here, lax.rsqrt(pivot), scale)
            kept = jnp.where(here, erow, kept)
            t = jnp.where(here, 1.0 - r, cols[k] * r)
            z = z - t * zrow
            ez = ez - t * erow
            for l in range(k + 1, 8):
                cols[l] = cols[l] - t * jnp.broadcast_to(cols[l][k:k + 1, :], (8, NB))
        done.append(kept * scale)
        if g + 1 < groups:
            zrows = [jnp.broadcast_to(z[k:k + 1, :], (8, NB)) for k in range(8)]
            erows = [jnp.broadcast_to(ez[k:k + 1, :], (8, NB)) for k in range(8)]
            for i in range(g + 1, groups):
                acc, eacc = w[i], e[i]
                for k in range(8):
                    c = jnp.broadcast_to(w[i][:, 8 * g + k:8 * g + k + 1], (8, NB))
                    acc = acc - c * zrows[k]
                    eacc = eacc - c * erows[k]
                w[i], e[i] = acc, eacc
    return jnp.concatenate(done, axis=0)


def factor_body(own, other, shifted, basis, triangle, work, inv):
    core = lax.rem(lax.axis_index("col"), 2)
    for p in range(16):
        for held, half in ((own, core), (other, 1 - core)):
            here = pl.ds(pl.multiple_of(p * 64 + half * 32, 32), 32)
            for d in range(5):
                block = (p // 2 + d) % 8
                work[here, block * NB:(block + 1) * NB] = held[p, :, d * NB:(d + 1) * NB]
    for i in range(3):
        for j in range(i + 5, 8):
            low = work[j * NB:(j + 1) * NB, i * NB:(i + 1) * NB]
            work[i * NB:(i + 1) * NB, j * NB:(j + 1) * NB] = low.T
    basis[...] = shifted[...]
    rows = lax.broadcasted_iota(jnp.int32, (NB, K), 0)
    lanes = lax.broadcasted_iota(jnp.int32, (NB, K), 1)

    def panel(j, _):
        offset = pl.multiple_of(j * NB, NB)
        here = pl.ds(offset, NB)
        inv[...] = inverse_factor(work[here, here])
        row = dot(inv[...], work[here, :])
        row = jnp.where(lanes >= rows + offset, row, 0.0)
        triangle[here, :] = row
        own = dot_nt(basis[:, here], inv[...])
        basis[...] = basis[...] - dot(own, row)
        basis[:, here] = own

        def trail(k, _):
            there = pl.ds(pl.multiple_of(k * NB, NB), NB)
            work[there, :] = work[there, :] - dot_tn(triangle[here, there], triangle[here, :])
            return 0

        lax.fori_loop(j + 1, K // NB, trail, 0)
        return 0

    lax.fori_loop(0, K // NB, panel, 0)


def after(value, *others):
    return lax.optimization_barrier((value, *others))[0]


def local(tile_values, tile_coords, tile_counts, sketch):
    tiles = pltpu.with_memory_space_constraint(tile_values[0, 0], pltpu.HBM)
    strips = pltpu.with_memory_space_constraint(sketch, pltpu.HBM)
    places = tile_coords[0, 0]
    sketch_rows = lax.dynamic_slice_in_dim(sketch, lax.axis_index("row") * 16, 16, 0)

    owns, others = [], []

    def pair(part):
        got = swap(part[2], 1)
        owns.append(part[0] + got[0])
        others.append(part[1] + got[1])

    for part in forward(list(range(PARTS)), places, tile_counts, tiles, strips):
        pair(part)
    images, crossed = [], []
    for q in range(PARTS):
        got = swap(others[q] if q < 2 else after(others[q], images[q - 2]), 2)
        if q == 0:
            got, others[1] = lax.optimization_barrier((got, others[1]))
        images.append((owns[q] + got).astype(BF16))
    for q in range(PARTS):
        crossed.append(swap(images[q], 2))
    summed = []
    for q, image in enumerate(images):
        across = crossed[q]
        if q < PARTS - 1:
            across, images[q + 1] = lax.optimization_barrier((across, images[q + 1]))
        four = (image, swap(image, 1), across, swap(across, 1))
        part = backward(places, tile_counts, tiles, four)
        if q == PARTS - 1:
            part, sketch_rows, *summed = lax.optimization_barrier((part, sketch_rows, *summed))
            summed.append(trade(part, PLANES))
        else:
            summed.append(jnp.sum(trade(part, PLANES), axis=0))
    joined = call(join_body, [((4, 16, K), F32)], [VMEM] * 4, summed, limit=16, moved=2 << 20)[0]
    shifted, spread = call(
        finish_body, [((16, K), F32), ((16, 16, WIDE), F32)], [VMEM] * 2, (trade(joined, COLUMNS), sketch_rows),
        limit=16, moved=1 << 20,
    )
    own, other = gram_parts(spread, sketch.shape[0] * 4)
    basis, triangle = call(
        factor_body, [((16, K), F32), ((K, K), F32)], [VMEM] * 3, (own, other, shifted),
        scratch=[pltpu.VMEM((K, K), F32), pltpu.VMEM((NB, NB), F32)], limit=40,
        flops=4 * K * K * K, moved=8 << 20,
    )
    return (basis[None], triangle)


def solution(mesh):
    in_specs = (
        P("row", "col", None, None, None),
        P("row", "col", None, None),
        P("row", "col"),
        P("col", None),
    )
    out_specs = (P("col", "row", None), P())
    return jax.shard_map(local, mesh=mesh, in_specs=in_specs, out_specs=out_specs, check_vma=False)
```

```python
import functools

import jax
import jax.numpy as jnp
from jax import lax
from jax.experimental import pallas as pl
from jax.experimental.pallas import tpu as pltpu
from jax.sharding import PartitionSpec as P

F32 = jnp.float32
BF16 = jnp.bfloat16
HI = lax.Precision.HIGHEST
TILE = 512
K = 1024
PARTS = 2
KW = K // PARTS
NB = 128
shift_weight = 0.5

VMEM = pl.BlockSpec(memory_space=pltpu.VMEM)
SMEM = pl.BlockSpec(memory_space=pltpu.SMEM)
HBM = pl.BlockSpec(memory_space=pltpu.HBM)


def call(body, outs, in_specs, args, scratch=(), limit=32, flops=0, moved=0):
    return pl.pallas_call(
        body,
        out_shape=tuple(jax.ShapeDtypeStruct(shape, dtype) for shape, dtype in outs),
        in_specs=in_specs,
        out_specs=tuple(VMEM for _ in outs),
        scratch_shapes=list(scratch),
        compiler_params=pltpu.CompilerParams(vmem_limit_bytes=limit << 20),
        cost_estimate=pl.CostEstimate(flops=flops, bytes_accessed=moved, transcendentals=0),
    )(*args)


PLANES = [[y * 16 + z * 4 + x for y in range(4) for x in range(4)] for z in range(4)]
COLUMNS = [[y * 16 + z * 4 + x for z in range(4)] for y in range(4) for x in range(4)]


def trade(value, groups):
    return lax.all_to_all(value, "row", 0, 0, tiled=True, axis_index_groups=groups)


def swap(value, bit):
    return lax.ppermute(value, "col", [(c, c ^ bit) for c in range(4)])


def swap_level(value, bit):
    return lax.ppermute(value, "row", [(r, r ^ (bit * 4)) for r in range(64)])


def find(places, count, i, j):
    slot, live = jnp.int32(0), jnp.int32(0)
    for s in range(8):
        match = (places[s, 0] == i) & (places[s, 1] == j) & (s < count)
        slot = jnp.where(match, s, slot)
        live = jnp.where(match, 1, live)
    return slot, live


def start_tiles(order, places, count, tiles, target, sems):
    copies, lives = {}, {}
    for n, (k, j) in enumerate(order):
        slot, lives[k, j] = find(places, count[0, 0], lax.axis_index("col") ^ k, j)
        copies[k, j] = pltpu.make_async_copy(tiles.at[slot], target(k, j), sems.at[n])
        copies[k, j].start()
    return copies, lives


def finish_tile(copy, live, target):
    copy.wait()

    @pl.when(live == 0)
    def _():
        target[...] = jnp.zeros((TILE, TILE), BF16)


def forward_body(places, count, tiles, sketch, *rest):
    outs, held, strip, sems = rest[:-3], rest[-3], rest[-2], rest[-1]
    order = [(k, j) for k in (1, 3, 0, 2) for j in range(2)]

    def target(k, j):
        return held.at[k, :, pl.ds(j * TILE, TILE)]

    load = pltpu.make_async_copy(sketch, strip, sems.at[8])
    load.start()
    copies, lives = start_tiles(order, places, count, tiles, target, sems)
    load.wait()
    for k in (1, 3, 0, 2):
        for j in range(2):
            finish_tile(copies[k, j], lives[k, j], target(k, j))
        total = jnp.dot(held[k], strip[...], preferred_element_type=F32)
        for n in range(PARTS):
            piece = total[:, n * KW:(n + 1) * KW]
            if k % 2:
                outs[3 * n + 2][k // 2] = piece
            else:
                outs[3 * n + k // 2][...] = piece


def forward(places, count, tiles, sketch):
    outs = call(
        forward_body, [((TILE, KW), F32), ((TILE, KW), F32), ((2, TILE, KW), F32)] * PARTS, [SMEM, SMEM, HBM, HBM],
        (places, count, tiles, sketch),
        scratch=[
            pltpu.VMEM((4, TILE, 2 * TILE), BF16), pltpu.VMEM((2 * TILE, K), BF16), pltpu.SemaphoreType.DMA((9,)),
        ],
        limit=24,
    )
    return [outs[3 * n:3 * n + 3] for n in range(PARTS)]


def backward_body(places, count, tiles, i0, i1, i2, i3, out, held, sems):
    order = [(k, j) for j in range(2) for k in range(4)]

    def target(k, j):
        return held.at[j, pl.ds(k * TILE, TILE), :]

    copies, lives = start_tiles(order, places, count, tiles, target, sems)
    image = jnp.concatenate([i0[...], i1[...], i2[...], i3[...]], axis=0)
    for j in range(2):
        for k in range(4):
            finish_tile(copies[k, j], lives[k, j], target(k, j))
        part = lax.dot_general(held[j], image, (((0,), (0,)), ((), ())), preferred_element_type=F32)
        for y in range(2):
            for z in range(4):
                for x in range(4):
                    start = y * 256 + z * 64 + x * 16
                    out[(2 * j + y) * 4 + x, z * 16:(z + 1) * 16, :] = part[start:start + 16, :]


def backward(places, count, tiles, images):
    return call(
        backward_body, [((16, 64, KW), F32)], [SMEM, SMEM, HBM] + [VMEM] * 4, (places, count, tiles, *images),
        scratch=[pltpu.VMEM((2, 4 * TILE, TILE), BF16), pltpu.SemaphoreType.DMA((8,))],
        limit=24, flops=16 * TILE * TILE * KW, moved=8 << 20,
    )[0]


def sum16(held, rows):
    total = held[0, rows, :]
    for p in range(1, 16):
        total = total + held[p, rows, :]
    return total


def first_body(held, out):
    for z in range(4):
        rows = slice(z * 16, (z + 1) * 16)
        out[rows, :] = sum16(held, rows)


def join_body(first, last, out):
    for z in range(4):
        rows = slice(z * 16, (z + 1) * 16)
        out[z, :, :KW] = first[rows, :]
        out[z, :, KW:] = sum16(last, rows)


WIDE = 5 * NB


def finish_body(got, sketch_rows, shifted, spread):
    total = (got[0] + got[1]) + (got[2] + got[3]) + shift_weight * sketch_rows[...].astype(F32)
    shifted[...] = total
    for p in range(16):
        for d in range(5):
            block = (p // 2 + d) % 8
            spread[p, :, d * NB:(d + 1) * NB] = total[:, block * NB:(block + 1) * NB]


def strip_body(scale, rows_in, keep, give, strip):
    rows = jnp.concatenate([rows_in[p] for p in range(16)], axis=0)
    strip[...] = scale * lax.dot_general(
        rows[:, :NB], rows, (((0,), (0,)), ((), ())), precision=HI, preferred_element_type=F32
    )
    core = lax.rem(lax.axis_index("col"), 2)
    half = lax.rem(lax.axis_index("row"), 2) * 64
    keep[...] = strip[pl.ds(pl.multiple_of(half + core * 32, 32), 32), :]
    give[...] = strip[pl.ds(pl.multiple_of(half + (1 - core) * 32, 32), 32), :]


def gram_parts(spread, total_columns):
    rows = trade(spread, PLANES)
    keep, give = call(
        functools.partial(strip_body, 1.0 / total_columns), [((32, WIDE), F32)] * 2, [VMEM], (rows,),
        scratch=[pltpu.VMEM((NB, WIDE), F32)], limit=16,
        flops=12 * 256 * NB * WIDE, moved=2 << 20,
    )
    total = keep + swap(give, 1)
    total = total + swap(total, 2)
    total = total + swap_level(total, 1)
    total = total + swap_level(total, 2)
    own = trade(jnp.broadcast_to(total[None], (16, *total.shape)), PLANES)
    return own, swap(own, 1)


def dot(a, b):
    return jnp.dot(a, b, precision=HI, preferred_element_type=F32)


def dot_tn(a, b):
    return lax.dot_general(a, b, (((0,), (0,)), ((), ())), precision=HI, preferred_element_type=F32)


def dot_nt(a, b):
    return lax.dot_general(a, b, (((1,), (1,)), ((), ())), precision=HI, preferred_element_type=F32)


def inverse_factor(block):
    groups = NB // 8
    sub = lax.broadcasted_iota(jnp.int32, (8, NB), 0)
    lane = lax.broadcasted_iota(jnp.int32, (8, NB), 1)
    w = [block[8 * g:8 * g + 8, :] for g in range(groups)]
    e = [jnp.where(lane == sub + 8 * g, 1.0, 0.0).astype(F32) for g in range(groups)]
    done = []
    for g in range(groups):
        z, ez = w[g], e[g]
        cols = [jnp.broadcast_to(z[:, 8 * g + k:8 * g + k + 1], (8, NB)) for k in range(8)]
        scale = jnp.zeros((8, NB), F32)
        kept = jnp.zeros((8, NB), F32)
        for k in range(8):
            here = sub == k
            pivot = jnp.broadcast_to(cols[k][k:k + 1, :], (8, NB))
            r = 1.0 / pivot
            zrow = jnp.broadcast_to(z[k:k + 1, :], (8, NB))
            erow = jnp.broadcast_to(ez[k:k + 1, :], (8, NB))
            scale = jnp.where(here, lax.rsqrt(pivot), scale)
            kept = jnp.where(here, erow, kept)
            t = jnp.where(here, 1.0 - r, cols[k] * r)
            z = z - t * zrow
            ez = ez - t * erow
            for l in range(k + 1, 8):
                cols[l] = cols[l] - t * jnp.broadcast_to(cols[l][k:k + 1, :], (8, NB))
        done.append(kept * scale)
        if g + 1 < groups:
            zrows = [jnp.broadcast_to(z[k:k + 1, :], (8, NB)) for k in range(8)]
            erows = [jnp.broadcast_to(ez[k:k + 1, :], (8, NB)) for k in range(8)]
            for i in range(g + 1, groups):
                acc, eacc = w[i], e[i]
                for k in range(8):
                    c = jnp.broadcast_to(w[i][:, 8 * g + k:8 * g + k + 1], (8, NB))
                    acc = acc - c * zrows[k]
                    eacc = eacc - c * erows[k]
                w[i], e[i] = acc, eacc
    return jnp.concatenate(done, axis=0)


def factor_body(own, other, shifted, basis, triangle, work, inv):
    core = lax.rem(lax.axis_index("col"), 2)
    for p in range(16):
        for held, half in ((own, core), (other, 1 - core)):
            here = pl.ds(pl.multiple_of(p * 64 + half * 32, 32), 32)
            for d in range(5):
                block = (p // 2 + d) % 8
                work[here, block * NB:(block + 1) * NB] = held[p, :, d * NB:(d + 1) * NB]
    for i in range(3):
        for j in range(i + 5, 8):
            low = work[j * NB:(j + 1) * NB, i * NB:(i + 1) * NB]
            work[i * NB:(i + 1) * NB, j * NB:(j + 1) * NB] = low.T
    basis[...] = shifted[...]
    rows = lax.broadcasted_iota(jnp.int32, (NB, K), 0)
    lanes = lax.broadcasted_iota(jnp.int32, (NB, K), 1)

    def panel(j, _):
        offset = pl.multiple_of(j * NB, NB)
        here = pl.ds(offset, NB)
        inv[...] = inverse_factor(work[here, here])
        row = dot(inv[...], work[here, :])
        row = jnp.where(lanes >= rows + offset, row, 0.0)
        triangle[here, :] = row
        own = dot_nt(basis[:, here], inv[...])
        basis[...] = basis[...] - dot(own, row)
        basis[:, here] = own

        def trail(k, _):
            there = pl.ds(pl.multiple_of(k * NB, NB), NB)
            work[there, :] = work[there, :] - dot_tn(triangle[here, there], triangle[here, :])
            return 0

        lax.fori_loop(j + 1, K // NB, trail, 0)
        return 0

    lax.fori_loop(0, K // NB, panel, 0)


def after(value, *others):
    return lax.optimization_barrier((value, *others))[0]


def local(tile_values, tile_coords, tile_counts, sketch):
    tiles = pltpu.with_memory_space_constraint(tile_values[0, 0], pltpu.HBM)
    strips = pltpu.with_memory_space_constraint(sketch, pltpu.HBM)
    places = tile_coords[0, 0]
    sketch_rows = lax.dynamic_slice_in_dim(sketch, lax.axis_index("row") * 16, 16, 0)

    owns, others = [], []

    def pair(part):
        got = swap(part[2], 1)
        owns.append(part[0] + got[0])
        others.append(part[1] + got[1])

    for part in forward(places, tile_counts, tiles, strips):
        pair(part)
    images = []
    for q in range(PARTS):
        image = (owns[q] + swap(others[q], 2)).astype(BF16)
        across, beside = swap(image, 2), swap(image, 1)
        across, *others = lax.optimization_barrier((across, *others))
        images.append((image, beside, across, swap(across, 1)))
    first = backward(places, tile_counts, tiles, images[0])
    first = call(first_body, [((64, KW), F32)], [VMEM], (trade(first, PLANES),), limit=16)[0]
    last = backward(places, tile_counts, tiles, images[1])
    last, first, sketch_rows = lax.optimization_barrier((last, first, sketch_rows))
    joined = call(join_body, [((4, 16, K), F32)], [VMEM] * 2, (first, trade(last, PLANES)), limit=16)[0]
    shifted, spread = call(
        finish_body, [((16, K), F32), ((16, 16, WIDE), F32)], [VMEM] * 2, (trade(joined, COLUMNS), sketch_rows),
        limit=16, moved=1 << 20,
    )
    own, other = gram_parts(spread, sketch.shape[0] * 4)
    basis, triangle = call(
        factor_body, [((16, K), F32), ((K, K), F32)], [VMEM] * 3, (own, other, shifted),
        scratch=[pltpu.VMEM((K, K), F32), pltpu.VMEM((NB, NB), F32)], limit=40,
        flops=4 * K * K * K, moved=8 << 20,
    )
    return (basis[None], triangle)


def solution(mesh):
    in_specs = (
        P("row", "col", None, None, None),
        P("row", "col", None, None),
        P("row", "col"),
        P("col", None),
    )
    out_specs = (P("col", "row", None), P())
    return jax.shard_map(local, mesh=mesh, in_specs=in_specs, out_specs=out_specs, check_vma=False)
```

```python
import functools

import jax
import jax.numpy as jnp
from jax import lax
from jax.experimental import pallas as pl
from jax.experimental.pallas import tpu as pltpu
from jax.sharding import PartitionSpec as P

F32 = jnp.float32
BF16 = jnp.bfloat16
HI = lax.Precision.HIGHEST
TILE = 512
K = 1024
PARTS = 2
KW = K // PARTS
NB = 128
shift_weight = 0.5

VMEM = pl.BlockSpec(memory_space=pltpu.VMEM)
SMEM = pl.BlockSpec(memory_space=pltpu.SMEM)
HBM = pl.BlockSpec(memory_space=pltpu.HBM)


def call(body, outs, in_specs, args, scratch=(), limit=32, flops=0, moved=0):
    return pl.pallas_call(
        body,
        out_shape=tuple(jax.ShapeDtypeStruct(shape, dtype) for shape, dtype in outs),
        in_specs=in_specs,
        out_specs=tuple(VMEM for _ in outs),
        scratch_shapes=list(scratch),
        compiler_params=pltpu.CompilerParams(vmem_limit_bytes=limit << 20),
        cost_estimate=pl.CostEstimate(flops=flops, bytes_accessed=moved, transcendentals=0),
    )(*args)


PLANES = [[y * 16 + z * 4 + x for y in range(4) for x in range(4)] for z in range(4)]
COLUMNS = [[y * 16 + z * 4 + x for z in range(4)] for y in range(4) for x in range(4)]


def trade(value, groups):
    return lax.all_to_all(value, "row", 0, 0, tiled=True, axis_index_groups=groups)


def swap(value, bit):
    return lax.ppermute(value, "col", [(c, c ^ bit) for c in range(4)])


def swap_level(value, bit):
    return lax.ppermute(value, "row", [(r, r ^ (bit * 4)) for r in range(64)])


def find(places, count, i, j):
    slot, live = jnp.int32(0), jnp.int32(0)
    for s in range(8):
        match = (places[s, 0] == i) & (places[s, 1] == j) & (s < count)
        slot = jnp.where(match, s, slot)
        live = jnp.where(match, 1, live)
    return slot, live


def start_tiles(order, places, count, tiles, target, sems):
    copies, lives = {}, {}
    for n, (k, j) in enumerate(order):
        slot, lives[k, j] = find(places, count[0, 0], lax.axis_index("col") ^ k, j)
        copies[k, j] = pltpu.make_async_copy(tiles.at[slot], target(k, j), sems.at[n])
        copies[k, j].start()
    return copies, lives


def finish_tile(copy, live, target):
    copy.wait()

    @pl.when(live == 0)
    def _():
        target[...] = jnp.zeros((TILE, TILE), BF16)


def forward_body(places, count, tiles, sketch, *rest):
    outs, held, strip, sems = rest[:-3], rest[-3], rest[-2], rest[-1]
    order = [(k, j) for k in (1, 3, 0, 2) for j in range(2)]

    def target(k, j):
        return held.at[k, :, pl.ds(j * TILE, TILE)]

    load = pltpu.make_async_copy(sketch, strip, sems.at[8])
    load.start()
    copies, lives = start_tiles(order, places, count, tiles, target, sems)
    load.wait()
    for k in (1, 3, 0, 2):
        for j in range(2):
            finish_tile(copies[k, j], lives[k, j], target(k, j))
        total = jnp.dot(held[k], strip[...], preferred_element_type=F32)
        for n in range(PARTS):
            piece = total[:, n * KW:(n + 1) * KW]
            if k % 2:
                outs[3 * n + 2][k // 2] = piece
            else:
                outs[3 * n + k // 2][...] = piece


def forward(places, count, tiles, sketch):
    outs = call(
        forward_body, [((TILE, KW), F32), ((TILE, KW), F32), ((2, TILE, KW), F32)] * PARTS, [SMEM, SMEM, HBM, HBM],
        (places, count, tiles, sketch),
        scratch=[
            pltpu.VMEM((4, TILE, 2 * TILE), BF16), pltpu.VMEM((2 * TILE, K), BF16), pltpu.SemaphoreType.DMA((9,)),
        ],
        limit=24,
    )
    return [outs[3 * n:3 * n + 3] for n in range(PARTS)]


def backward_body(places, count, tiles, i0, i1, i2, i3, out, held, sems):
    order = [(k, j) for j in range(2) for k in range(4)]

    def target(k, j):
        return held.at[j, pl.ds(k * TILE, TILE), :]

    copies, lives = start_tiles(order, places, count, tiles, target, sems)
    image = jnp.concatenate([i0[...], i1[...], i2[...], i3[...]], axis=0)
    for j in range(2):
        for k in range(4):
            finish_tile(copies[k, j], lives[k, j], target(k, j))
        part = lax.dot_general(held[j], image, (((0,), (0,)), ((), ())), preferred_element_type=F32)
        for y in range(2):
            for z in range(4):
                for x in range(4):
                    start = y * 256 + z * 64 + x * 16
                    out[(2 * j + y) * 4 + x, z * 16:(z + 1) * 16, :] = part[start:start + 16, :]


def backward(places, count, tiles, images):
    return call(
        backward_body, [((16, 64, KW), F32)], [SMEM, SMEM, HBM] + [VMEM] * 4, (places, count, tiles, *images),
        scratch=[pltpu.VMEM((2, 4 * TILE, TILE), BF16), pltpu.SemaphoreType.DMA((8,))],
        limit=24, flops=16 * TILE * TILE * KW, moved=8 << 20,
    )[0]


def sum16(held, rows):
    total = held[0, rows, :]
    for p in range(1, 16):
        total = total + held[p, rows, :]
    return total


def first_body(held, out):
    for z in range(4):
        rows = slice(z * 16, (z + 1) * 16)
        out[rows, :] = sum16(held, rows)


def join_body(first, last, out):
    for z in range(4):
        rows = slice(z * 16, (z + 1) * 16)
        out[z, :, :KW] = first[rows, :]
        out[z, :, KW:] = sum16(last, rows)


WIDE = 5 * NB


def finish_body(got, sketch_rows, shifted, spread):
    total = (got[0] + got[1]) + (got[2] + got[3]) + shift_weight * sketch_rows[...].astype(F32)
    shifted[...] = total
    for p in range(16):
        for d in range(5):
            block = (p // 2 + d) % 8
            spread[p, :, d * NB:(d + 1) * NB] = total[:, block * NB:(block + 1) * NB]


def strip_body(scale, rows_in, keep, give, strip):
    rows = jnp.concatenate([rows_in[p] for p in range(16)], axis=0)
    strip[...] = scale * lax.dot_general(
        rows[:, :NB], rows, (((0,), (0,)), ((), ())), precision=HI, preferred_element_type=F32
    )
    core = lax.rem(lax.axis_index("col"), 2)
    half = lax.rem(lax.axis_index("row"), 2) * 64
    keep[...] = strip[pl.ds(pl.multiple_of(half + core * 32, 32), 32), :]
    give[...] = strip[pl.ds(pl.multiple_of(half + (1 - core) * 32, 32), 32), :]


def gram_parts(spread, total_columns):
    rows = trade(spread, PLANES)
    keep, give = call(
        functools.partial(strip_body, 1.0 / total_columns), [((32, WIDE), F32)] * 2, [VMEM], (rows,),
        scratch=[pltpu.VMEM((NB, WIDE), F32)], limit=16,
        flops=12 * 256 * NB * WIDE, moved=2 << 20,
    )
    total = keep + swap(give, 1)
    total = total + swap(total, 2)
    total = total + swap_level(total, 1)
    total = total + swap_level(total, 2)
    own = trade(jnp.broadcast_to(total[None], (16, *total.shape)), PLANES)
    return own, swap(own, 1)


def dot(a, b):
    return jnp.dot(a, b, precision=HI, preferred_element_type=F32)


def dot_tn(a, b):
    return lax.dot_general(a, b, (((0,), (0,)), ((), ())), precision=HI, preferred_element_type=F32)


def dot_nt(a, b):
    return lax.dot_general(a, b, (((1,), (1,)), ((), ())), precision=HI, preferred_element_type=F32)


def down(value, k):
    return jnp.broadcast_to(value[k:k + 1, :], (8, NB))


def along(value, k):
    return jnp.broadcast_to(value[:, k:k + 1], (8, NB))


def add_up(terms):
    while len(terms) > 1:
        pairs = [a + b for a, b in zip(terms[::2], terms[1::2])]
        terms = pairs + terms[2 * len(pairs):]
    return terms[0]


def inverse_factor(block):
    groups = NB // 8
    sub = lax.broadcasted_iota(jnp.int32, (8, NB), 0)
    lane = lax.broadcasted_iota(jnp.int32, (8, NB), 1)
    w = [block[8 * g:8 * g + 8, :] for g in range(groups)]
    e = [jnp.where(lane == sub + 8 * g, 1.0, 0.0).astype(F32) for g in range(groups)]
    done = []
    cols = [along(w[0], k) for k in range(8)]
    for g in range(groups):
        z, ez = w[g], e[g]
        ahead, base = [], []
        if g + 1 < groups:
            ahead = [along(z, 8 * g + 8 + k) for k in range(8)]
            base = [along(w[g + 1], 8 * g + 8 + k) for k in range(8)]
        factors = [[along(w[i], 8 * g + k) for k in range(8)] for i in range(g + 1, groups)]
        scale = jnp.zeros((8, NB), F32)
        kept = jnp.zeros((8, NB), F32)
        for k in range(8):
            here = sub == k
            pivot = down(cols[k], k)
            r = 1.0 / pivot
            t = jnp.where(here, 1.0 - r, cols[k] * r)
            for n in range(k + 1, 8):
                cols[n] = cols[n] - t * down(cols[n], k)
            zrow, erow = down(z, k), down(ez, k)
            scale = jnp.where(here, lax.rsqrt(pivot), scale)
            kept = jnp.where(here, erow, kept)
            z = z - t * zrow
            ez = ez - t * erow
            ahead = [v - t * down(v, k) for v in ahead]
        done.append(kept * scale)
        if g + 1 < groups:
            cols = [base[k] - add_up([factors[0][m] * down(ahead[k], m) for m in range(8)]) for k in range(8)]
            zrows, erows = [down(z, k) for k in range(8)], [down(ez, k) for k in range(8)]
            for f, i in zip(factors, range(g + 1, groups)):
                w[i] = w[i] - add_up([f[k] * zrows[k] for k in range(8)])
                e[i] = e[i] - add_up([f[k] * erows[k] for k in range(8)])
    return jnp.concatenate(done, axis=0)


def factor_body(own, other, shifted, basis, triangle, work):
    core = lax.rem(lax.axis_index("col"), 2)
    for p in range(16):
        for held, half in ((own, core), (other, 1 - core)):
            here = pl.ds(pl.multiple_of(p * 64 + half * 32, 32), 32)
            for d in range(5):
                block = (p // 2 + d) % 8
                work[here, block * NB:(block + 1) * NB] = held[p, :, d * NB:(d + 1) * NB]
    for i in range(3):
        for j in range(i + 5, 8):
            low = work[j * NB:(j + 1) * NB, i * NB:(i + 1) * NB]
            work[i * NB:(i + 1) * NB, j * NB:(j + 1) * NB] = low.T
    basis[...] = shifted[...]
    upper = lax.broadcasted_iota(jnp.int32, (NB, NB), 1) >= lax.broadcasted_iota(jnp.int32, (NB, NB), 0)
    for j in range(K // NB):
        here, near, far = slice(j * NB, (j + 1) * NB), slice((j + 1) * NB, (j + 2) * NB), slice((j + 2) * NB, K)
        inverse = inverse_factor(work[here, here])
        if near.start < K:
            beside = dot(inverse, work[here, near])
            work[near, near] = work[near, near] - dot_tn(beside, beside)
            triangle[here, near] = beside
        if j:
            triangle[here, :j * NB] = jnp.zeros((NB, j * NB), F32)
        triangle[here, here] = jnp.where(upper, dot(inverse, work[here, here]), 0.0)
        if far.start < K:
            rest = dot(inverse, work[here, far])
            triangle[here, far] = rest
            work[near, far] = work[near, far] - dot_tn(beside, rest)
            work[far, far] = work[far, far] - dot_tn(rest, rest)
        own = dot_nt(basis[:, here], inverse)
        basis[:, here] = own
        if near.start < K:
            basis[:, near.start:] = basis[:, near.start:] - dot(own, triangle[here, near.start:])


def after(value, *others):
    return lax.optimization_barrier((value, *others))[0]


def local(tile_values, tile_coords, tile_counts, sketch):
    tiles = pltpu.with_memory_space_constraint(tile_values[0, 0], pltpu.HBM)
    strips = pltpu.with_memory_space_constraint(sketch, pltpu.HBM)
    places = tile_coords[0, 0]
    sketch_rows = lax.dynamic_slice_in_dim(sketch, lax.axis_index("row") * 16, 16, 0)

    owns, others = [], []

    def pair(part):
        got = swap(part[2], 1)
        owns.append(part[0] + got[0])
        others.append(part[1] + got[1])

    for part in forward(places, tile_counts, tiles, strips):
        pair(part)
    images = []
    for q in range(PARTS):
        image = (owns[q] + swap(others[q], 2)).astype(BF16)
        across, beside = swap(image, 2), swap(image, 1)
        across, *others = lax.optimization_barrier((across, *others))
        images.append((image, beside, across, swap(across, 1)))
    first = backward(places, tile_counts, tiles, images[0])
    first = call(first_body, [((64, KW), F32)], [VMEM], (trade(first, PLANES),), limit=16)[0]
    last = backward(places, tile_counts, tiles, images[1])
    last, first, sketch_rows = lax.optimization_barrier((last, first, sketch_rows))
    joined = call(join_body, [((4, 16, K), F32)], [VMEM] * 2, (first, trade(last, PLANES)), limit=16)[0]
    shifted, spread = call(
        finish_body, [((16, K), F32), ((16, 16, WIDE), F32)], [VMEM] * 2, (trade(joined, COLUMNS), sketch_rows),
        limit=16, moved=1 << 20,
    )
    own, other = gram_parts(spread, sketch.shape[0] * 4)
    basis, triangle = call(
        factor_body, [((16, K), F32), ((K, K), F32)], [VMEM] * 3, (own, other, shifted),
        scratch=[pltpu.VMEM((K, K), F32)], limit=40,
        flops=4 * K * K * K, moved=8 << 20,
    )
    return (basis[None], triangle)


def solution(mesh):
    in_specs = (
        P("row", "col", None, None, None),
        P("row", "col", None, None),
        P("row", "col"),
        P("col", None),
    )
    out_specs = (P("col", "row", None), P())
    return jax.shard_map(local, mesh=mesh, in_specs=in_specs, out_specs=out_specs, check_vma=False)
```

```python
import functools

import jax
import jax.numpy as jnp
from jax import lax
from jax.experimental import pallas as pl
from jax.experimental.pallas import tpu as pltpu
from jax.sharding import PartitionSpec as P

F32 = jnp.float32
BF16 = jnp.bfloat16
HI = lax.Precision.HIGHEST
TILE = 512
K = 1024
PARTS = 2
KW = K // PARTS
NB = 128
shift_weight = 0.5

VMEM = pl.BlockSpec(memory_space=pltpu.VMEM)
SMEM = pl.BlockSpec(memory_space=pltpu.SMEM)
HBM = pl.BlockSpec(memory_space=pltpu.HBM)


def call(body, outs, in_specs, args, scratch=(), limit=32, flops=0, moved=0):
    return pl.pallas_call(
        body,
        out_shape=tuple(jax.ShapeDtypeStruct(shape, dtype) for shape, dtype in outs),
        in_specs=in_specs,
        out_specs=tuple(VMEM for _ in outs),
        scratch_shapes=list(scratch),
        compiler_params=pltpu.CompilerParams(vmem_limit_bytes=limit << 20),
        cost_estimate=pl.CostEstimate(flops=flops, bytes_accessed=moved, transcendentals=0),
    )(*args)


PLANES = [[y * 16 + z * 4 + x for y in range(4) for x in range(4)] for z in range(4)]
COLUMNS = [[y * 16 + z * 4 + x for z in range(4)] for y in range(4) for x in range(4)]


def trade(value, groups):
    return lax.all_to_all(value, "row", 0, 0, tiled=True, axis_index_groups=groups)


def swap(value, bit):
    return lax.ppermute(value, "col", [(c, c ^ bit) for c in range(4)])


def swap_level(value, bit):
    return lax.ppermute(value, "row", [(r, r ^ (bit * 4)) for r in range(64)])


CODED = 80


def encode(value):
    top = jnp.maximum(jnp.max(jnp.abs(value), axis=0, keepdims=True), 1e-30)
    power = jnp.floor(jnp.log2(top)) + 1.0
    scaled = jnp.clip(jnp.round(value * jnp.exp2(15.0 - power)), -32767.0, 32767.0)
    return scaled.astype(jnp.int32).astype(jnp.int16), power


def widen(power):
    return jnp.broadcast_to(power, (16, power.shape[1])).astype(jnp.int32).astype(jnp.int16)


def floats(code):
    return code.astype(jnp.int32).astype(F32)


def find(places, count, i, j):
    slot, live = jnp.int32(0), jnp.int32(0)
    for s in range(8):
        match = (places[s, 0] == i) & (places[s, 1] == j) & (s < count)
        slot = jnp.where(match, s, slot)
        live = jnp.where(match, 1, live)
    return slot, live


def start_tiles(order, places, count, tiles, target, sems):
    copies, lives = {}, {}
    for n, (k, j) in enumerate(order):
        slot, lives[k, j] = find(places, count[0, 0], lax.axis_index("col") ^ k, j)
        copies[k, j] = pltpu.make_async_copy(tiles.at[slot], target(k, j), sems.at[n])
        copies[k, j].start()
    return copies, lives


def finish_tile(copy, live, target):
    copy.wait()

    @pl.when(live == 0)
    def _():
        target[...] = jnp.zeros((TILE, TILE), BF16)


def forward_body(places, count, tiles, sketch, *rest):
    outs, held, strip, sems = rest[:-3], rest[-3], rest[-2], rest[-1]
    order = [(k, j) for k in (1, 3, 0, 2) for j in range(2)]

    def target(k, j):
        return held.at[k, :, pl.ds(j * TILE, TILE)]

    load = pltpu.make_async_copy(sketch, strip, sems.at[8])
    load.start()
    copies, lives = start_tiles(order, places, count, tiles, target, sems)
    load.wait()
    for k in (1, 3, 0, 2):
        for j in range(2):
            finish_tile(copies[k, j], lives[k, j], target(k, j))
        total = jnp.dot(held[k], strip[...], preferred_element_type=F32)
        for n in range(PARTS):
            piece = total[:, n * KW:(n + 1) * KW]
            if k % 2:
                outs[3 * n + 2][k // 2] = piece
            else:
                outs[3 * n + k // 2][...] = piece


def forward(places, count, tiles, sketch):
    outs = call(
        forward_body, [((TILE, KW), F32), ((TILE, KW), F32), ((2, TILE, KW), F32)] * PARTS, [SMEM, SMEM, HBM, HBM],
        (places, count, tiles, sketch),
        scratch=[
            pltpu.VMEM((4, TILE, 2 * TILE), BF16), pltpu.VMEM((2 * TILE, K), BF16), pltpu.SemaphoreType.DMA((9,)),
        ],
        limit=24,
    )
    return [outs[3 * n:3 * n + 3] for n in range(PARTS)]


def backward_body(places, count, tiles, i0, i1, i2, i3, out, held, sems):
    order = [(k, j) for j in range(2) for k in range(4)]

    def target(k, j):
        return held.at[j, pl.ds(k * TILE, TILE), :]

    copies, lives = start_tiles(order, places, count, tiles, target, sems)
    image = jnp.concatenate([i0[...], i1[...], i2[...], i3[...]], axis=0)
    for j in range(2):
        for k in range(4):
            finish_tile(copies[k, j], lives[k, j], target(k, j))
        part = lax.dot_general(held[j], image, (((0,), (0,)), ((), ())), preferred_element_type=F32)
        for y in range(2):
            for x in range(4):
                starts = [y * 256 + z * 64 + x * 16 for z in range(4)]
                code, power = encode(jnp.concatenate([part[r:r + 16, :] for r in starts], axis=0))
                out[(2 * j + y) * 4 + x, :64, :] = code
                out[(2 * j + y) * 4 + x, 64:, :] = widen(power)


def backward(places, count, tiles, images):
    return call(
        backward_body, [((16, CODED, KW), jnp.int16)], [SMEM, SMEM, HBM] + [VMEM] * 4, (places, count, tiles, *images),
        scratch=[pltpu.VMEM((2, 4 * TILE, TILE), BF16), pltpu.SemaphoreType.DMA((8,))],
        limit=24, flops=16 * TILE * TILE * KW, moved=8 << 20,
    )[0]


def sum16(held):
    total = jnp.zeros((64, KW), F32)
    for p in range(16):
        unit = jnp.exp2(floats(held[p, 64:, :])[:1, :] - 15.0)
        total = total + floats(held[p, :64, :]) * unit
    return total


def first_body(held, out):
    out[...] = sum16(held)


def join_body(first, last, out):
    total = sum16(last)
    for z in range(4):
        rows = slice(z * 16, (z + 1) * 16)
        out[z, :, :KW] = first[rows, :]
        out[z, :, KW:] = total[rows, :]


WIDE = 5 * NB


def finish_body(got, sketch_rows, shifted, spread):
    total = (got[0] + got[1]) + (got[2] + got[3]) + shift_weight * sketch_rows[...].astype(F32)
    shifted[...] = total
    for p in range(16):
        for d in range(5):
            block = (p // 2 + d) % 8
            spread[p, :, d * NB:(d + 1) * NB] = total[:, block * NB:(block + 1) * NB]


def strip_body(scale, rows_in, keep, give, strip):
    rows = jnp.concatenate([rows_in[p] for p in range(16)], axis=0)
    strip[...] = scale * lax.dot_general(
        rows[:, :NB], rows, (((0,), (0,)), ((), ())), precision=HI, preferred_element_type=F32
    )
    core = lax.rem(lax.axis_index("col"), 2)
    half = lax.rem(lax.axis_index("row"), 2) * 64
    keep[...] = strip[pl.ds(pl.multiple_of(half + core * 32, 32), 32), :]
    give[...] = strip[pl.ds(pl.multiple_of(half + (1 - core) * 32, 32), 32), :]


def gram_parts(spread, total_columns):
    rows = trade(spread, PLANES)
    keep, give = call(
        functools.partial(strip_body, 1.0 / total_columns), [((32, WIDE), F32)] * 2, [VMEM], (rows,),
        scratch=[pltpu.VMEM((NB, WIDE), F32)], limit=16,
        flops=12 * 256 * NB * WIDE, moved=2 << 20,
    )
    total = keep + swap(give, 1)
    total = total + swap(total, 2)
    total = total + swap_level(total, 1)
    total = total + swap_level(total, 2)
    own = trade(jnp.broadcast_to(total[None], (16, *total.shape)), PLANES)
    return own, swap(own, 1)


def dot(a, b):
    return jnp.dot(a, b, precision=HI, preferred_element_type=F32)


def dot_tn(a, b):
    return lax.dot_general(a, b, (((0,), (0,)), ((), ())), precision=HI, preferred_element_type=F32)


def dot_nt(a, b):
    return lax.dot_general(a, b, (((1,), (1,)), ((), ())), precision=HI, preferred_element_type=F32)


def down(value, k):
    return jnp.broadcast_to(value[k:k + 1, :], (8, NB))


def along(value, k):
    return jnp.broadcast_to(value[:, k:k + 1], (8, NB))


def add_up(terms):
    while len(terms) > 1:
        pairs = [a + b for a, b in zip(terms[::2], terms[1::2])]
        terms = pairs + terms[2 * len(pairs):]
    return terms[0]


def inverse_factor(block):
    groups = NB // 8
    sub = lax.broadcasted_iota(jnp.int32, (8, NB), 0)
    lane = lax.broadcasted_iota(jnp.int32, (8, NB), 1)
    w = [block[8 * g:8 * g + 8, :] for g in range(groups)]
    e = [jnp.where(lane == sub + 8 * g, 1.0, 0.0).astype(F32) for g in range(groups)]
    done = []
    cols = [along(w[0], k) for k in range(8)]
    for g in range(groups):
        z, ez = w[g], e[g]
        ahead, base = [], []
        if g + 1 < groups:
            ahead = [along(z, 8 * g + 8 + k) for k in range(8)]
            base = [along(w[g + 1], 8 * g + 8 + k) for k in range(8)]
        factors = [[along(w[i], 8 * g + k) for k in range(8)] for i in range(g + 1, groups)]
        scale = jnp.zeros((8, NB), F32)
        kept = jnp.zeros((8, NB), F32)
        for k in range(8):
            here = sub == k
            pivot = down(cols[k], k)
            r = 1.0 / pivot
            t = jnp.where(here, 1.0 - r, cols[k] * r)
            for n in range(k + 1, 8):
                cols[n] = cols[n] - t * down(cols[n], k)
            zrow, erow = down(z, k), down(ez, k)
            scale = jnp.where(here, lax.rsqrt(pivot), scale)
            kept = jnp.where(here, erow, kept)
            z = z - t * zrow
            ez = ez - t * erow
            ahead = [v - t * down(v, k) for v in ahead]
        done.append(kept * scale)
        if g + 1 < groups:
            cols = [base[k] - add_up([factors[0][m] * down(ahead[k], m) for m in range(8)]) for k in range(8)]
            zrows, erows = [down(z, k) for k in range(8)], [down(ez, k) for k in range(8)]
            for f, i in zip(factors, range(g + 1, groups)):
                w[i] = w[i] - add_up([f[k] * zrows[k] for k in range(8)])
                e[i] = e[i] - add_up([f[k] * erows[k] for k in range(8)])
    return jnp.concatenate(done, axis=0)


def factor_body(own, other, shifted, basis, triangle, work):
    core = lax.rem(lax.axis_index("col"), 2)
    for p in range(16):
        for held, half in ((own, core), (other, 1 - core)):
            here = pl.ds(pl.multiple_of(p * 64 + half * 32, 32), 32)
            for d in range(5):
                block = (p // 2 + d) % 8
                work[here, block * NB:(block + 1) * NB] = held[p, :, d * NB:(d + 1) * NB]
    for i in range(3):
        for j in range(i + 5, 8):
            low = work[j * NB:(j + 1) * NB, i * NB:(i + 1) * NB]
            work[i * NB:(i + 1) * NB, j * NB:(j + 1) * NB] = low.T
    basis[...] = shifted[...]
    upper = lax.broadcasted_iota(jnp.int32, (NB, NB), 1) >= lax.broadcasted_iota(jnp.int32, (NB, NB), 0)
    for j in range(K // NB):
        here, near, far = slice(j * NB, (j + 1) * NB), slice((j + 1) * NB, (j + 2) * NB), slice((j + 2) * NB, K)
        inverse = inverse_factor(work[here, here])
        if near.start < K:
            beside = dot(inverse, work[here, near])
            work[near, near] = work[near, near] - dot_tn(beside, beside)
            triangle[here, near] = beside
        if j:
            triangle[here, :j * NB] = jnp.zeros((NB, j * NB), F32)
        triangle[here, here] = jnp.where(upper, dot(inverse, work[here, here]), 0.0)
        if far.start < K:
            rest = dot(inverse, work[here, far])
            triangle[here, far] = rest
            work[near, far] = work[near, far] - dot_tn(beside, rest)
            work[far, far] = work[far, far] - dot_tn(rest, rest)
        own = dot_nt(basis[:, here], inverse)
        basis[:, here] = own
        if near.start < K:
            basis[:, near.start:] = basis[:, near.start:] - dot(own, triangle[here, near.start:])


def after(value, *others):
    return lax.optimization_barrier((value, *others))[0]


def local(tile_values, tile_coords, tile_counts, sketch):
    tiles = pltpu.with_memory_space_constraint(tile_values[0, 0], pltpu.HBM)
    strips = pltpu.with_memory_space_constraint(sketch, pltpu.HBM)
    places = tile_coords[0, 0]
    sketch_rows = lax.dynamic_slice_in_dim(sketch, lax.axis_index("row") * 16, 16, 0)

    owns, others = [], []

    def pair(part):
        got = swap(part[2], 1)
        owns.append(part[0] + got[0])
        others.append(part[1] + got[1])

    for part in forward(places, tile_counts, tiles, strips):
        pair(part)
    images = []
    for q in range(PARTS):
        image = (owns[q] + swap(others[q], 2)).astype(BF16)
        across, beside = swap(image, 2), swap(image, 1)
        across, *others = lax.optimization_barrier((across, *others))
        images.append((image, beside, across, swap(across, 1)))
    first = backward(places, tile_counts, tiles, images[0])
    first = call(first_body, [((64, KW), F32)], [VMEM], (trade(first, PLANES),), limit=16)[0]
    last = backward(places, tile_counts, tiles, images[1])
    last, first, sketch_rows = lax.optimization_barrier((last, first, sketch_rows))
    joined = call(join_body, [((4, 16, K), F32)], [VMEM] * 2, (first, trade(last, PLANES)), limit=16)[0]
    shifted, spread = call(
        finish_body, [((16, K), F32), ((16, 16, WIDE), F32)], [VMEM] * 2, (trade(joined, COLUMNS), sketch_rows),
        limit=16, moved=1 << 20,
    )
    own, other = gram_parts(spread, sketch.shape[0] * 4)
    basis, triangle = call(
        factor_body, [((16, K), F32), ((K, K), F32)], [VMEM] * 3, (own, other, shifted),
        scratch=[pltpu.VMEM((K, K), F32)], limit=40,
        flops=4 * K * K * K, moved=8 << 20,
    )
    return (basis[None], triangle)


def solution(mesh):
    in_specs = (
        P("row", "col", None, None, None),
        P("row", "col", None, None),
        P("row", "col"),
        P("col", None),
    )
    out_specs = (P("col", "row", None), P())
    return jax.shard_map(local, mesh=mesh, in_specs=in_specs, out_specs=out_specs, check_vma=False)
```

```python
import functools

import jax
import jax.numpy as jnp
from jax import lax
from jax.experimental import pallas as pl
from jax.experimental.pallas import tpu as pltpu
from jax.sharding import PartitionSpec as P

F32 = jnp.float32
BF16 = jnp.bfloat16
HI = lax.Precision.HIGHEST
TILE = 512
K = 1024
PARTS = 2
KW = K // PARTS
NB = 128
shift_weight = 0.5

VMEM = pl.BlockSpec(memory_space=pltpu.VMEM)
SMEM = pl.BlockSpec(memory_space=pltpu.SMEM)
HBM = pl.BlockSpec(memory_space=pltpu.HBM)


def call(body, outs, in_specs, args, scratch=(), limit=32, flops=0, moved=0):
    return pl.pallas_call(
        body,
        out_shape=tuple(jax.ShapeDtypeStruct(shape, dtype) for shape, dtype in outs),
        in_specs=in_specs,
        out_specs=tuple(VMEM for _ in outs),
        scratch_shapes=list(scratch),
        compiler_params=pltpu.CompilerParams(vmem_limit_bytes=limit << 20),
        cost_estimate=pl.CostEstimate(flops=flops, bytes_accessed=moved, transcendentals=0),
    )(*args)


PLANES = [[y * 16 + z * 4 + x for y in range(4) for x in range(4)] for z in range(4)]
COLUMNS = [[y * 16 + z * 4 + x for z in range(4)] for y in range(4) for x in range(4)]


def trade(value, groups):
    return lax.all_to_all(value, "row", 0, 0, tiled=True, axis_index_groups=groups)


def swap(value, bit):
    return lax.ppermute(value, "col", [(c, c ^ bit) for c in range(4)])


def swap_level(value, bit):
    return lax.ppermute(value, "row", [(r, r ^ (bit * 4)) for r in range(64)])


CODED = 80


def encode(value):
    top = jnp.maximum(jnp.max(jnp.abs(value), axis=0, keepdims=True), 1e-30)
    power = jnp.floor(jnp.log2(top)) + 1.0
    scaled = jnp.clip(jnp.round(value * jnp.exp2(15.0 - power)), -32767.0, 32767.0)
    return scaled.astype(jnp.int32).astype(jnp.int16), power


def widen(power):
    return jnp.broadcast_to(power, (16, power.shape[1])).astype(jnp.int32).astype(jnp.int16)


def floats(code):
    return code.astype(jnp.int32).astype(F32)


def decode(code, power):
    return floats(code) * jnp.exp2(floats(power) - 15.0)


def code_body(kept, got, out):
    powers = []
    for n in range(TILE // 64):
        rows = slice(n * 64, (n + 1) * 64)
        out[rows, :], power = encode(kept[rows, :] + got[1, rows, :])
        powers.append(power)
    powers = jnp.concatenate(powers + [jnp.zeros((8, KW), F32)], axis=0)
    out[TILE:, :] = powers.astype(jnp.int32).astype(jnp.int16)


def image_body(kept, got, code, out):
    powers = code[TILE:, :]
    for n in range(TILE // 64):
        rows = slice(n * 64, (n + 1) * 64)
        sent = decode(code[rows, :], powers[n:n + 1, :])
        out[rows, :] = (kept[rows, :] + got[0, rows, :] + sent).astype(BF16)


def find(places, count, i, j):
    slot, live = jnp.int32(0), jnp.int32(0)
    for s in range(8):
        match = (places[s, 0] == i) & (places[s, 1] == j) & (s < count)
        slot = jnp.where(match, s, slot)
        live = jnp.where(match, 1, live)
    return slot, live


def start_tiles(order, places, count, tiles, target, sems):
    copies, lives = {}, {}
    for n, (k, j) in enumerate(order):
        slot, lives[k, j] = find(places, count[0, 0], lax.axis_index("col") ^ k, j)
        copies[k, j] = pltpu.make_async_copy(tiles.at[slot], target(k, j), sems.at[n])
        copies[k, j].start()
    return copies, lives


def finish_tile(copy, live, target):
    copy.wait()

    @pl.when(live == 0)
    def _():
        target[...] = jnp.zeros((TILE, TILE), BF16)


def forward_body(places, count, tiles, sketch, *rest):
    outs, held, strip, sems = rest[:-3], rest[-3], rest[-2], rest[-1]
    order = [(k, j) for k in (1, 3, 0, 2) for j in range(2)]

    def target(k, j):
        return held.at[k, :, pl.ds(j * TILE, TILE)]

    load = pltpu.make_async_copy(sketch, strip, sems.at[8])
    load.start()
    copies, lives = start_tiles(order, places, count, tiles, target, sems)
    load.wait()
    for k in (1, 3, 0, 2):
        for j in range(2):
            finish_tile(copies[k, j], lives[k, j], target(k, j))
        total = jnp.dot(held[k], strip[...], preferred_element_type=F32)
        for n in range(PARTS):
            piece = total[:, n * KW:(n + 1) * KW]
            if k % 2:
                outs[3 * n + 2][k // 2] = piece
            else:
                outs[3 * n + k // 2][...] = piece


def forward(places, count, tiles, sketch):
    outs = call(
        forward_body, [((TILE, KW), F32), ((TILE, KW), F32), ((2, TILE, KW), F32)] * PARTS, [SMEM, SMEM, HBM, HBM],
        (places, count, tiles, sketch),
        scratch=[
            pltpu.VMEM((4, TILE, 2 * TILE), BF16), pltpu.VMEM((2 * TILE, K), BF16), pltpu.SemaphoreType.DMA((9,)),
        ],
        limit=24,
    )
    return [outs[3 * n:3 * n + 3] for n in range(PARTS)]


def backward_body(places, count, tiles, i0, i1, i2, i3, out, held, sems):
    order = [(k, j) for j in range(2) for k in range(4)]

    def target(k, j):
        return held.at[j, pl.ds(k * TILE, TILE), :]

    copies, lives = start_tiles(order, places, count, tiles, target, sems)
    image = jnp.concatenate([i0[...], i1[...], i2[...], i3[...]], axis=0)
    for j in range(2):
        for k in range(4):
            finish_tile(copies[k, j], lives[k, j], target(k, j))
        part = lax.dot_general(held[j], image, (((0,), (0,)), ((), ())), preferred_element_type=F32)
        for y in range(2):
            for x in range(4):
                starts = [y * 256 + z * 64 + x * 16 for z in range(4)]
                code, power = encode(jnp.concatenate([part[r:r + 16, :] for r in starts], axis=0))
                out[(2 * j + y) * 4 + x, :64, :] = code
                out[(2 * j + y) * 4 + x, 64:, :] = widen(power)


def backward(places, count, tiles, images):
    return call(
        backward_body, [((16, CODED, KW), jnp.int16)], [SMEM, SMEM, HBM] + [VMEM] * 4, (places, count, tiles, *images),
        scratch=[pltpu.VMEM((2, 4 * TILE, TILE), BF16), pltpu.SemaphoreType.DMA((8,))],
        limit=24, flops=16 * TILE * TILE * KW, moved=8 << 20,
    )[0]


def sum16(held):
    total = jnp.zeros((64, KW), F32)
    for p in range(16):
        total = total + decode(held[p, :64, :], held[p, 64:, :][:1, :])
    return total


def first_body(held, out):
    out[...] = sum16(held)


def join_body(first, last, out):
    total = sum16(last)
    for z in range(4):
        rows = slice(z * 16, (z + 1) * 16)
        out[z, :, :KW] = first[rows, :]
        out[z, :, KW:] = total[rows, :]


WIDE = 5 * NB


def finish_body(got, sketch_rows, shifted, spread):
    total = (got[0] + got[1]) + (got[2] + got[3]) + shift_weight * sketch_rows[...].astype(F32)
    shifted[...] = total
    for p in range(16):
        for d in range(5):
            block = (p // 2 + d) % 8
            spread[p, :, d * NB:(d + 1) * NB] = total[:, block * NB:(block + 1) * NB]


def strip_body(scale, rows_in, keep, give, strip):
    rows = jnp.concatenate([rows_in[p] for p in range(16)], axis=0)
    strip[...] = scale * lax.dot_general(
        rows[:, :NB], rows, (((0,), (0,)), ((), ())), precision=HI, preferred_element_type=F32
    )
    core = lax.rem(lax.axis_index("col"), 2)
    half = lax.rem(lax.axis_index("row"), 2) * 64
    keep[...] = strip[pl.ds(pl.multiple_of(half + core * 32, 32), 32), :]
    give[...] = strip[pl.ds(pl.multiple_of(half + (1 - core) * 32, 32), 32), :]


def gram_parts(spread, total_columns):
    rows = trade(spread, PLANES)
    keep, give = call(
        functools.partial(strip_body, 1.0 / total_columns), [((32, WIDE), F32)] * 2, [VMEM], (rows,),
        scratch=[pltpu.VMEM((NB, WIDE), F32)], limit=16,
        flops=12 * 256 * NB * WIDE, moved=2 << 20,
    )
    total = keep + swap(give, 1)
    total = total + swap(total, 2)
    total = total + swap_level(total, 1)
    total = total + swap_level(total, 2)
    own = trade(jnp.broadcast_to(total[None], (16, *total.shape)), PLANES)
    return own, swap(own, 1)


def dot(a, b):
    return jnp.dot(a, b, precision=HI, preferred_element_type=F32)


def dot_tn(a, b):
    return lax.dot_general(a, b, (((0,), (0,)), ((), ())), precision=HI, preferred_element_type=F32)


def dot_nt(a, b):
    return lax.dot_general(a, b, (((1,), (1,)), ((), ())), precision=HI, preferred_element_type=F32)


def down(value, k):
    return jnp.broadcast_to(value[k:k + 1, :], (8, NB))


def along(value, k):
    return jnp.broadcast_to(value[:, k:k + 1], (8, NB))


def add_up(terms):
    while len(terms) > 1:
        pairs = [a + b for a, b in zip(terms[::2], terms[1::2])]
        terms = pairs + terms[2 * len(pairs):]
    return terms[0]


def inverse_factor(block):
    groups = NB // 8
    sub = lax.broadcasted_iota(jnp.int32, (8, NB), 0)
    lane = lax.broadcasted_iota(jnp.int32, (8, NB), 1)
    w = [block[8 * g:8 * g + 8, :] for g in range(groups)]
    e = [jnp.where(lane == sub + 8 * g, 1.0, 0.0).astype(F32) for g in range(groups)]
    done = []
    cols = [along(w[0], k) for k in range(8)]
    for g in range(groups):
        z, ez = w[g], e[g]
        ahead, base = [], []
        if g + 1 < groups:
            ahead = [along(z, 8 * g + 8 + k) for k in range(8)]
            base = [along(w[g + 1], 8 * g + 8 + k) for k in range(8)]
        factors = [[along(w[i], 8 * g + k) for k in range(8)] for i in range(g + 1, groups)]
        scale = jnp.zeros((8, NB), F32)
        kept = jnp.zeros((8, NB), F32)
        for k in range(8):
            here = sub == k
            pivot = down(cols[k], k)
            r = 1.0 / pivot
            t = jnp.where(here, 1.0 - r, cols[k] * r)
            for n in range(k + 1, 8):
                cols[n] = cols[n] - t * down(cols[n], k)
            zrow, erow = down(z, k), down(ez, k)
            scale = jnp.where(here, lax.rsqrt(pivot), scale)
            kept = jnp.where(here, erow, kept)
            z = z - t * zrow
            ez = ez - t * erow
            ahead = [v - t * down(v, k) for v in ahead]
        done.append(kept * scale)
        if g + 1 < groups:
            cols = [base[k] - add_up([factors[0][m] * down(ahead[k], m) for m in range(8)]) for k in range(8)]
            zrows, erows = [down(z, k) for k in range(8)], [down(ez, k) for k in range(8)]
            for f, i in zip(factors, range(g + 1, groups)):
                w[i] = w[i] - add_up([f[k] * zrows[k] for k in range(8)])
                e[i] = e[i] - add_up([f[k] * erows[k] for k in range(8)])
    return jnp.concatenate(done, axis=0)


def factor_body(own, other, shifted, basis, triangle, work):
    core = lax.rem(lax.axis_index("col"), 2)
    for p in range(16):
        for held, half in ((own, core), (other, 1 - core)):
            here = pl.ds(pl.multiple_of(p * 64 + half * 32, 32), 32)
            for d in range(5):
                block = (p // 2 + d) % 8
                work[here, block * NB:(block + 1) * NB] = held[p, :, d * NB:(d + 1) * NB]
    for i in range(3):
        for j in range(i + 5, 8):
            low = work[j * NB:(j + 1) * NB, i * NB:(i + 1) * NB]
            work[i * NB:(i + 1) * NB, j * NB:(j + 1) * NB] = low.T
    basis[...] = shifted[...]
    upper = lax.broadcasted_iota(jnp.int32, (NB, NB), 1) >= lax.broadcasted_iota(jnp.int32, (NB, NB), 0)
    for j in range(K // NB):
        here, near, far = slice(j * NB, (j + 1) * NB), slice((j + 1) * NB, (j + 2) * NB), slice((j + 2) * NB, K)
        inverse = inverse_factor(work[here, here])
        if near.start < K:
            beside = dot(inverse, work[here, near])
            work[near, near] = work[near, near] - dot_tn(beside, beside)
            triangle[here, near] = beside
        if j:
            triangle[here, :j * NB] = jnp.zeros((NB, j * NB), F32)
        triangle[here, here] = jnp.where(upper, dot(inverse, work[here, here]), 0.0)
        if far.start < K:
            rest = dot(inverse, work[here, far])
            triangle[here, far] = rest
            work[near, far] = work[near, far] - dot_tn(beside, rest)
            work[far, far] = work[far, far] - dot_tn(rest, rest)
        own = dot_nt(basis[:, here], inverse)
        basis[:, here] = own
        if near.start < K:
            basis[:, near.start:] = basis[:, near.start:] - dot(own, triangle[here, near.start:])


def after(value, *others):
    return lax.optimization_barrier((value, *others))[0]


def local(tile_values, tile_coords, tile_counts, sketch):
    tiles = pltpu.with_memory_space_constraint(tile_values[0, 0], pltpu.HBM)
    strips = pltpu.with_memory_space_constraint(sketch, pltpu.HBM)
    places = tile_coords[0, 0]
    sketch_rows = lax.dynamic_slice_in_dim(sketch, lax.axis_index("row") * 16, 16, 0)

    parts = forward(places, tile_counts, tiles, strips)
    gots = [swap(parts[0][2], 1)]
    gots.append(swap(after(parts[1][2], gots[0]), 1))
    others = [
        call(code_body, [((TILE + 16, KW), jnp.int16)], [VMEM] * 2, (part[1], got), limit=16)[0]
        for part, got in zip(parts, gots)
    ]
    images = []
    for q in range(PARTS):
        code = swap(others[q], 2)
        image = call(image_body, [((TILE, KW), BF16)], [VMEM] * 3, (parts[q][0], gots[q], code), limit=16)[0]
        across, beside = swap(image, 2), swap(image, 1)
        across, *others = lax.optimization_barrier((across, *others))
        images.append((image, beside, across, swap(across, 1)))
    first = backward(places, tile_counts, tiles, images[0])
    first = call(first_body, [((64, KW), F32)], [VMEM], (trade(first, PLANES),), limit=16)[0]
    last = backward(places, tile_counts, tiles, images[1])
    last, first, sketch_rows = lax.optimization_barrier((last, first, sketch_rows))
    joined = call(join_body, [((4, 16, K), F32)], [VMEM] * 2, (first, trade(last, PLANES)), limit=16)[0]
    shifted, spread = call(
        finish_body, [((16, K), F32), ((16, 16, WIDE), F32)], [VMEM] * 2, (trade(joined, COLUMNS), sketch_rows),
        limit=16, moved=1 << 20,
    )
    own, other = gram_parts(spread, sketch.shape[0] * 4)
    basis, triangle = call(
        factor_body, [((16, K), F32), ((K, K), F32)], [VMEM] * 3, (own, other, shifted),
        scratch=[pltpu.VMEM((K, K), F32)], limit=40,
        flops=4 * K * K * K, moved=8 << 20,
    )
    return (basis[None], triangle)


def solution(mesh):
    in_specs = (
        P("row", "col", None, None, None),
        P("row", "col", None, None),
        P("row", "col"),
        P("col", None),
    )
    out_specs = (P("col", "row", None), P())
    return jax.shard_map(local, mesh=mesh, in_specs=in_specs, out_specs=out_specs, check_vma=False)
```

```python
import functools

import jax
import jax.numpy as jnp
from jax import lax
from jax.experimental import pallas as pl
from jax.experimental.pallas import tpu as pltpu
from jax.sharding import PartitionSpec as P

F32 = jnp.float32
BF16 = jnp.bfloat16
HI = lax.Precision.HIGHEST
TILE = 512
K = 1024
PARTS = 2
KW = K // PARTS
NB = 128
shift_weight = 0.5

VMEM = pl.BlockSpec(memory_space=pltpu.VMEM)
SMEM = pl.BlockSpec(memory_space=pltpu.SMEM)
HBM = pl.BlockSpec(memory_space=pltpu.HBM)


def call(body, outs, in_specs, args, scratch=(), limit=32, flops=0, moved=0):
    return pl.pallas_call(
        body,
        out_shape=tuple(jax.ShapeDtypeStruct(shape, dtype) for shape, dtype in outs),
        in_specs=in_specs,
        out_specs=tuple(VMEM for _ in outs),
        scratch_shapes=list(scratch),
        compiler_params=pltpu.CompilerParams(vmem_limit_bytes=limit << 20),
        cost_estimate=pl.CostEstimate(flops=flops, bytes_accessed=moved, transcendentals=0),
    )(*args)


PLANES = [[y * 16 + z * 4 + x for y in range(4) for x in range(4)] for z in range(4)]
COLUMNS = [[y * 16 + z * 4 + x for z in range(4)] for y in range(4) for x in range(4)]
LEVELS = [
    [(y * 16 + z * 4 + x) * 4 + low * 2 + core for z in range(4) for low in range(2)]
    for y in range(4) for x in range(4) for core in range(2)
]


def trade(value, groups):
    return lax.all_to_all(value, "row", 0, 0, tiled=True, axis_index_groups=groups)


def swap(value, bit):
    return lax.ppermute(value, "col", [(c, c ^ bit) for c in range(4)])


CODED = 80


def encode(value):
    top = jnp.maximum(jnp.max(jnp.abs(value), axis=0, keepdims=True), 1e-30)
    power = jnp.floor(jnp.log2(top)) + 1.0
    scaled = jnp.clip(jnp.round(value * jnp.exp2(15.0 - power)), -32767.0, 32767.0)
    return scaled.astype(jnp.int32).astype(jnp.int16), power


def widen(power):
    return jnp.broadcast_to(power, (16, power.shape[1])).astype(jnp.int32).astype(jnp.int16)


def floats(code):
    return code.astype(jnp.int32).astype(F32)


def decode(code, power):
    return floats(code) * jnp.exp2(floats(power) - 15.0)


def code_body(kept, got, out):
    powers = []
    for n in range(TILE // 64):
        rows = slice(n * 64, (n + 1) * 64)
        out[rows, :], power = encode(kept[rows, :] + got[rows, :])
        powers.append(power)
    powers = jnp.concatenate(powers + [jnp.zeros((8, KW), F32)], axis=0)
    out[TILE:, :] = powers.astype(jnp.int32).astype(jnp.int16)


def image_body(kept, got, code, out):
    powers = code[TILE:, :]
    for n in range(TILE // 64):
        rows = slice(n * 64, (n + 1) * 64)
        sent = decode(code[rows, :], powers[n:n + 1, :])
        out[rows, :] = (kept[rows, :] + got[rows, :] + sent).astype(BF16)


def find(places, count, i, j):
    slot, live = jnp.int32(0), jnp.int32(0)
    for s in range(8):
        match = (places[0, s] == i) & (places[1, s] == j) & (s < count)
        slot = jnp.where(match, s, slot)
        live = jnp.where(match, 1, live)
    return slot, live


def start_tiles(order, places, count, tiles, target, sems):
    copies, lives = {}, {}
    for n, (k, j) in enumerate(order):
        slot, lives[k, j] = find(places, count[0, 0], lax.axis_index("col") ^ k, j)
        copies[k, j] = pltpu.make_async_copy(tiles.at[slot], target(k, j), sems.at[n])
        copies[k, j].start()
    return copies, lives


def finish_tile(copy, live, target):
    copy.wait()

    @pl.when(live == 0)
    def _():
        target[...] = jnp.zeros((TILE, TILE), BF16)


def forward_body(places, count, tiles, sketch, *rest):
    outs, held, strip, sems = rest[:-3], rest[-3], rest[-2], rest[-1]
    order = [(k, j) for k in (3, 2, 1, 0) for j in range(2)]

    def target(k, j):
        return held.at[k, :, pl.ds(j * TILE, TILE)]

    load = pltpu.make_async_copy(sketch, strip, sems.at[8])
    load.start()
    copies, lives = start_tiles(order, places, count, tiles, target, sems)
    load.wait()
    for k in (3, 2, 1, 0):
        for j in range(2):
            finish_tile(copies[k, j], lives[k, j], target(k, j))
        total = jnp.dot(held[k], strip[...], preferred_element_type=F32)
        for n in range(PARTS):
            piece = total[:, n * KW:(n + 1) * KW]
            outs[4 * n + k][...] = piece


def forward(places, count, tiles, sketch):
    outs = call(
        forward_body, [((TILE, KW), F32)] * (4 * PARTS), [SMEM, SMEM, HBM, HBM],
        (places, count, tiles, sketch),
        scratch=[
            pltpu.VMEM((4, TILE, 2 * TILE), BF16), pltpu.VMEM((2 * TILE, K), BF16), pltpu.SemaphoreType.DMA((9,)),
        ],
        limit=24,
    )
    return [outs[4 * n:4 * n + 4] for n in range(PARTS)]


def backward_body(places, count, tiles, i0, i1, i2, i3, out, held, sems):
    order = [(k, j) for j in range(2) for k in range(4)]

    def target(k, j):
        return held.at[j, pl.ds(k * TILE, TILE), :]

    copies, lives = start_tiles(order, places, count, tiles, target, sems)
    image = jnp.concatenate([i0[...], i1[...], i2[...], i3[...]], axis=0)
    for j in range(2):
        for k in range(4):
            finish_tile(copies[k, j], lives[k, j], target(k, j))
        part = lax.dot_general(held[j], image, (((0,), (0,)), ((), ())), preferred_element_type=F32)
        for y in range(2):
            for x in range(4):
                starts = [y * 256 + z * 64 + x * 16 for z in range(4)]
                code, power = encode(jnp.concatenate([part[r:r + 16, :] for r in starts], axis=0))
                out[(2 * j + y) * 4 + x, :64, :] = code
                out[(2 * j + y) * 4 + x, 64:, :] = widen(power)


def backward(places, count, tiles, images):
    return call(
        backward_body, [((16, CODED, KW), jnp.int16)], [SMEM, SMEM, HBM] + [VMEM] * 4, (places, count, tiles, *images),
        scratch=[pltpu.VMEM((2, 4 * TILE, TILE), BF16), pltpu.SemaphoreType.DMA((8,))],
        limit=24, flops=16 * TILE * TILE * KW, moved=8 << 20,
    )[0]


def sum16(held):
    total = jnp.zeros((64, KW), F32)
    for p in range(16):
        total = total + decode(held[p, :64, :], held[p, 64:, :][:1, :])
    return total


def first_body(held, out):
    out[...] = sum16(held)


def join_body(first, last, out):
    total = sum16(last)
    for z in range(4):
        rows = slice(z * 16, (z + 1) * 16)
        out[z, :, :KW] = first[rows, :]
        out[z, :, KW:] = total[rows, :]


WIDE = 5 * NB


def finish_body(got, sketch, shifted, spread, held, sem):
    start = pl.multiple_of(lax.axis_index("row") * 16, 16)
    copy = pltpu.make_async_copy(sketch.at[pl.ds(start, 16), :], held, sem)
    copy.start()
    total = (got[0] + got[1]) + (got[2] + got[3])
    copy.wait()
    total = total + shift_weight * held[...].astype(F32)
    shifted[...] = total
    for p in range(16):
        for d in range(5):
            block = (p // 2 + d) % 8
            spread[p, :, d * NB:(d + 1) * NB] = total[:, block * NB:(block + 1) * NB]


def strip_body(scale, rows_in, keep, give, strip):
    rows = jnp.concatenate([rows_in[p] for p in range(16)], axis=0)
    strip[...] = scale * lax.dot_general(
        rows[:, :NB], rows, (((0,), (0,)), ((), ())), precision=HI, preferred_element_type=F32
    )
    core = lax.rem(lax.axis_index("col"), 2)
    half = lax.rem(lax.axis_index("row"), 2) * 64
    keep[...] = strip[pl.ds(pl.multiple_of(half + core * 32, 32), 32), :]
    give[...] = strip[pl.ds(pl.multiple_of(half + (1 - core) * 32, 32), 32), :]


def levels_body(levels, out):
    total = levels[0]
    for z in range(1, 8):
        total = total + levels[z]
    for p in range(16):
        out[p] = total


def gram_parts(spread, total_columns):
    rows = trade(spread, PLANES)
    keep, give = call(
        functools.partial(strip_body, 1.0 / total_columns), [((32, WIDE), F32)] * 2, [VMEM], (rows,),
        scratch=[pltpu.VMEM((NB, WIDE), F32)], limit=16,
        flops=12 * 256 * NB * WIDE, moved=2 << 20,
    )
    half = keep + swap(give, 1)
    levels = lax.all_to_all(
        jnp.broadcast_to(half[None], (8, *half.shape)), ("row", "col"), 0, 0, tiled=True, axis_index_groups=LEVELS
    )
    copies = call(levels_body, [((16, 32, WIDE), F32)], [VMEM], (levels,), limit=16)[0]
    own = trade(copies, PLANES)
    return own, swap(own, 1)


def dot(a, b):
    return jnp.dot(a, b, precision=HI, preferred_element_type=F32)


def dot_tn(a, b):
    return lax.dot_general(a, b, (((0,), (0,)), ((), ())), precision=HI, preferred_element_type=F32)


def dot_nt(a, b):
    return lax.dot_general(a, b, (((1,), (1,)), ((), ())), precision=HI, preferred_element_type=F32)


def down(value, k):
    return jnp.broadcast_to(value[k:k + 1, :], (8, NB))


def along(value, k):
    return jnp.broadcast_to(value[:, k:k + 1], (8, NB))


def add_up(terms):
    while len(terms) > 1:
        pairs = [a + b for a, b in zip(terms[::2], terms[1::2])]
        terms = pairs + terms[2 * len(pairs):]
    return terms[0]


def inverse_factor(block):
    groups = NB // 8
    sub = lax.broadcasted_iota(jnp.int32, (8, NB), 0)
    lane = lax.broadcasted_iota(jnp.int32, (8, NB), 1)
    w = [block[8 * g:8 * g + 8, :] for g in range(groups)]
    e = [jnp.where(lane == sub + 8 * g, 1.0, 0.0).astype(F32) for g in range(groups)]
    done = []
    cols = [along(w[0], k) for k in range(8)]
    for g in range(groups):
        z, ez = w[g], e[g]
        ahead, base = [], []
        if g + 1 < groups:
            ahead = [along(z, 8 * g + 8 + k) for k in range(8)]
            base = [along(w[g + 1], 8 * g + 8 + k) for k in range(8)]
        factors = [[along(w[i], 8 * g + k) for k in range(8)] for i in range(g + 1, groups)]
        scale = jnp.zeros((8, NB), F32)
        kept = jnp.zeros((8, NB), F32)
        for k in range(8):
            here = sub == k
            pivot = down(cols[k], k)
            r = 1.0 / pivot
            t = jnp.where(here, 1.0 - r, cols[k] * r)
            for n in range(k + 1, 8):
                cols[n] = cols[n] - t * down(cols[n], k)
            zrow, erow = down(z, k), down(ez, k)
            scale = jnp.where(here, lax.rsqrt(pivot), scale)
            kept = jnp.where(here, erow, kept)
            z = z - t * zrow
            ez = ez - t * erow
            ahead = [v - t * down(v, k) for v in ahead]
        done.append(kept * scale)
        if g + 1 < groups:
            cols = [base[k] - add_up([factors[0][m] * down(ahead[k], m) for m in range(8)]) for k in range(8)]
            zrows, erows = [down(z, k) for k in range(8)], [down(ez, k) for k in range(8)]
            for f, i in zip(factors, range(g + 1, groups)):
                w[i] = w[i] - add_up([f[k] * zrows[k] for k in range(8)])
                e[i] = e[i] - add_up([f[k] * erows[k] for k in range(8)])
    return jnp.concatenate(done, axis=0)


def factor_body(own, other, shifted, basis, triangle, work):
    core = lax.rem(lax.axis_index("col"), 2)
    for p in range(16):
        for held, half in ((own, core), (other, 1 - core)):
            here = pl.ds(pl.multiple_of(p * 64 + half * 32, 32), 32)
            for d in range(5):
                block = (p // 2 + d) % 8
                work[here, block * NB:(block + 1) * NB] = held[p, :, d * NB:(d + 1) * NB]
    for i in range(3):
        for j in range(i + 5, 8):
            low = work[j * NB:(j + 1) * NB, i * NB:(i + 1) * NB]
            work[i * NB:(i + 1) * NB, j * NB:(j + 1) * NB] = low.T
    basis[...] = shifted[...]
    upper = lax.broadcasted_iota(jnp.int32, (NB, NB), 1) >= lax.broadcasted_iota(jnp.int32, (NB, NB), 0)
    for j in range(K // NB):
        here, near, far = slice(j * NB, (j + 1) * NB), slice((j + 1) * NB, (j + 2) * NB), slice((j + 2) * NB, K)
        inverse = inverse_factor(work[here, here])
        if near.start < K:
            beside = dot(inverse, work[here, near])
            work[near, near] = work[near, near] - dot_tn(beside, beside)
            triangle[here, near] = beside
        if j:
            triangle[here, :j * NB] = jnp.zeros((NB, j * NB), F32)
        triangle[here, here] = jnp.where(upper, dot(inverse, work[here, here]), 0.0)
        if far.start < K:
            rest = dot(inverse, work[here, far])
            triangle[here, far] = rest
            work[near, far] = work[near, far] - dot_tn(beside, rest)
            work[far, far] = work[far, far] - dot_tn(rest, rest)
        own = dot_nt(basis[:, here], inverse)
        basis[:, here] = own
        if near.start < K:
            basis[:, near.start:] = basis[:, near.start:] - dot(own, triangle[here, near.start:])


def after(value, *others):
    return lax.optimization_barrier((value, *others))[0]


def local(tile_values, tile_coords, tile_counts, sketch):
    tiles = pltpu.with_memory_space_constraint(tile_values[0, 0], pltpu.HBM)
    strips = pltpu.with_memory_space_constraint(sketch, pltpu.HBM)
    places = tile_coords[0, 0].T

    parts = forward(places, tile_counts, tiles, strips)

    def code_of(part, far):
        return call(code_body, [((TILE + 16, KW), jnp.int16)], [VMEM] * 2, (part[2], far), limit=16)[0]

    def image_of(part, near, code):
        image = call(image_body, [((TILE, KW), BF16)], [VMEM] * 3, (part[0], near, code), limit=16)[0]
        return image, swap(image, 2), swap(image, 1)

    far = swap(parts[0][3], 1)
    far, near, far1, near1 = lax.optimization_barrier((far, parts[0][1], parts[1][3], parts[1][1]))
    code, code1 = code_of(parts[0], far), code_of(parts[1], swap(far1, 1))
    near, near1 = swap(near, 1), swap(near1, 1)
    image, across, beside = image_of(parts[0], near, swap(code, 2))
    across, code1 = lax.optimization_barrier((across, code1))
    first = backward(places, tile_counts, tiles, (image, beside, across, swap(across, 1)))
    code1, first = lax.optimization_barrier((swap(code1, 2), first))
    image, across, beside = image_of(parts[1], near1, code1)
    first = call(first_body, [((64, KW), F32)], [VMEM], (trade(first, PLANES),), limit=16)[0]
    last = backward(places, tile_counts, tiles, (image, beside, across, swap(across, 1)))
    last, first = lax.optimization_barrier((last, first))
    joined = call(join_body, [((4, 16, K), F32)], [VMEM] * 2, (first, trade(last, PLANES)), limit=16)[0]
    shifted, spread = call(
        finish_body, [((16, K), F32), ((16, 16, WIDE), F32)], [VMEM, HBM], (trade(joined, COLUMNS), strips),
        scratch=[pltpu.VMEM((16, K), BF16), pltpu.SemaphoreType.DMA], limit=16,
    )
    own, other = gram_parts(spread, sketch.shape[0] * 4)
    basis, triangle = call(
        factor_body, [((16, K), F32), ((K, K), F32)], [VMEM] * 3, (own, other, shifted),
        scratch=[pltpu.VMEM((K, K), F32)], limit=40,
        flops=4 * K * K * K, moved=8 << 20,
    )
    return (basis[None], triangle)


def solution(mesh):
    in_specs = (
        P("row", "col", None, None, None),
        P("row", "col", None, None),
        P("row", "col"),
        P("col", None),
    )
    out_specs = (P("col", "row", None), P())
    return jax.shard_map(local, mesh=mesh, in_specs=in_specs, out_specs=out_specs, check_vma=False)
```

```python
import functools

import jax
import jax.numpy as jnp
from jax import lax
from jax.experimental import pallas as pl
from jax.experimental.pallas import tpu as pltpu
from jax.sharding import PartitionSpec as P

F32 = jnp.float32
BF16 = jnp.bfloat16
HI = lax.Precision.HIGHEST
TILE = 512
K = 1024
PARTS = 2
KW = K // PARTS
NB = 128
shift_weight = 0.5

VMEM = pl.BlockSpec(memory_space=pltpu.VMEM)
SMEM = pl.BlockSpec(memory_space=pltpu.SMEM)
HBM = pl.BlockSpec(memory_space=pltpu.HBM)


def call(body, outs, in_specs, args, scratch=(), limit=32, flops=0, moved=0):
    return pl.pallas_call(
        body,
        out_shape=tuple(jax.ShapeDtypeStruct(shape, dtype) for shape, dtype in outs),
        in_specs=in_specs,
        out_specs=tuple(VMEM for _ in outs),
        scratch_shapes=list(scratch),
        compiler_params=pltpu.CompilerParams(vmem_limit_bytes=limit << 20),
        cost_estimate=pl.CostEstimate(flops=flops, bytes_accessed=moved, transcendentals=0),
    )(*args)


PLANES = [[y * 16 + z * 4 + x for y in range(4) for x in range(4)] for z in range(4)]
COLUMNS = [[y * 16 + z * 4 + x for z in range(4)] for y in range(4) for x in range(4)]
def trade(value, groups):
    return lax.all_to_all(value, "row", 0, 0, tiled=True, axis_index_groups=groups)


def swap(value, bit):
    return lax.ppermute(value, "col", [(c, c ^ bit) for c in range(4)])


def swap_level(value, bit):
    return lax.ppermute(value, "row", [(r, r ^ (bit * 4)) for r in range(64)])


LANES = 128
CODED = 64 * KW // LANES + 16


def encode(value):
    top = jnp.maximum(jnp.max(jnp.abs(value), axis=0, keepdims=True), 1e-30)
    power = jnp.floor(jnp.log2(top)) + 1.0
    scaled = jnp.clip(jnp.round(value * jnp.exp2(15.0 - power)), -32767.0, 32767.0)
    return scaled.astype(jnp.int32).astype(jnp.int16), power


def stack_powers(powers):
    filler = jnp.zeros((16 - len(powers), powers[0].shape[1]), F32)
    return jnp.concatenate(powers + [filler], axis=0).astype(jnp.int32).astype(jnp.int16)


def floats(code):
    return code.astype(jnp.int32).astype(F32)


def decode(code, power):
    return floats(code) * jnp.exp2(floats(power) - 15.0)


def code_body(kept, got, out):
    powers = []
    for n in range(TILE // 64):
        rows = slice(n * 64, (n + 1) * 64)
        out[rows, :], power = encode(kept[rows, :] + got[rows, :])
        powers.append(power)
    out[TILE:, :] = stack_powers(powers)


def image_body(kept, got, code, out):
    powers = code[TILE:, :]
    for n in range(TILE // 64):
        rows = slice(n * 64, (n + 1) * 64)
        sent = decode(code[rows, :], powers[n:n + 1, :])
        out[rows, :] = (kept[rows, :] + got[rows, :] + sent).astype(BF16)


def find(places, count, i, j):
    slot, live = jnp.int32(0), jnp.int32(0)
    for s in range(8):
        match = (places[0, s] == i) & (places[1, s] == j) & (s < count)
        slot = jnp.where(match, s, slot)
        live = jnp.where(match, 1, live)
    return slot, live


def start_tiles(order, places, count, tiles, target, sems):
    copies, lives = {}, {}
    for n, (k, j) in enumerate(order):
        slot, lives[k, j] = find(places, count[0, 0], lax.axis_index("col") ^ k, j)
        copies[k, j] = pltpu.make_async_copy(tiles.at[slot], target(k, j), sems.at[n])
        copies[k, j].start()
    return copies, lives


def finish_tile(copy, live, target):
    copy.wait()

    @pl.when(live == 0)
    def _():
        target[...] = jnp.zeros((TILE, TILE), BF16)


def forward_body(places, count, tiles, sketch, *rest):
    outs, held, strip, sems = rest[:-3], rest[-3], rest[-2], rest[-1]
    order = [(k, j) for k in (3, 2, 1, 0) for j in range(2)]

    def target(k, j):
        return held.at[k, :, pl.ds(j * TILE, TILE)]

    load = pltpu.make_async_copy(sketch, strip, sems.at[8])
    load.start()
    copies, lives = start_tiles(order, places, count, tiles, target, sems)
    load.wait()
    for k in (3, 2, 1, 0):
        for j in range(2):
            finish_tile(copies[k, j], lives[k, j], target(k, j))
        total = jnp.dot(held[k], strip[...], preferred_element_type=F32)
        for n in range(PARTS):
            piece = total[:, n * KW:(n + 1) * KW]
            outs[4 * n + k][...] = piece


def forward(places, count, tiles, sketch):
    outs = call(
        forward_body, [((TILE, KW), F32)] * (4 * PARTS), [SMEM, SMEM, HBM, HBM],
        (places, count, tiles, sketch),
        scratch=[
            pltpu.VMEM((4, TILE, 2 * TILE), BF16), pltpu.VMEM((2 * TILE, K), BF16), pltpu.SemaphoreType.DMA((9,)),
        ],
        limit=24,
    )
    return [outs[4 * n:4 * n + 4] for n in range(PARTS)]


def backward_body(places, count, tiles, i0, i1, i2, i3, out, held, sems):
    order = [(k, j) for j in range(2) for k in range(4)]

    def target(k, j):
        return held.at[j, pl.ds(k * TILE, TILE), :]

    copies, lives = start_tiles(order, places, count, tiles, target, sems)
    image = jnp.concatenate([i0[...], i1[...], i2[...], i3[...]], axis=0)
    for j in range(2):
        for k in range(4):
            finish_tile(copies[k, j], lives[k, j], target(k, j))
        part = lax.dot_general(held[j], image, (((0,), (0,)), ((), ())), preferred_element_type=F32)
        for y in range(2):
            for x in range(4):
                starts = [y * 256 + z * 64 + x * 16 for z in range(4)]
                code, power = encode(jnp.concatenate([part[r:r + 16, :] for r in starts], axis=0))
                blocks = KW // LANES
                for b in range(blocks):
                    out[(2 * j + y) * 4 + x, b * 64:(b + 1) * 64, :] = code[:, b * LANES:(b + 1) * LANES]
                out[(2 * j + y) * 4 + x, blocks * 64:, :] = stack_powers(
                    [power[:, b * LANES:(b + 1) * LANES] for b in range(blocks)]
                )


def backward(places, count, tiles, images):
    return call(
        backward_body, [((16, CODED, LANES), jnp.int16)], [SMEM, SMEM, HBM] + [VMEM] * 4, (places, count, tiles, *images),
        scratch=[pltpu.VMEM((2, 4 * TILE, TILE), BF16), pltpu.SemaphoreType.DMA((8,))],
        limit=24, flops=16 * TILE * TILE * KW, moved=8 << 20,
    )[0]


def sum16(held):
    blocks = KW // LANES
    totals = [jnp.zeros((64, LANES), F32) for _ in range(blocks)]
    for p in range(16):
        powers = held[p, blocks * 64:, :]
        for b in range(blocks):
            totals[b] = totals[b] + decode(held[p, b * 64:(b + 1) * 64, :], powers[b:b + 1, :])
    return jnp.concatenate(totals, axis=1)


def first_body(held, out):
    out[...] = sum16(held)


def join_body(first, last, out):
    total = sum16(last)
    for z in range(4):
        rows = slice(z * 16, (z + 1) * 16)
        out[z, :, :KW] = first[rows, :]
        out[z, :, KW:] = total[rows, :]


WIDE = 5 * NB


def finish_body(got, sketch, shifted, spread, held, sem):
    start = pl.multiple_of(lax.axis_index("row") * 16, 16)
    copy = pltpu.make_async_copy(sketch.at[pl.ds(start, 16), :], held, sem)
    copy.start()
    total = (got[0] + got[1]) + (got[2] + got[3])
    copy.wait()
    total = total + shift_weight * held[...].astype(F32)
    shifted[...] = total
    for p in range(16):
        for d in range(5):
            block = (p // 2 + d) % 8
            spread[p, :, d * NB:(d + 1) * NB] = total[:, block * NB:(block + 1) * NB]


def strip_body(scale, rows_in, keep, give, strip):
    rows = jnp.concatenate([rows_in[p] for p in range(16)], axis=0)
    strip[...] = scale * lax.dot_general(
        rows[:, :NB], rows, (((0,), (0,)), ((), ())), precision=HI, preferred_element_type=F32
    )
    core = lax.rem(lax.axis_index("col"), 2)
    half = lax.rem(lax.axis_index("row"), 2) * 64
    keep[...] = strip[pl.ds(pl.multiple_of(half + core * 32, 32), 32), :]
    give[...] = strip[pl.ds(pl.multiple_of(half + (1 - core) * 32, 32), 32), :]


def gram_parts(spread, total_columns):
    rows = trade(spread, PLANES)
    keep, give = call(
        functools.partial(strip_body, 1.0 / total_columns), [((32, WIDE), F32)] * 2, [VMEM], (rows,),
        scratch=[pltpu.VMEM((NB, WIDE), F32)], limit=16,
        flops=12 * 256 * NB * WIDE, moved=2 << 20,
    )
    total = keep + swap(give, 1)
    total = total + swap(total, 2)
    total = total + swap_level(total, 1)
    total = total + swap_level(total, 2)
    own = trade(jnp.broadcast_to(total[None], (16, *total.shape)), PLANES)
    return own, swap(own, 1)


def dot(a, b):
    return jnp.dot(a, b, precision=HI, preferred_element_type=F32)


def dot_tn(a, b):
    return lax.dot_general(a, b, (((0,), (0,)), ((), ())), precision=HI, preferred_element_type=F32)


def dot_nt(a, b):
    return lax.dot_general(a, b, (((1,), (1,)), ((), ())), precision=HI, preferred_element_type=F32)


def down(value, k):
    return jnp.broadcast_to(value[k:k + 1, :], (8, NB))


def along(value, k):
    return jnp.broadcast_to(value[:, k:k + 1], (8, NB))


def add_up(terms):
    while len(terms) > 1:
        pairs = [a + b for a, b in zip(terms[::2], terms[1::2])]
        terms = pairs + terms[2 * len(pairs):]
    return terms[0]


def inverse_factor(block):
    groups = NB // 8
    sub = lax.broadcasted_iota(jnp.int32, (8, NB), 0)
    lane = lax.broadcasted_iota(jnp.int32, (8, NB), 1)
    w = [block[8 * g:8 * g + 8, :] for g in range(groups)]
    e = [jnp.where(lane == sub + 8 * g, 1.0, 0.0).astype(F32) for g in range(groups)]
    done = []
    cols = [along(w[0], k) for k in range(8)]
    for g in range(groups):
        z, ez = w[g], e[g]
        ahead, base = [], []
        if g + 1 < groups:
            ahead = [along(z, 8 * g + 8 + k) for k in range(8)]
            base = [along(w[g + 1], 8 * g + 8 + k) for k in range(8)]
        factors = [[along(w[i], 8 * g + k) for k in range(8)] for i in range(g + 1, groups)]
        scale = jnp.zeros((8, NB), F32)
        kept = jnp.zeros((8, NB), F32)
        for k in range(8):
            here = sub == k
            pivot = down(cols[k], k)
            r = 1.0 / pivot
            t = jnp.where(here, 1.0 - r, cols[k] * r)
            for n in range(k + 1, 8):
                cols[n] = cols[n] - t * down(cols[n], k)
            zrow, erow = down(z, k), down(ez, k)
            scale = jnp.where(here, lax.rsqrt(pivot), scale)
            kept = jnp.where(here, erow, kept)
            z = z - t * zrow
            ez = ez - t * erow
            ahead = [v - t * down(v, k) for v in ahead]
        done.append(kept * scale)
        if g + 1 < groups:
            cols = [base[k] - add_up([factors[0][m] * down(ahead[k], m) for m in range(8)]) for k in range(8)]
            zrows, erows = [down(z, k) for k in range(8)], [down(ez, k) for k in range(8)]
            for f, i in zip(factors, range(g + 1, groups)):
                w[i] = w[i] - add_up([f[k] * zrows[k] for k in range(8)])
                e[i] = e[i] - add_up([f[k] * erows[k] for k in range(8)])
    return jnp.concatenate(done, axis=0)


def factor_body(own, other, shifted, basis, triangle, work):
    core = lax.rem(lax.axis_index("col"), 2)
    for p in range(16):
        for held, half in ((own, core), (other, 1 - core)):
            here = pl.ds(pl.multiple_of(p * 64 + half * 32, 32), 32)
            for d in range(5):
                block = (p // 2 + d) % 8
                work[here, block * NB:(block + 1) * NB] = held[p, :, d * NB:(d + 1) * NB]
    for i in range(3):
        for j in range(i + 5, 8):
            low = work[j * NB:(j + 1) * NB, i * NB:(i + 1) * NB]
            work[i * NB:(i + 1) * NB, j * NB:(j + 1) * NB] = low.T
    basis[...] = shifted[...]
    upper = lax.broadcasted_iota(jnp.int32, (NB, NB), 1) >= lax.broadcasted_iota(jnp.int32, (NB, NB), 0)
    for j in range(K // NB):
        here, near, far = slice(j * NB, (j + 1) * NB), slice((j + 1) * NB, (j + 2) * NB), slice((j + 2) * NB, K)
        inverse = inverse_factor(work[here, here])
        if near.start < K:
            beside = dot(inverse, work[here, near])
            work[near, near] = work[near, near] - dot_tn(beside, beside)
            triangle[here, near] = beside
        if j:
            triangle[here, :j * NB] = jnp.zeros((NB, j * NB), F32)
        triangle[here, here] = jnp.where(upper, dot(inverse, work[here, here]), 0.0)
        if far.start < K:
            rest = dot(inverse, work[here, far])
            triangle[here, far] = rest
            work[near, far] = work[near, far] - dot_tn(beside, rest)
            work[far, far] = work[far, far] - dot_tn(rest, rest)
        own = dot_nt(basis[:, here], inverse)
        basis[:, here] = own
        if near.start < K:
            basis[:, near.start:] = basis[:, near.start:] - dot(own, triangle[here, near.start:])


def after(value, *others):
    return lax.optimization_barrier((value, *others))[0]


def local(tile_values, tile_coords, tile_counts, sketch):
    tiles = pltpu.with_memory_space_constraint(tile_values[0, 0], pltpu.HBM)
    strips = pltpu.with_memory_space_constraint(sketch, pltpu.HBM)
    places = tile_coords[0, 0].T

    parts = forward(places, tile_counts, tiles, strips)

    def code_of(part, far):
        return call(code_body, [((TILE + 16, KW), jnp.int16)], [VMEM] * 2, (part[2], far), limit=16)[0]

    def image_of(part, near, code):
        image = call(image_body, [((TILE, KW), BF16)], [VMEM] * 3, (part[0], near, code), limit=16)[0]
        return image, swap(image, 2), swap(image, 1)

    far = swap(parts[0][3], 1)
    far, near, far1, near1 = lax.optimization_barrier((far, parts[0][1], parts[1][3], parts[1][1]))
    code, code1 = code_of(parts[0], far), code_of(parts[1], swap(far1, 1))
    near, near1 = swap(near, 1), swap(near1, 1)
    image, across, beside = image_of(parts[0], near, swap(code, 2))
    image1, across1, beside1 = image_of(parts[1], near1, swap(code1, 2))
    image, image1 = lax.optimization_barrier((image, image1))
    first = backward(places, tile_counts, tiles, (image, beside, across, swap(across, 1)))
    first = call(first_body, [((64, KW), F32)], [VMEM], (trade(first, PLANES),), limit=16)[0]
    first, across1, beside1 = lax.optimization_barrier((first, across1, beside1))
    last = backward(places, tile_counts, tiles, (image1, beside1, across1, swap(across1, 1)))
    last, first = lax.optimization_barrier((last, first))
    joined = call(join_body, [((4, 16, K), F32)], [VMEM] * 2, (first, trade(last, PLANES)), limit=16)[0]
    shifted, spread = call(
        finish_body, [((16, K), F32), ((16, 16, WIDE), F32)], [VMEM, HBM], (trade(joined, COLUMNS), strips),
        scratch=[pltpu.VMEM((16, K), BF16), pltpu.SemaphoreType.DMA], limit=16,
    )
    own, other = gram_parts(spread, sketch.shape[0] * 4)
    basis, triangle = call(
        factor_body, [((16, K), F32), ((K, K), F32)], [VMEM] * 3, (own, other, shifted),
        scratch=[pltpu.VMEM((K, K), F32)], limit=40,
        flops=4 * K * K * K, moved=8 << 20,
    )
    return (basis[None], triangle)


def solution(mesh):
    in_specs = (
        P("row", "col", None, None, None),
        P("row", "col", None, None),
        P("row", "col"),
        P("col", None),
    )
    out_specs = (P("col", "row", None), P())
    return jax.shard_map(local, mesh=mesh, in_specs=in_specs, out_specs=out_specs, check_vma=False)
```

```python
import functools

import jax
import jax.numpy as jnp
from jax import lax
from jax.experimental import pallas as pl
from jax.experimental.pallas import tpu as pltpu
from jax.sharding import PartitionSpec as P

F32 = jnp.float32
BF16 = jnp.bfloat16
HI = lax.Precision.HIGHEST
TILE = 512
K = 1024
PARTS = 2
KW = K // PARTS
NB = 128
shift_weight = 0.5

VMEM = pl.BlockSpec(memory_space=pltpu.VMEM)
SMEM = pl.BlockSpec(memory_space=pltpu.SMEM)
HBM = pl.BlockSpec(memory_space=pltpu.HBM)


def call(body, outs, in_specs, args, scratch=(), limit=32, flops=0, moved=0):
    return pl.pallas_call(
        body,
        out_shape=tuple(jax.ShapeDtypeStruct(shape, dtype) for shape, dtype in outs),
        in_specs=in_specs,
        out_specs=tuple(VMEM for _ in outs),
        scratch_shapes=list(scratch),
        compiler_params=pltpu.CompilerParams(vmem_limit_bytes=limit << 20),
        cost_estimate=pl.CostEstimate(flops=flops, bytes_accessed=moved, transcendentals=0),
    )(*args)


PLANES = [[y * 16 + z * 4 + x for y in range(4) for x in range(4)] for z in range(4)]
COLUMNS = [[y * 16 + z * 4 + x for z in range(4)] for y in range(4) for x in range(4)]
def trade(value, groups):
    return lax.all_to_all(value, "row", 0, 0, tiled=True, axis_index_groups=groups)


def swap(value, bit):
    return lax.ppermute(value, "col", [(c, c ^ bit) for c in range(4)])


def swap_level(value, bit):
    return lax.ppermute(value, "row", [(r, r ^ (bit * 4)) for r in range(64)])


LANES = 128
CODED = 64 * KW // LANES + 16


def encode(value):
    top = jnp.maximum(jnp.max(jnp.abs(value), axis=0, keepdims=True), 1e-30)
    power = jnp.floor(jnp.log2(top)) + 1.0
    scaled = jnp.clip(jnp.round(value * jnp.exp2(15.0 - power)), -32767.0, 32767.0)
    return scaled.astype(jnp.int32).astype(jnp.int16), power


def stack_powers(powers):
    filler = jnp.zeros((16 - len(powers), powers[0].shape[1]), F32)
    return jnp.concatenate(powers + [filler], axis=0).astype(jnp.int32).astype(jnp.int16)


def floats(code):
    return code.astype(jnp.int32).astype(F32)


def decode(code, power):
    return floats(code) * jnp.exp2(floats(power) - 15.0)


def code_body(kept, got, out):
    powers = []
    for n in range(TILE // 64):
        rows = slice(n * 64, (n + 1) * 64)
        out[rows, :], power = encode(kept[rows, :] + got[rows, :])
        powers.append(power)
    out[TILE:, :] = stack_powers(powers)


def image_body(kept, got, code, out):
    powers = code[TILE:, :]
    for n in range(TILE // 64):
        rows = slice(n * 64, (n + 1) * 64)
        sent = decode(code[rows, :], powers[n:n + 1, :])
        out[rows, :] = (kept[rows, :] + got[rows, :] + sent).astype(BF16)


def find(places, count, i, j):
    slot, live = jnp.int32(0), jnp.int32(0)
    for s in range(8):
        match = (places[0, s] == i) & (places[1, s] == j) & (s < count)
        slot = jnp.where(match, s, slot)
        live = jnp.where(match, 1, live)
    return slot, live


def start_tiles(order, places, count, tiles, target, sems):
    copies, lives = {}, {}
    for n, (k, j) in enumerate(order):
        slot, lives[k, j] = find(places, count[0, 0], lax.axis_index("col") ^ k, j)
        copies[k, j] = pltpu.make_async_copy(tiles.at[slot], target(k, j), sems.at[n])
        copies[k, j].start()
    return copies, lives


def finish_tile(copy, live, target):
    copy.wait()

    @pl.when(live == 0)
    def _():
        target[...] = jnp.zeros((TILE, TILE), BF16)


def forward_body(places, count, tiles, sketch, *rest):
    outs, held, strip, sems = rest[:-3], rest[-3], rest[-2], rest[-1]
    order = [(k, j) for k in (3, 2, 1, 0) for j in range(2)]

    def target(k, j):
        return held.at[k, :, pl.ds(j * TILE, TILE)]

    loads = []
    for n in range(PARTS):
        columns = pl.ds(n * KW, KW)
        loads.append(pltpu.make_async_copy(sketch.at[:, columns], strip.at[:, columns], sems.at[8 + n]))
    loads[0].start()
    copies, lives = start_tiles(order, places, count, tiles, target, sems)
    for load in loads[1:]:
        load.start()
    for n in range(PARTS):
        loads[n].wait()
        for k in (3, 2, 1, 0):
            if n == 0:
                for j in range(2):
                    finish_tile(copies[k, j], lives[k, j], target(k, j))
            outs[4 * n + k][...] = jnp.dot(
                held[k], strip[:, n * KW:(n + 1) * KW], preferred_element_type=F32
            )


def forward(places, count, tiles, sketch):
    outs = call(
        forward_body, [((TILE, KW), F32)] * (4 * PARTS), [SMEM, SMEM, HBM, HBM],
        (places, count, tiles, sketch),
        scratch=[
            pltpu.VMEM((4, TILE, 2 * TILE), BF16), pltpu.VMEM((2 * TILE, K), BF16),
            pltpu.SemaphoreType.DMA((8 + PARTS,)),
        ],
        limit=24,
    )
    return [outs[4 * n:4 * n + 4] for n in range(PARTS)]


def backward_body(places, count, tiles, i0, i1, i2, i3, *rest):
    before, out, held, sems = rest[:-3], rest[-3], rest[-2], rest[-1]
    top = CODED * len(before)
    order = [(k, j) for j in range(2) for k in range(4)]

    def target(k, j):
        return held.at[j, pl.ds(k * TILE, TILE), :]

    copies, lives = start_tiles(order, places, count, tiles, target, sems)
    image = jnp.concatenate([i0[...], i1[...], i2[...], i3[...]], axis=0)
    for codes in before:
        for p in range(16):
            out[p, :top, :] = codes[p]
    for j in range(2):
        for k in range(4):
            finish_tile(copies[k, j], lives[k, j], target(k, j))
        part = lax.dot_general(held[j], image, (((0,), (0,)), ((), ())), preferred_element_type=F32)
        for y in range(2):
            for x in range(4):
                starts = [y * 256 + z * 64 + x * 16 for z in range(4)]
                code, power = encode(jnp.concatenate([part[r:r + 16, :] for r in starts], axis=0))
                blocks = KW // LANES
                for b in range(blocks):
                    rows = slice(top + b * 64, top + (b + 1) * 64)
                    out[(2 * j + y) * 4 + x, rows, :] = code[:, b * LANES:(b + 1) * LANES]
                out[(2 * j + y) * 4 + x, top + blocks * 64:, :] = stack_powers(
                    [power[:, b * LANES:(b + 1) * LANES] for b in range(blocks)]
                )


def backward(places, count, tiles, images, before=()):
    return call(
        backward_body, [((16, CODED * (1 + len(before)), LANES), jnp.int16)],
        [SMEM, SMEM, HBM] + [VMEM] * (4 + len(before)), (places, count, tiles, *images, *before),
        scratch=[pltpu.VMEM((2, 4 * TILE, TILE), BF16), pltpu.SemaphoreType.DMA((8,))],
        limit=24, flops=16 * TILE * TILE * KW, moved=8 << 20,
    )[0]


def join_body(held, out):
    blocks = KW // LANES
    for n in range(PARTS):
        top = n * CODED
        totals = [jnp.zeros((64, LANES), F32) for _ in range(blocks)]
        for p in range(16):
            powers = held[p, top + blocks * 64:top + CODED, :]
            for b in range(blocks):
                codes = held[p, top + b * 64:top + (b + 1) * 64, :]
                totals[b] = totals[b] + decode(codes, powers[b:b + 1, :])
        for b in range(blocks):
            for z in range(4):
                left = n * KW + b * LANES
                out[z, :, left:left + LANES] = totals[b][z * 16:(z + 1) * 16, :]


WIDE = 5 * NB


def finish_body(got, sketch, shifted, spread, held, sem):
    start = pl.multiple_of(lax.axis_index("row") * 16, 16)
    copy = pltpu.make_async_copy(sketch.at[pl.ds(start, 16), :], held, sem)
    copy.start()
    total = (got[0] + got[1]) + (got[2] + got[3])
    copy.wait()
    total = total + shift_weight * held[...].astype(F32)
    shifted[...] = total
    for p in range(16):
        for d in range(5):
            block = (p // 2 + d) % 8
            spread[p, :, d * NB:(d + 1) * NB] = total[:, block * NB:(block + 1) * NB]


def strip_body(scale, rows_in, keep, give, strip):
    rows = jnp.concatenate([rows_in[p] for p in range(16)], axis=0)
    strip[...] = scale * lax.dot_general(
        rows[:, :NB], rows, (((0,), (0,)), ((), ())), precision=HI, preferred_element_type=F32
    )
    core = lax.rem(lax.axis_index("col"), 2)
    half = lax.rem(lax.axis_index("row"), 2) * 64
    keep[...] = strip[pl.ds(pl.multiple_of(half + core * 32, 32), 32), :]
    give[...] = strip[pl.ds(pl.multiple_of(half + (1 - core) * 32, 32), 32), :]


def gram_parts(spread, total_columns):
    rows = trade(spread, PLANES)
    keep, give = call(
        functools.partial(strip_body, 1.0 / total_columns), [((32, WIDE), F32)] * 2, [VMEM], (rows,),
        scratch=[pltpu.VMEM((NB, WIDE), F32)], limit=16,
        flops=12 * 256 * NB * WIDE, moved=2 << 20,
    )
    total = keep + swap(give, 1)
    total = total + swap(total, 2)
    total = total + swap_level(total, 1)
    total = total + swap_level(total, 2)
    own = trade(jnp.broadcast_to(total[None], (16, *total.shape)), PLANES)
    return own, swap(own, 1)


def dot(a, b):
    return jnp.dot(a, b, precision=HI, preferred_element_type=F32)


def dot_tn(a, b):
    return lax.dot_general(a, b, (((0,), (0,)), ((), ())), precision=HI, preferred_element_type=F32)


def dot_nt(a, b):
    return lax.dot_general(a, b, (((1,), (1,)), ((), ())), precision=HI, preferred_element_type=F32)


def down(value, k):
    return jnp.broadcast_to(value[k:k + 1, :], (8, NB))


def along(value, k):
    return jnp.broadcast_to(value[:, k:k + 1], (8, NB))


def add_up(terms):
    while len(terms) > 1:
        pairs = [a + b for a, b in zip(terms[::2], terms[1::2])]
        terms = pairs + terms[2 * len(pairs):]
    return terms[0]


def inverse_factor(block):
    groups = NB // 8
    sub = lax.broadcasted_iota(jnp.int32, (8, NB), 0)
    lane = lax.broadcasted_iota(jnp.int32, (8, NB), 1)
    w = [block[8 * g:8 * g + 8, :] for g in range(groups)]
    e = [jnp.where(lane == sub + 8 * g, 1.0, 0.0).astype(F32) for g in range(groups)]
    done = []
    cols = [along(w[0], k) for k in range(8)]
    for g in range(groups):
        z, ez = w[g], e[g]
        ahead, base = [], []
        if g + 1 < groups:
            ahead = [along(z, 8 * g + 8 + k) for k in range(8)]
            base = [along(w[g + 1], 8 * g + 8 + k) for k in range(8)]
        factors = [[along(w[i], 8 * g + k) for k in range(8)] for i in range(g + 1, groups)]
        scale = jnp.zeros((8, NB), F32)
        kept = jnp.zeros((8, NB), F32)
        for k in range(8):
            here = sub == k
            pivot = down(cols[k], k)
            r = 1.0 / pivot
            t = jnp.where(here, 1.0 - r, cols[k] * r)
            for n in range(k + 1, 8):
                cols[n] = cols[n] - t * down(cols[n], k)
            zrow, erow = down(z, k), down(ez, k)
            scale = jnp.where(here, lax.rsqrt(pivot), scale)
            kept = jnp.where(here, erow, kept)
            z = z - t * zrow
            ez = ez - t * erow
            ahead = [v - t * down(v, k) for v in ahead]
        done.append(kept * scale)
        if g + 1 < groups:
            cols = [base[k] - add_up([factors[0][m] * down(ahead[k], m) for m in range(8)]) for k in range(8)]
            zrows, erows = [down(z, k) for k in range(8)], [down(ez, k) for k in range(8)]
            for f, i in zip(factors, range(g + 1, groups)):
                w[i] = w[i] - add_up([f[k] * zrows[k] for k in range(8)])
                e[i] = e[i] - add_up([f[k] * erows[k] for k in range(8)])
    return jnp.concatenate(done, axis=0)


def factor_body(own, other, shifted, basis, triangle, work):
    core = lax.rem(lax.axis_index("col"), 2)
    for p in range(16):
        for held, half in ((own, core), (other, 1 - core)):
            here = pl.ds(pl.multiple_of(p * 64 + half * 32, 32), 32)
            for d in range(5):
                block = (p // 2 + d) % 8
                work[here, block * NB:(block + 1) * NB] = held[p, :, d * NB:(d + 1) * NB]
    for i in range(3):
        for j in range(i + 5, 8):
            low = work[j * NB:(j + 1) * NB, i * NB:(i + 1) * NB]
            work[i * NB:(i + 1) * NB, j * NB:(j + 1) * NB] = low.T
    basis[...] = shifted[...]
    upper = lax.broadcasted_iota(jnp.int32, (NB, NB), 1) >= lax.broadcasted_iota(jnp.int32, (NB, NB), 0)
    for j in range(K // NB):
        here, near, far = slice(j * NB, (j + 1) * NB), slice((j + 1) * NB, (j + 2) * NB), slice((j + 2) * NB, K)
        inverse = inverse_factor(work[here, here])
        if near.start < K:
            beside = dot(inverse, work[here, near])
            work[near, near] = work[near, near] - dot_tn(beside, beside)
            triangle[here, near] = beside
        if j:
            triangle[here, :j * NB] = jnp.zeros((NB, j * NB), F32)
        triangle[here, here] = jnp.where(upper, dot(inverse, work[here, here]), 0.0)
        if far.start < K:
            rest = dot(inverse, work[here, far])
            triangle[here, far] = rest
            work[near, far] = work[near, far] - dot_tn(beside, rest)
            work[far, far] = work[far, far] - dot_tn(rest, rest)
        own = dot_nt(basis[:, here], inverse)
        basis[:, here] = own
        if near.start < K:
            basis[:, near.start:] = basis[:, near.start:] - dot(own, triangle[here, near.start:])


def after(value, *others):
    return lax.optimization_barrier((value, *others))[0]


def local(tile_values, tile_coords, tile_counts, sketch):
    tiles = pltpu.with_memory_space_constraint(tile_values[0, 0], pltpu.HBM)
    strips = pltpu.with_memory_space_constraint(sketch, pltpu.HBM)
    places = tile_coords[0, 0].T

    parts = forward(places, tile_counts, tiles, strips)

    def code_of(part, far):
        return call(code_body, [((TILE + 16, KW), jnp.int16)], [VMEM] * 2, (part[2], far), limit=16)[0]

    def image_of(part, near, code):
        image = call(image_body, [((TILE, KW), BF16)], [VMEM] * 3, (part[0], near, code), limit=16)[0]
        return image, swap(image, 2), swap(image, 1)

    far = swap(parts[0][3], 1)
    far, near, far1, near1 = lax.optimization_barrier((far, parts[0][1], parts[1][3], parts[1][1]))
    code, code1 = code_of(parts[0], far), code_of(parts[1], swap(far1, 1))
    near, near1 = swap(near, 1), swap(near1, 1)
    image, across, beside = image_of(parts[0], near, swap(code, 2))
    image1, across1, beside1 = image_of(parts[1], near1, swap(code1, 2))
    image, image1 = lax.optimization_barrier((image, image1))
    first = backward(places, tile_counts, tiles, (image, beside, across, swap(across, 1)))
    first, across1, beside1 = lax.optimization_barrier((first, across1, beside1))
    codes = backward(places, tile_counts, tiles, (image1, beside1, across1, swap(across1, 1)), (first,))
    joined = call(join_body, [((4, 16, K), F32)], [VMEM], (trade(codes, PLANES),), limit=16)[0]
    shifted, spread = call(
        finish_body, [((16, K), F32), ((16, 16, WIDE), F32)], [VMEM, HBM], (trade(joined, COLUMNS), strips),
        scratch=[pltpu.VMEM((16, K), BF16), pltpu.SemaphoreType.DMA], limit=16,
    )
    own, other = gram_parts(spread, sketch.shape[0] * 4)
    basis, triangle = call(
        factor_body, [((16, K), F32), ((K, K), F32)], [VMEM] * 3, (own, other, shifted),
        scratch=[pltpu.VMEM((K, K), F32)], limit=40,
        flops=4 * K * K * K, moved=8 << 20,
    )
    return (basis[None], triangle)


def solution(mesh):
    in_specs = (
        P("row", "col", None, None, None),
        P("row", "col", None, None),
        P("row", "col"),
        P("col", None),
    )
    out_specs = (P("col", "row", None), P())
    return jax.shard_map(local, mesh=mesh, in_specs=in_specs, out_specs=out_specs, check_vma=False)
```

```python
import functools

import jax
import jax.numpy as jnp
from jax import lax
from jax.experimental import pallas as pl
from jax.experimental.pallas import tpu as pltpu
from jax.sharding import PartitionSpec as P

F32 = jnp.float32
BF16 = jnp.bfloat16
HI = lax.Precision.HIGHEST
TILE = 512
K = 1024
PARTS = 2
KW = K // PARTS
NB = 128
shift_weight = 0.5

VMEM = pl.BlockSpec(memory_space=pltpu.VMEM)
SMEM = pl.BlockSpec(memory_space=pltpu.SMEM)
HBM = pl.BlockSpec(memory_space=pltpu.HBM)


def call(body, outs, in_specs, args, scratch=(), limit=32, flops=0, moved=0):
    return pl.pallas_call(
        body,
        out_shape=tuple(jax.ShapeDtypeStruct(shape, dtype) for shape, dtype in outs),
        in_specs=in_specs,
        out_specs=tuple(VMEM for _ in outs),
        scratch_shapes=list(scratch),
        compiler_params=pltpu.CompilerParams(vmem_limit_bytes=limit << 20),
        cost_estimate=pl.CostEstimate(flops=flops, bytes_accessed=moved, transcendentals=0),
    )(*args)


PLANES = [[y * 16 + z * 4 + x for y in range(4) for x in range(4)] for z in range(4)]
COLUMNS = [[y * 16 + z * 4 + x for z in range(4)] for y in range(4) for x in range(4)]
def trade(value, groups):
    return lax.all_to_all(value, "row", 0, 0, tiled=True, axis_index_groups=groups)


def swap(value, bit):
    return lax.ppermute(value, "col", [(c, c ^ bit) for c in range(4)])


def swap_level(value, bit):
    return lax.ppermute(value, "row", [(r, r ^ (bit * 4)) for r in range(64)])


LANES = 128
CODED = 64 * KW // LANES + 16


def encode(value):
    top = jnp.maximum(jnp.max(jnp.abs(value), axis=0, keepdims=True), 1e-30)
    power = jnp.floor(jnp.log2(top)) + 1.0
    scaled = jnp.clip(jnp.round(value * jnp.exp2(15.0 - power)), -32767.0, 32767.0)
    return scaled.astype(jnp.int32).astype(jnp.int16), power


def stack_powers(powers):
    filler = jnp.zeros((16 - len(powers), powers[0].shape[1]), F32)
    return jnp.concatenate(powers + [filler], axis=0).astype(jnp.int32).astype(jnp.int16)


def floats(code):
    return code.astype(jnp.int32).astype(F32)


def decode(code, power):
    return floats(code) * jnp.exp2(floats(power) - 15.0)


def code_body(kept, got, out):
    powers = []
    for n in range(TILE // 64):
        rows = slice(n * 64, (n + 1) * 64)
        out[rows, :], power = encode(kept[rows, :] + got[rows, :])
        powers.append(power)
    out[TILE:, :] = stack_powers(powers)


def image_body(kept, got, code, out):
    powers = code[TILE:, :]
    for n in range(TILE // 64):
        rows = slice(n * 64, (n + 1) * 64)
        sent = decode(code[rows, :], powers[n:n + 1, :])
        out[rows, :] = (kept[rows, :] + got[rows, :] + sent).astype(BF16)


def find(places, count, i, j):
    slot, live = jnp.int32(0), jnp.int32(0)
    for s in range(8):
        match = (places[0, s] == i) & (places[1, s] == j) & (s < count)
        slot = jnp.where(match, s, slot)
        live = jnp.where(match, 1, live)
    return slot, live


def start_tiles(order, places, count, tiles, target, sems):
    copies, lives = {}, {}
    for n, (k, j) in enumerate(order):
        slot, lives[k, j] = find(places, count[0, 0], lax.axis_index("col") ^ k, j)
        copies[k, j] = pltpu.make_async_copy(tiles.at[slot], target(k, j), sems.at[n])
        copies[k, j].start()
    return copies, lives


def finish_tile(copy, live, target):
    copy.wait()

    @pl.when(live == 0)
    def _():
        target[...] = jnp.zeros((TILE, TILE), BF16)


def forward_body(places, count, tiles, sketch, *rest):
    outs, held, strip, sems = rest[:-3], rest[-3], rest[-2], rest[-1]
    order = [(k, j) for k in (3, 2, 1, 0) for j in range(2)]

    def target(k, j):
        return held.at[k, :, pl.ds(j * TILE, TILE)]

    load = pltpu.make_async_copy(sketch, strip, sems.at[8])
    load.start()
    copies, lives = start_tiles(order, places, count, tiles, target, sems)
    load.wait()
    for k in (3, 2, 1, 0):
        for j in range(2):
            finish_tile(copies[k, j], lives[k, j], target(k, j))
        total = jnp.dot(held[k], strip[...], preferred_element_type=F32)
        for n in range(PARTS):
            piece = total[:, n * KW:(n + 1) * KW]
            outs[4 * n + k][...] = piece


def forward(places, count, tiles, sketch):
    outs = call(
        forward_body, [((TILE, KW), F32)] * (4 * PARTS), [SMEM, SMEM, HBM, HBM],
        (places, count, tiles, sketch),
        scratch=[
            pltpu.VMEM((4, TILE, 2 * TILE), BF16), pltpu.VMEM((2 * TILE, K), BF16), pltpu.SemaphoreType.DMA((9,)),
        ],
        limit=24,
    )
    return [outs[4 * n:4 * n + 4] for n in range(PARTS)]


def backward_body(places, count, tiles, i0, i1, i2, i3, out, held, sems):
    order = [(k, j) for j in range(2) for k in range(4)]

    def target(k, j):
        return held.at[j, pl.ds(k * TILE, TILE), :]

    copies, lives = start_tiles(order, places, count, tiles, target, sems)
    image = jnp.concatenate([i0[...], i1[...], i2[...], i3[...]], axis=0)
    for j in range(2):
        for k in range(4):
            finish_tile(copies[k, j], lives[k, j], target(k, j))
        part = lax.dot_general(held[j], image, (((0,), (0,)), ((), ())), preferred_element_type=F32)
        for y in range(2):
            for x in range(4):
                starts = [y * 256 + z * 64 + x * 16 for z in range(4)]
                code, power = encode(jnp.concatenate([part[r:r + 16, :] for r in starts], axis=0))
                blocks = KW // LANES
                for b in range(blocks):
                    out[(2 * j + y) * 4 + x, b * 64:(b + 1) * 64, :] = code[:, b * LANES:(b + 1) * LANES]
                out[(2 * j + y) * 4 + x, blocks * 64:, :] = stack_powers(
                    [power[:, b * LANES:(b + 1) * LANES] for b in range(blocks)]
                )


def backward(places, count, tiles, images):
    return call(
        backward_body, [((16, CODED, LANES), jnp.int16)], [SMEM, SMEM, HBM] + [VMEM] * 4, (places, count, tiles, *images),
        scratch=[pltpu.VMEM((2, 4 * TILE, TILE), BF16), pltpu.SemaphoreType.DMA((8,))],
        limit=24, flops=16 * TILE * TILE * KW, moved=8 << 20,
    )[0]


def sum16(held):
    blocks = KW // LANES
    totals = [jnp.zeros((64, LANES), F32) for _ in range(blocks)]
    for p in range(16):
        powers = held[p, blocks * 64:, :]
        for b in range(blocks):
            totals[b] = totals[b] + decode(held[p, b * 64:(b + 1) * 64, :], powers[b:b + 1, :])
    return jnp.concatenate(totals, axis=1)


def first_body(held, out):
    out[...] = sum16(held)


def join_body(first, last, out):
    total = sum16(last)
    for z in range(4):
        rows = slice(z * 16, (z + 1) * 16)
        out[z, :, :KW] = first[rows, :]
        out[z, :, KW:] = total[rows, :]


WIDE = 5 * NB


def finish_body(got, sketch, shifted, spread, held, sem):
    start = pl.multiple_of(lax.axis_index("row") * 16, 16)
    copy = pltpu.make_async_copy(sketch.at[pl.ds(start, 16), :], held, sem)
    copy.start()
    total = (got[0] + got[1]) + (got[2] + got[3])
    copy.wait()
    total = total + shift_weight * held[...].astype(F32)
    shifted[...] = total
    for p in range(16):
        for d in range(5):
            block = (p // 2 + d) % 8
            spread[p, :, d * NB:(d + 1) * NB] = total[:, block * NB:(block + 1) * NB]


def strip_body(scale, rows_in, keep, give, strip):
    rows = jnp.concatenate([rows_in[p] for p in range(16)], axis=0)
    strip[...] = scale * lax.dot_general(
        rows[:, :NB], rows, (((0,), (0,)), ((), ())), precision=HI, preferred_element_type=F32
    )
    core = lax.rem(lax.axis_index("col"), 2)
    half = lax.rem(lax.axis_index("row"), 2) * 64
    keep[...] = strip[pl.ds(pl.multiple_of(half + core * 32, 32), 32), :]
    give[...] = strip[pl.ds(pl.multiple_of(half + (1 - core) * 32, 32), 32), :]


def gram_parts(spread, total_columns):
    rows = trade(spread, PLANES)
    keep, give = call(
        functools.partial(strip_body, 1.0 / total_columns), [((32, WIDE), F32)] * 2, [VMEM], (rows,),
        scratch=[pltpu.VMEM((NB, WIDE), F32)], limit=16,
        flops=12 * 256 * NB * WIDE, moved=2 << 20,
    )
    total = keep + swap(give, 1)
    total = total + swap(total, 2)
    total = total + swap_level(total, 1)
    total = total + swap_level(total, 2)
    own = trade(jnp.broadcast_to(total[None], (16, *total.shape)), PLANES)
    return own, swap(own, 1)


def dot(a, b):
    return jnp.dot(a, b, precision=HI, preferred_element_type=F32)


def dot_tn(a, b):
    return lax.dot_general(a, b, (((0,), (0,)), ((), ())), precision=HI, preferred_element_type=F32)


def dot_nt(a, b):
    return lax.dot_general(a, b, (((1,), (1,)), ((), ())), precision=HI, preferred_element_type=F32)


def down(value, k):
    return jnp.broadcast_to(value[k:k + 1, :], (8, NB))


def along(value, k):
    return jnp.broadcast_to(value[:, k:k + 1], (8, NB))


def add_up(terms):
    while len(terms) > 1:
        pairs = [a + b for a, b in zip(terms[::2], terms[1::2])]
        terms = pairs + terms[2 * len(pairs):]
    return terms[0]


def inverse_factor(block):
    groups = NB // 8
    sub = lax.broadcasted_iota(jnp.int32, (8, NB), 0)
    lane = lax.broadcasted_iota(jnp.int32, (8, NB), 1)
    w = [block[8 * g:8 * g + 8, :] for g in range(groups)]
    e = [jnp.where(lane == sub + 8 * g, 1.0, 0.0).astype(F32) for g in range(groups)]
    done = []
    cols = [along(w[0], k) for k in range(8)]
    for g in range(groups):
        z, ez = w[g], e[g]
        ahead, base = [], []
        if g + 1 < groups:
            ahead = [along(z, 8 * g + 8 + k) for k in range(8)]
            base = [along(w[g + 1], 8 * g + 8 + k) for k in range(8)]
        factors = [[along(w[i], 8 * g + k) for k in range(8)] for i in range(g + 1, groups)]
        scale = jnp.zeros((8, NB), F32)
        kept = jnp.zeros((8, NB), F32)
        for k in range(8):
            here = sub == k
            pivot = down(cols[k], k)
            r = 1.0 / pivot
            t = jnp.where(here, 1.0 - r, cols[k] * r)
            for n in range(k + 1, 8):
                cols[n] = cols[n] - t * down(cols[n], k)
            zrow, erow = down(z, k), down(ez, k)
            scale = jnp.where(here, lax.rsqrt(pivot), scale)
            kept = jnp.where(here, erow, kept)
            z = z - t * zrow
            ez = ez - t * erow
            ahead = [v - t * down(v, k) for v in ahead]
        done.append(kept * scale)
        if g + 1 < groups:
            cols = [base[k] - add_up([factors[0][m] * down(ahead[k], m) for m in range(8)]) for k in range(8)]
            zrows, erows = [down(z, k) for k in range(8)], [down(ez, k) for k in range(8)]
            for f, i in zip(factors, range(g + 1, groups)):
                w[i] = w[i] - add_up([f[k] * zrows[k] for k in range(8)])
                e[i] = e[i] - add_up([f[k] * erows[k] for k in range(8)])
    return jnp.concatenate(done, axis=0)


def factor_body(own, other, shifted, basis, triangle, work):
    core = lax.rem(lax.axis_index("col"), 2)
    for p in range(16):
        for held, half in ((own, core), (other, 1 - core)):
            here = pl.ds(pl.multiple_of(p * 64 + half * 32, 32), 32)
            for d in range(5):
                block = (p // 2 + d) % 8
                work[here, block * NB:(block + 1) * NB] = held[p, :, d * NB:(d + 1) * NB]
    for i in range(3):
        for j in range(i + 5, 8):
            low = work[j * NB:(j + 1) * NB, i * NB:(i + 1) * NB]
            work[i * NB:(i + 1) * NB, j * NB:(j + 1) * NB] = low.T
    basis[...] = shifted[...]
    upper = lax.broadcasted_iota(jnp.int32, (NB, NB), 1) >= lax.broadcasted_iota(jnp.int32, (NB, NB), 0)
    for j in range(K // NB):
        here, near, far = slice(j * NB, (j + 1) * NB), slice((j + 1) * NB, (j + 2) * NB), slice((j + 2) * NB, K)
        inverse = inverse_factor(work[here, here])
        if near.start < K:
            beside = dot(inverse, work[here, near])
            work[near, near] = work[near, near] - dot_tn(beside, beside)
            triangle[here, near] = beside
        if j:
            triangle[here, :j * NB] = jnp.zeros((NB, j * NB), F32)
        triangle[here, here] = jnp.where(upper, dot(inverse, work[here, here]), 0.0)
        if far.start < K:
            rest = dot(inverse, work[here, far])
            triangle[here, far] = rest
            work[near, far] = work[near, far] - dot_tn(beside, rest)
            work[far, far] = work[far, far] - dot_tn(rest, rest)
        own = dot_nt(basis[:, here], inverse)
        basis[:, here] = own
        if near.start < K:
            basis[:, near.start:] = basis[:, near.start:] - dot(own, triangle[here, near.start:])


def after(value, *others):
    return lax.optimization_barrier((value, *others))[0]


def local(tile_values, tile_coords, tile_counts, sketch):
    tiles = pltpu.with_memory_space_constraint(tile_values[0, 0], pltpu.HBM)
    strips = pltpu.with_memory_space_constraint(sketch, pltpu.HBM)
    places = tile_coords[0, 0].T

    parts = forward(places, tile_counts, tiles, strips)

    def code_of(part, far):
        return call(code_body, [((TILE + 16, KW), jnp.int16)], [VMEM] * 2, (part[2], far), limit=16)[0]

    def image_of(part, near, code):
        image = call(image_body, [((TILE, KW), BF16)], [VMEM] * 3, (part[0], near, code), limit=16)[0]
        return image, swap(image, 2), swap(image, 1)

    far = swap(parts[0][3], 1)
    far, near, far1, near1 = lax.optimization_barrier((far, parts[0][1], parts[1][3], parts[1][1]))
    code, code1 = code_of(parts[0], far), code_of(parts[1], swap(far1, 1))
    near, near1 = swap(near, 1), swap(near1, 1)
    image, across, beside = image_of(parts[0], near, swap(code, 2))
    image1, across1, beside1 = image_of(parts[1], near1, swap(code1, 2))
    image, image1 = lax.optimization_barrier((image, image1))
    first = backward(places, tile_counts, tiles, (image, beside, across, swap(across, 1)))
    first = call(first_body, [((64, KW), F32)], [VMEM], (trade(first, PLANES),), limit=16)[0]
    last = backward(places, tile_counts, tiles, (image1, beside1, across1, swap(across1, 1)))
    last, first = lax.optimization_barrier((last, first))
    joined = call(join_body, [((4, 16, K), F32)], [VMEM] * 2, (first, trade(last, PLANES)), limit=16)[0]
    shifted, spread = call(
        finish_body, [((16, K), F32), ((16, 16, WIDE), F32)], [VMEM, HBM], (trade(joined, COLUMNS), strips),
        scratch=[pltpu.VMEM((16, K), BF16), pltpu.SemaphoreType.DMA], limit=16,
    )
    own, other = gram_parts(spread, sketch.shape[0] * 4)
    basis, triangle = call(
        factor_body, [((16, K), F32), ((K, K), F32)], [VMEM] * 3, (own, other, shifted),
        scratch=[pltpu.VMEM((K, K), F32)], limit=40,
        flops=4 * K * K * K, moved=8 << 20,
    )
    return (basis[None], triangle)


def solution(mesh):
    in_specs = (
        P("row", "col", None, None, None),
        P("row", "col", None, None),
        P("row", "col"),
        P("col", None),
    )
    out_specs = (P("col", "row", None), P())
    return jax.shard_map(local, mesh=mesh, in_specs=in_specs, out_specs=out_specs, check_vma=False)
```

```python
import functools

import jax
import jax.numpy as jnp
from jax import lax
from jax.experimental import pallas as pl
from jax.experimental.pallas import tpu as pltpu
from jax.sharding import PartitionSpec as P

F32 = jnp.float32
BF16 = jnp.bfloat16
HI = lax.Precision.HIGHEST
TILE = 512
K = 1024
PARTS = 2
KW = K // PARTS
NB = 128
shift_weight = 0.5

VMEM = pl.BlockSpec(memory_space=pltpu.VMEM)
SMEM = pl.BlockSpec(memory_space=pltpu.SMEM)
HBM = pl.BlockSpec(memory_space=pltpu.HBM)


def call(body, outs, in_specs, args, scratch=(), limit=32, flops=0, moved=0):
    return pl.pallas_call(
        body,
        out_shape=tuple(jax.ShapeDtypeStruct(shape, dtype) for shape, dtype in outs),
        in_specs=in_specs,
        out_specs=tuple(VMEM for _ in outs),
        scratch_shapes=list(scratch),
        compiler_params=pltpu.CompilerParams(vmem_limit_bytes=limit << 20),
        cost_estimate=pl.CostEstimate(flops=flops, bytes_accessed=moved, transcendentals=0),
    )(*args)


PLANES = [[y * 16 + z * 4 + x for y in range(4) for x in range(4)] for z in range(4)]
COLUMNS = [[y * 16 + z * 4 + x for z in range(4)] for y in range(4) for x in range(4)]
def trade(value, groups):
    return lax.all_to_all(value, "row", 0, 0, tiled=True, axis_index_groups=groups)


def swap(value, bit):
    return lax.ppermute(value, "col", [(c, c ^ bit) for c in range(4)])


def swap_level(value, bit):
    return lax.ppermute(value, "row", [(r, r ^ (bit * 4)) for r in range(64)])


LANES = 128
CODED = 64 * KW // LANES + 16


def encode(value):
    top = jnp.maximum(jnp.max(jnp.abs(value), axis=0, keepdims=True), 1e-30)
    power = jnp.floor(jnp.log2(top)) + 1.0
    scaled = jnp.clip(jnp.round(value * jnp.exp2(15.0 - power)), -32767.0, 32767.0)
    return scaled.astype(jnp.int32).astype(jnp.int16), power


def stack_powers(powers):
    filler = jnp.zeros((16 - len(powers), powers[0].shape[1]), F32)
    return jnp.concatenate(powers + [filler], axis=0).astype(jnp.int32).astype(jnp.int16)


def floats(code):
    return code.astype(jnp.int32).astype(F32)


def decode(code, power):
    return floats(code) * jnp.exp2(floats(power) - 15.0)


def code_body(kept, got, out):
    powers = []
    for n in range(TILE // 64):
        rows = slice(n * 64, (n + 1) * 64)
        out[rows, :], power = encode(kept[rows, :] + got[rows, :])
        powers.append(power)
    out[TILE:, :] = stack_powers(powers)


def image_body(kept, got, code, out):
    powers = code[TILE:, :]
    for n in range(TILE // 64):
        rows = slice(n * 64, (n + 1) * 64)
        sent = decode(code[rows, :], powers[n:n + 1, :])
        out[rows, :] = (kept[rows, :] + got[rows, :] + sent).astype(BF16)


def find(places, count, i, j):
    slot, live = jnp.int32(0), jnp.int32(0)
    for s in range(8):
        match = (places[0, s] == i) & (places[1, s] == j) & (s < count)
        slot = jnp.where(match, s, slot)
        live = jnp.where(match, 1, live)
    return slot, live


def start_tiles(order, places, count, tiles, target, sems):
    copies, lives = {}, {}
    for n, (k, j) in enumerate(order):
        slot, lives[k, j] = find(places, count[0, 0], lax.axis_index("col") ^ k, j)
        copies[k, j] = pltpu.make_async_copy(tiles.at[slot], target(k, j), sems.at[n])
        copies[k, j].start()
    return copies, lives


def finish_tile(copy, live, target):
    copy.wait()

    @pl.when(live == 0)
    def _():
        target[...] = jnp.zeros((TILE, TILE), BF16)


def forward_body(places, count, tiles, sketch, *rest):
    outs, held, strip, sems = rest[:-3], rest[-3], rest[-2], rest[-1]
    order = [(k, j) for k in (3, 2, 1, 0) for j in range(2)]

    def target(k, j):
        return held.at[k, :, pl.ds(j * TILE, TILE)]

    load = pltpu.make_async_copy(sketch, strip, sems.at[8])
    load.start()
    copies, lives = start_tiles(order, places, count, tiles, target, sems)
    load.wait()
    for k in (3, 2, 1, 0):
        for j in range(2):
            finish_tile(copies[k, j], lives[k, j], target(k, j))
        total = jnp.dot(held[k], strip[...], preferred_element_type=F32)
        for n in range(PARTS):
            piece = total[:, n * KW:(n + 1) * KW]
            outs[4 * n + k][...] = piece


def forward(places, count, tiles, sketch):
    outs = call(
        forward_body, [((TILE, KW), F32)] * (4 * PARTS), [SMEM, SMEM, HBM, HBM],
        (places, count, tiles, sketch),
        scratch=[
            pltpu.VMEM((4, TILE, 2 * TILE), BF16), pltpu.VMEM((2 * TILE, K), BF16), pltpu.SemaphoreType.DMA((9,)),
        ],
        limit=24,
    )
    return [outs[4 * n:4 * n + 4] for n in range(PARTS)]


def backward_body(places, count, tiles, i0, i1, i2, i3, out, held, sems):
    order = [(k, j) for j in range(2) for k in range(4)]

    def target(k, j):
        return held.at[j, pl.ds(k * TILE, TILE), :]

    copies, lives = start_tiles(order, places, count, tiles, target, sems)
    image = jnp.concatenate([i0[...], i1[...], i2[...], i3[...]], axis=0)
    for j in range(2):
        for k in range(4):
            finish_tile(copies[k, j], lives[k, j], target(k, j))
        part = lax.dot_general(held[j], image, (((0,), (0,)), ((), ())), preferred_element_type=F32)
        for y in range(2):
            for x in range(4):
                starts = [y * 256 + z * 64 + x * 16 for z in range(4)]
                code, power = encode(jnp.concatenate([part[r:r + 16, :] for r in starts], axis=0))
                blocks = KW // LANES
                for b in range(blocks):
                    out[(2 * j + y) * 4 + x, b * 64:(b + 1) * 64, :] = code[:, b * LANES:(b + 1) * LANES]
                out[(2 * j + y) * 4 + x, blocks * 64:, :] = stack_powers(
                    [power[:, b * LANES:(b + 1) * LANES] for b in range(blocks)]
                )


def backward(places, count, tiles, images):
    return call(
        backward_body, [((16, CODED, LANES), jnp.int16)], [SMEM, SMEM, HBM] + [VMEM] * 4, (places, count, tiles, *images),
        scratch=[pltpu.VMEM((2, 4 * TILE, TILE), BF16), pltpu.SemaphoreType.DMA((8,))],
        limit=24, flops=16 * TILE * TILE * KW, moved=8 << 20,
    )[0]


def sum16(held):
    blocks = KW // LANES
    totals = [jnp.zeros((64, LANES), F32) for _ in range(blocks)]
    for p in range(16):
        powers = held[p, blocks * 64:, :]
        for b in range(blocks):
            totals[b] = totals[b] + decode(held[p, b * 64:(b + 1) * 64, :], powers[b:b + 1, :])
    return jnp.concatenate(totals, axis=1)


def first_body(held, out):
    out[...] = sum16(held)


def join_body(first, last, out):
    total = sum16(last)
    for z in range(4):
        rows = slice(z * 16, (z + 1) * 16)
        out[z, :, :KW] = first[rows, :]
        out[z, :, KW:] = total[rows, :]


WIDE = 5 * NB


def finish_body(got, sketch, shifted, spread, held, sem):
    start = pl.multiple_of(lax.axis_index("row") * 16, 16)
    copy = pltpu.make_async_copy(sketch.at[pl.ds(start, 16), :], held, sem)
    copy.start()
    total = (got[0] + got[1]) + (got[2] + got[3])
    copy.wait()
    total = total + shift_weight * held[...].astype(F32)
    shifted[...] = total
    for p in range(16):
        for d in range(5):
            block = (p // 2 + d) % 8
            spread[p, :, d * NB:(d + 1) * NB] = total[:, block * NB:(block + 1) * NB]


def strip_body(scale, rows_in, keep, give, strip):
    rows = jnp.concatenate([rows_in[p] for p in range(16)], axis=0)
    strip[...] = scale * lax.dot_general(
        rows[:, :NB], rows, (((0,), (0,)), ((), ())), precision=HI, preferred_element_type=F32
    )
    core = lax.rem(lax.axis_index("col"), 2)
    half = lax.rem(lax.axis_index("row"), 2) * 64
    keep[...] = strip[pl.ds(pl.multiple_of(half + core * 32, 32), 32), :]
    give[...] = strip[pl.ds(pl.multiple_of(half + (1 - core) * 32, 32), 32), :]


def gram_parts(spread, total_columns):
    rows = trade(spread, PLANES)
    keep, give = call(
        functools.partial(strip_body, 1.0 / total_columns), [((32, WIDE), F32)] * 2, [VMEM], (rows,),
        scratch=[pltpu.VMEM((NB, WIDE), F32)], limit=16,
        flops=12 * 256 * NB * WIDE, moved=2 << 20,
    )
    total = keep + swap(give, 1)
    total = total + swap(total, 2)
    total = total + swap_level(total, 1)
    total = total + swap_level(total, 2)
    own = trade(jnp.broadcast_to(total[None], (16, *total.shape)), PLANES)
    return own, swap(own, 1)


def dot(a, b):
    return jnp.dot(a, b, precision=HI, preferred_element_type=F32)


def dot_tn(a, b):
    return lax.dot_general(a, b, (((0,), (0,)), ((), ())), precision=HI, preferred_element_type=F32)


def dot_nt(a, b):
    return lax.dot_general(a, b, (((1,), (1,)), ((), ())), precision=HI, preferred_element_type=F32)


def down(value, k):
    return jnp.broadcast_to(value[k:k + 1, :], (8, NB))


def along(value, k):
    return jnp.broadcast_to(value[:, k:k + 1], (8, NB))


def add_up(terms):
    while len(terms) > 1:
        pairs = [a + b for a, b in zip(terms[::2], terms[1::2])]
        terms = pairs + terms[2 * len(pairs):]
    return terms[0]


def inverse_factor(block):
    groups = NB // 8
    sub = lax.broadcasted_iota(jnp.int32, (8, NB), 0)
    lane = lax.broadcasted_iota(jnp.int32, (8, NB), 1)
    w = [block[8 * g:8 * g + 8, :] for g in range(groups)]
    done = []
    cols = [along(w[0], k) for k in range(8)]
    for g in range(groups):
        within = (lane >= 8 * g) & (lane < 8 * g + 8)
        ahead, base = [], []
        if g + 1 < groups:
            ahead = [along(w[g], 8 * g + 8 + k) for k in range(8)]
            base = [along(w[g + 1], 8 * g + 8 + k) for k in range(8)]
        factors = [[along(w[i], 8 * g + k) for k in range(8)] for i in range(g + 1, groups)]
        z = jnp.where(within, jnp.where(lane == sub + 8 * g, 1.0, 0.0).astype(F32), w[g])
        scale = jnp.zeros((8, NB), F32)
        kept = jnp.zeros((8, NB), F32)
        for k in range(8):
            here = sub == k
            pivot = down(cols[k], k)
            r = 1.0 / pivot
            t = jnp.where(here, 1.0 - r, cols[k] * r)
            for n in range(k + 1, 8):
                cols[n] = cols[n] - t * down(cols[n], k)
            zrow = down(z, k)
            scale = jnp.where(here, lax.rsqrt(pivot), scale)
            kept = jnp.where(here, zrow, kept)
            z = z - t * zrow
            ahead = [v - t * down(v, k) for v in ahead]
        done.append(jnp.where(lane < 8 * g + 8, kept * scale, 0.0))
        if g + 1 < groups:
            cols = [base[k] - add_up([factors[0][m] * down(ahead[k], m) for m in range(8)]) for k in range(8)]
            zrows = [down(z, k) for k in range(8)]
            for f, i in zip(factors, range(g + 1, groups)):
                w[i] = jnp.where(within, 0.0, w[i]) - add_up([f[k] * zrows[k] for k in range(8)])
    return jnp.concatenate(done, axis=0)


def factor_body(own, other, shifted, basis, triangle, work):
    core = lax.rem(lax.axis_index("col"), 2)
    for p in range(16):
        for held, half in ((own, core), (other, 1 - core)):
            here = pl.ds(pl.multiple_of(p * 64 + half * 32, 32), 32)
            for d in range(5):
                block = (p // 2 + d) % 8
                work[here, block * NB:(block + 1) * NB] = held[p, :, d * NB:(d + 1) * NB]
    for i in range(3):
        for j in range(i + 5, 8):
            low = work[j * NB:(j + 1) * NB, i * NB:(i + 1) * NB]
            work[i * NB:(i + 1) * NB, j * NB:(j + 1) * NB] = low.T
    basis[...] = shifted[...]
    upper = lax.broadcasted_iota(jnp.int32, (NB, NB), 1) >= lax.broadcasted_iota(jnp.int32, (NB, NB), 0)
    for j in range(K // NB):
        here, near, far = slice(j * NB, (j + 1) * NB), slice((j + 1) * NB, (j + 2) * NB), slice((j + 2) * NB, K)
        inverse = inverse_factor(work[here, here])
        if near.start < K:
            beside = dot(inverse, work[here, near])
            work[near, near] = work[near, near] - dot_tn(beside, beside)
            triangle[here, near] = beside
        if j:
            triangle[here, :j * NB] = jnp.zeros((NB, j * NB), F32)
        triangle[here, here] = jnp.where(upper, dot(inverse, work[here, here]), 0.0)
        if far.start < K:
            rest = dot(inverse, work[here, far])
            triangle[here, far] = rest
            work[near, far] = work[near, far] - dot_tn(beside, rest)
            work[far, far] = work[far, far] - dot_tn(rest, rest)
        own = dot_nt(basis[:, here], inverse)
        basis[:, here] = own
        if near.start < K:
            basis[:, near.start:] = basis[:, near.start:] - dot(own, triangle[here, near.start:])


def after(value, *others):
    return lax.optimization_barrier((value, *others))[0]


def local(tile_values, tile_coords, tile_counts, sketch):
    tiles = pltpu.with_memory_space_constraint(tile_values[0, 0], pltpu.HBM)
    strips = pltpu.with_memory_space_constraint(sketch, pltpu.HBM)
    places = tile_coords[0, 0].T

    parts = forward(places, tile_counts, tiles, strips)

    def code_of(part, far):
        return call(code_body, [((TILE + 16, KW), jnp.int16)], [VMEM] * 2, (part[2], far), limit=16)[0]

    def image_of(part, near, code):
        image = call(image_body, [((TILE, KW), BF16)], [VMEM] * 3, (part[0], near, code), limit=16)[0]
        return image, swap(image, 2), swap(image, 1)

    far = swap(parts[0][3], 1)
    far, near, far1, near1 = lax.optimization_barrier((far, parts[0][1], parts[1][3], parts[1][1]))
    code, code1 = code_of(parts[0], far), code_of(parts[1], swap(far1, 1))
    near, near1 = swap(near, 1), swap(near1, 1)
    image, across, beside = image_of(parts[0], near, swap(code, 2))
    image1, across1, beside1 = image_of(parts[1], near1, swap(code1, 2))
    image, image1 = lax.optimization_barrier((image, image1))
    first = backward(places, tile_counts, tiles, (image, beside, across, swap(across, 1)))
    first = call(first_body, [((64, KW), F32)], [VMEM], (trade(first, PLANES),), limit=16)[0]
    last = backward(places, tile_counts, tiles, (image1, beside1, across1, swap(across1, 1)))
    last, first = lax.optimization_barrier((last, first))
    joined = call(join_body, [((4, 16, K), F32)], [VMEM] * 2, (first, trade(last, PLANES)), limit=16)[0]
    shifted, spread = call(
        finish_body, [((16, K), F32), ((16, 16, WIDE), F32)], [VMEM, HBM], (trade(joined, COLUMNS), strips),
        scratch=[pltpu.VMEM((16, K), BF16), pltpu.SemaphoreType.DMA], limit=16,
    )
    own, other = gram_parts(spread, sketch.shape[0] * 4)
    basis, triangle = call(
        factor_body, [((16, K), F32), ((K, K), F32)], [VMEM] * 3, (own, other, shifted),
        scratch=[pltpu.VMEM((K, K), F32)], limit=40,
        flops=4 * K * K * K, moved=8 << 20,
    )
    return (basis[None], triangle)


def solution(mesh):
    in_specs = (
        P("row", "col", None, None, None),
        P("row", "col", None, None),
        P("row", "col"),
        P("col", None),
    )
    out_specs = (P("col", "row", None), P())
    return jax.shard_map(local, mesh=mesh, in_specs=in_specs, out_specs=out_specs, check_vma=False)
```
